512 devices in a mesh: tm: 64 (over z, y), state: 8 (over x, core).
Axes of the slice: x: 4, y: 8, z: 8, core: 2. Of those that a mesh axis runs over, the one named last changes fastest.
Arguments:
- diagonal: float32 [128, 256, 256], P('tm', 'state'), may hold values from -1 to 12, as said below
- coupling: float32 [128, 256, 256], P('tm', 'state'), may hold values from -1.6 to 0.6, as said below
- info: float32 [128, 256], P('tm', 'state'), may hold values from -19 to 19
Outputs:
- smoothed: float32 [128, 256], P('tm', 'state')
The draws below stay inside these ranges and needn't reach their ends.
Inputs may be any that keep to these rules, and one draw needn't show every extreme that they name: Each diagonal block is symmetric, and the matrix J built from diagonal and coupling is positive definite. `coupling`: together with diagonal it forms a positive definite J.
All inputs are finite; a program needn't handle non-finite values.
Results may differ from the reference program's by a relative error of at most 0.0022.
Values sent between devices are 32-bit elements; how exact they have to be, the bound alone decides.
A program may use at most 64 MiB of HBM per device.

```python
import math
import jax
import jax.numpy as jnp
from jax import lax

LATENT_SIZE = 256
STEP_DEV = 2
HORIZON_LENGTH = 128


def model_rates(key, slow_count):
    stochastic_seed_sequence = jax.random.split(jax.random.fold_in(key, 101), 7)
    slow_mask = jax.random.randint(stochastic_seed_sequence[0], (LATENT_SIZE,), 0, 8) < slow_count
    slow_log = jax.random.uniform(stochastic_seed_sequence[1], (LATENT_SIZE,), jnp.float32, math.log(5e-07), math.log(5e-06))
    fast_log = jax.random.uniform(stochastic_seed_sequence[2], (LATENT_SIZE,), jnp.float32, math.log(0.003), math.log(3.0))
    base_rate = jnp.exp(jnp.where(slow_mask, slow_log, fast_log))
    stiffness = jnp.sqrt(base_rate + (2.0 / HORIZON_LENGTH) ** 2)
    step_log = jax.random.uniform(stochastic_seed_sequence[3], (HORIZON_LENGTH, 1), jnp.float32, -0.5, 0.5)
    block_log = jnp.repeat(jax.random.uniform(stochastic_seed_sequence[4], (HORIZON_LENGTH // STEP_DEV, 1), jnp.float32, -0.5, 0.5), STEP_DEV, axis=0)
    occurrence_frequencies = jnp.minimum(base_rate[None, :] * jnp.exp(step_log + block_log), 3.0)
    spike_occurrences = jax.random.randint(stochastic_seed_sequence[5], (HORIZON_LENGTH, LATENT_SIZE), 0, HORIZON_LENGTH) < 2
    link_magnitude = jax.random.uniform(stochastic_seed_sequence[6], (HORIZON_LENGTH, LATENT_SIZE), jnp.float32, 0.5, 2.0) * stiffness[None, :]
    occurrence_frequencies = occurrence_frequencies + jnp.where(spike_occurrences, link_magnitude, 0.0)
    return (base_rate, stiffness, occurrence_frequencies)


def mixing_weights(base_rate):
    return jnp.maximum(jnp.minimum(1.0, base_rate / 0.25), 0.005)


def transition_blocks(key, base_rate):
    stochastic_seed_sequence = jax.random.split(jax.random.fold_in(key, 202), 2)
    jitter = jax.random.uniform(stochastic_seed_sequence[0], (HORIZON_LENGTH, LATENT_SIZE), jnp.float32, 0.5, 1.5)
    leading = 1.0 - 0.3 * jnp.sqrt(base_rate)[None, :] * jitter
    mix_weight = mixing_weights(base_rate)
    weak_dims = (base_rate < 0.0001).astype(jnp.float32)
    pair_weight = mix_weight[:, None] * mix_weight[None, :] + 0.02 * weak_dims[:, None] * weak_dims[None, :]
    mixing = jnp.clip(jax.random.normal(stochastic_seed_sequence[1], (HORIZON_LENGTH, LATENT_SIZE, LATENT_SIZE), jnp.float32), -4.0, 4.0) * (1.0 / math.sqrt(LATENT_SIZE))
    mixing = mixing * pair_weight[None]
    return mixing + leading[:, :, None] * jnp.eye(LATENT_SIZE, dtype=jnp.float32)[None]


def observation_term(key, base_rate):
    mix_weight = mixing_weights(base_rate)
    sensing = jnp.clip(jax.random.normal(key, (HORIZON_LENGTH, LATENT_SIZE, LATENT_SIZE), jnp.float32), -4.0, 4.0) * (1.0 / math.sqrt(LATENT_SIZE))
    sensing = sensing * mix_weight[None, None, :]
    product = jnp.einsum('tki,tkj->tij', sensing, sensing, precision=lax.Precision.HIGHEST)
    return 0.15 * (product + jnp.swapaxes(product, 1, 2))


def draw_diagonal(key, part):
    base_rate, stiffness, occurrence_frequencies = model_rates(key, 4)
    transition_matrix = transition_blocks(key, base_rate)
    key = jax.random.fold_in(key, 1)
    gram = jnp.einsum('tki,tkj->tij', transition_matrix, transition_matrix, precision=lax.Precision.HIGHEST)
    gram = 0.5 * (gram + jnp.swapaxes(gram, 1, 2))
    follower_exists = (jnp.arange(HORIZON_LENGTH) < HORIZON_LENGTH - 1)[:, None, None]
    identity = jnp.eye(LATENT_SIZE, dtype=jnp.float32)
    sensed = observation_term(jax.random.fold_in(key, 303), base_rate)
    return identity[None] + jnp.where(follower_exists, gram, 0.0) + sensed + occurrence_frequencies[:, :, None] * identity[None]


def draw_coupling(key, part):
    base_rate, stiffness, occurrence_frequencies = model_rates(key, 4)
    transition_matrix = transition_blocks(key, base_rate)
    return -jnp.swapaxes(transition_matrix, 1, 2)


def draw_info(key, part):
    base_rate, stiffness, occurrence_frequencies = model_rates(key, 4)
    key = jax.random.fold_in(key, 3)
    rough = jnp.clip(jax.random.normal(key, (HORIZON_LENGTH, LATENT_SIZE), jnp.float32), -4.0, 4.0)
    return 2.0 * (stiffness ** 1.5)[None, :] * rough


def setup_inputs(seed: int = 0) -> dict:
    splits = jax.random.split(jax.random.key(seed), 4)
    diagonal = draw_diagonal(jax.random.fold_in(splits[3], 71), 0)
    coupling = draw_coupling(jax.random.fold_in(splits[3], 71), 0)
    info = draw_info(jax.random.fold_in(splits[3], 71), 0)
    return {"diagonal": diagonal, "coupling": coupling, "info": info}


def solve_with(factor, right_side):
    return jax.scipy.linalg.cho_solve((factor, True), right_side)

def reference(diagonal, coupling, info):
    exact = lax.Precision.HIGHEST

    def forward(carry, observed_arguments):
        corr_block, corr_vector = carry
        block, link, vector = observed_arguments
        factor = jnp.linalg.cholesky(block - corr_block)
        gain = solve_with(factor, link)
        mean = solve_with(factor, vector - corr_vector)
        next_block = jnp.dot(link.T, gain, precision=exact)
        next_vector = jnp.dot(link.T, mean, precision=exact)
        return ((next_block, next_vector), (gain, mean))
    start = (jnp.zeros((LATENT_SIZE, LATENT_SIZE), jnp.float32), jnp.zeros((LATENT_SIZE,), jnp.float32))
    _, (gains, means) = lax.scan(forward, start, (diagonal, coupling, info))

    def backward(later, observed_arguments):
        gain, mean = observed_arguments
        current = mean - jnp.dot(gain, later, precision=exact)
        return (current, current)
    last_mean = means[-1]
    _, earlier = lax.scan(backward, last_mean, (gains[:-1], means[:-1]), reverse=True)
    return jnp.concatenate([earlier, last_mean[None]], axis=0)
```

```python
import jax
import jax.numpy as jnp
from jax import lax
from jax.experimental import pallas as pl
from jax.experimental.pallas import tpu as pltpu
from jax.sharding import PartitionSpec as P

N = 256
H = 128
F32 = jnp.float32
MESH = pl.DeviceIdType.MESH
EXACT = lax.Precision.HIGHEST


def nt(a, b):
    return lax.dot_general(
        a, b, (((1,), (1,)), ((), ())), precision=EXACT, preferred_element_type=F32
    )


def nn(a, b):
    return jnp.dot(a, b, precision=EXACT, preferred_element_type=F32)


def row_of(x, k):
    return jnp.broadcast_to(x[k : k + 1, :], x.shape)


def lane_of(x, l):
    return jnp.broadcast_to(x[:, l : l + 1], (x.shape[0], H))


def sum8(t):
    return ((t[0] + t[1]) + (t[2] + t[3])) + ((t[4] + t[5]) + (t[6] + t[7]))


def invert8(columns, sub):
    c = list(columns)
    factor_rows = []
    for k in range(8):
        row = [row_of(c[j], k) for j in range(8)]
        inverse = 1.0 / row[k]
        root = lax.rsqrt(row[k])
        factor_rows.append([row[j] * root for j in range(k)] + [root])
        pivot_column = c[k]
        at = sub == k
        for j in range(8):
            if j != k:
                t = row[j] * inverse
                c[j] = jnp.where(at, t, c[j] - pivot_column * t)
        c[k] = jnp.where(at, inverse, -pivot_column * inverse)
    return c, factor_rows


def inverse_factor(a):
    w = [a[8 * r : 8 * r + 8, :] for r in range(16)]
    sub = lax.broadcasted_iota(jnp.int32, (8, H), 0)
    lane = lax.broadcasted_iota(jnp.int32, (8, H), 1)
    out = []
    for b in range(16):
        at = 8 * b
        inverse, factor_rows = invert8([lane_of(w[b], at + j) for j in range(8)], sub)
        inside = (lane >= at) & (lane < at + 8)
        panel = jnp.where(inside, (lane - at == sub).astype(F32), w[b])
        rows = [row_of(panel, j) for j in range(8)]
        scaled = sum8([inverse[j] * rows[j] for j in range(8)])
        done = []
        for j in range(8):
            column = jnp.zeros((8, H), F32)
            for i in range(j, 8):
                column = jnp.where(sub == i, factor_rows[i][j], column)
            done.append(column * rows[j])
        out.append(jnp.where(lane < at + 8, sum8(done), 0.0))
        if b < 15:
            scaled_rows = [row_of(scaled, j) for j in range(8)]
            for i in range(b + 1, 16):
                cols = [lane_of(w[i], at + j) for j in range(8)]
                w[i] = jnp.where(inside, 0.0, w[i]) - sum8(
                    [cols[j] * scaled_rows[j] for j in range(8)]
                )
    return jnp.concatenate(out, axis=0)


def eliminate(block, x, v, f1, f2, z):
    f1[...] = inverse_factor(block[0:H, 0:H])
    z[...] = nt(block[H:N, 0:H], f1[...])
    v[:, 0:H] = nt(x[:, 0:H], f1[...])
    f2[...] = inverse_factor(block[H:N, H:N] - nt(z[...], z[...]))
    y = x[:, H:N] - nt(v[:, 0:H], z[...])
    v[:, H:N] = nt(y, f2[...])


def means(v, f1, f2, z):
    hi = nn(v[:, H:N], f2[...])
    lo = nn(v[:, 0:H] - nn(hi, z[...]), f1[...])
    return lo, hi


def kernel(
    diag, coup, info, out,
    d1, c0, c1, hin, d2, xl, xu, xcat, v1, v2, f1a, f2a, za, f1b, f2b, zb, ga, gb,
    own_d, own_h, rc, rxl, rxu, su0, sx0, sl, su, sx, xin, xown,
    g1_send, g1_recv, g2_send, g2_recv, rc_recv, rx_recv, s_send, x_send, x_recv,
):
    s = lax.axis_index("tm")
    j = lax.axis_index("state")
    rows = pl.ds(pl.multiple_of(j * 32, 32), 32)

    def divides(d):
        return lax.rem(s, d) == 0

    barrier = pltpu.get_barrier_semaphore()
    count = jnp.int32(7)
    for r in range(1, 8):
        pl.semaphore_signal(
            barrier, inc=1, device_id=(s, lax.rem(j + r, 8)), device_id_type=MESH
        )
    for k in range(6):
        d = 2**k
        down = divides(d) & (s >= d)
        up = divides(d) & (s + d < 64)
        count = count + down.astype(jnp.int32) + up.astype(jnp.int32)

        @pl.when(down)
        def _():
            pl.semaphore_signal(barrier, inc=1, device_id=(s - d, j), device_id_type=MESH)

        @pl.when(up)
        def _():
            pl.semaphore_signal(barrier, inc=1, device_id=(s + d, j), device_id_type=MESH)

    pl.semaphore_wait(barrier, count)

    def to(src, dst, send, recv, tm, state):
        return pltpu.make_async_remote_copy(
            src_ref=src, dst_ref=dst, send_sem=send, recv_sem=recv,
            device_id=(tm, state), device_id_type=MESH,
        )

    def peer(src, dst, sends, recvs, a, r):
        return to(src, dst, sends.at[a, r], recvs.at[a, r], s, lax.rem(j + r, 8))

    first = [
        (diag.at[1], d1.at[rows]),
        (coup.at[0], c0.at[rows]),
        (coup.at[1], c1.at[rows]),
        (info, hin.at[pl.ds(pl.multiple_of(j * 8, 8), 8)]),
    ]
    for a, (src, dst) in enumerate(first):
        for r in range(1, 8):
            peer(src, dst, g1_send, g1_recv, a, r).start()
    for src, dst in first:
        dst[...] = src[...]
    for a, (src, dst) in enumerate(first):
        for r in range(1, 8):
            peer(src, dst, g1_send, g1_recv, a, r).wait_recv()

    info_all = sum8([hin[8 * i : 8 * i + 8, :] for i in range(8)])
    xcat[0:N, :] = c0[...]
    xcat[N : 2 * N, :] = jnp.where(s == 63, 0.0, c1[...].T)
    xcat[2 * N : 2 * N + 8, :] = row_of(info_all, 1)
    eliminate(d1, xcat, v1, f1a, f2a, za)

    def gram(v):
        start = pl.multiple_of(j * 32, 32)
        left = jnp.concatenate(
            [v[pl.ds(start, 32), :], v[pl.ds(start + N, 32), :], v[2 * N : 2 * N + 8, :]], axis=0
        )
        return nt(left, v[0 : 2 * N, :])

    prod = gram(v1)
    su0[0:32, :] = prod[32:64, N : 2 * N]
    su0[32:40, :] = prod[64:72, N : 2 * N]
    sx0[...] = -prod[0:32, N : 2 * N]
    rxu_local = -prod[32:64, 0:N]
    own_d[...] = diag[0] - prod[0:32, 0:N]
    own_h[...] = row_of(info_all, 0) - prod[64:72, 0:N]
    up0 = s < 63
    even = divides(2)

    def send_up0():
        return to(su0, rc.at[0], s_send.at[0], rc_recv.at[0], s + 1, j)

    def send_x0():
        return to(sx0, rxl, s_send.at[1], rx_recv.at[0], s + 1, j)

    @pl.when(up0)
    def _():
        send_up0().start()

    @pl.when(even)
    def _():
        send_x0().start()

    def take(slot, tm):
        to(sl, rc.at[slot], s_send.at[2], rc_recv.at[slot], tm, j).wait_recv()
        own_d[...] = own_d[...] - rc[slot, 0:32, :]
        own_h[...] = own_h[...] - rc[slot, 32:40, :]

    @pl.when(s > 0)
    def _():
        take(0, s - 1)

    for k in range(6):
        d = 2**k

        @pl.when(divides(2 * d) & (s > 0))
        def _():
            take(1 + 2 * k, s - d)

        @pl.when(divides(2 * d))
        def _():
            take(2 + 2 * k, s + d)

    def each_peer(src, dst, a, act):
        for r in range(1, 8):
            act(peer(src, dst, g2_send, g2_recv, a, r))

    each_peer(own_d, d2.at[rows], 0, lambda c: c.start())
    d2[rows, :] = own_d[...]

    @pl.when(s > 0)
    def _():
        to(sx0, rxl, s_send.at[1], rx_recv.at[0], s - 1, j).wait_recv()
        each_peer(rxl, xl.at[rows], 1, lambda c: c.start())
        xl[rows, :] = rxl[...]

        @pl.when(even)
        def _():
            to(sx, rxu, s_send.at[4], rx_recv.at[1], s - 1, j).wait_recv()

        @pl.when(jnp.logical_not(even))
        def _():
            rxu[...] = rxu_local

        each_peer(rxu, xu.at[rows], 2, lambda c: c.start())
        xu[rows, :] = rxu[...]

    each_peer(own_d, d2.at[rows], 0, lambda c: c.wait_recv())

    @pl.when(s > 0)
    def _():
        each_peer(rxl, xl.at[rows], 1, lambda c: c.wait_recv())
        each_peer(rxu, xu.at[rows], 2, lambda c: c.wait_recv())
        xcat[0:N, :] = xl[...]
        xcat[N : 2 * N, :] = xu[...]

    @pl.when(s == 0)
    def _():
        xcat[0 : 2 * N, :] = jnp.zeros((2 * N, N), F32)

    xcat[2 * N : 2 * N + 8, :] = own_h[...]
    eliminate(d2, xcat, v2, f1b, f2b, zb)
    prod = gram(v2)
    sl[0:32, :] = prod[0:32, 0:N]
    sl[32:40, :] = prod[64:72, 0:N]
    su[0:32, :] = prod[32:64, N : 2 * N]
    su[32:40, :] = prod[64:72, N : 2 * N]

    own_level = []
    for k in range(6):
        d = 2**k
        mine = lax.rem(s, 2 * d) == d
        own_level.append((k, d, mine))

    def sends(act):
        for k, d, mine in own_level:

            @pl.when(mine)
            def _():
                act(to(sl, rc.at[2 + 2 * k], s_send.at[2], rc_recv.at[2 + 2 * k], s - d, j))

            @pl.when(mine & (s + d < 64))
            def _():
                act(to(su, rc.at[1 + 2 * k], s_send.at[3], rc_recv.at[1 + 2 * k], s + d, j))

    def x_sends(act):
        for k, d, mine in own_level:
            if k == 5:
                continue

            @pl.when(mine & (lax.rem(s - d, 4 * d) == 2 * d))
            def _():
                act(to(sx, rxu, s_send.at[4], rx_recv.at[1], s - d, j))

            @pl.when(mine & (s + d < 64) & (lax.rem(s + d, 4 * d) == 2 * d))
            def _():
                act(to(sx, rxl, s_send.at[4], rx_recv.at[0], s + d, j))

    sends(lambda c: c.start())
    to_lower = jnp.bool_(False)
    for k, d, mine in own_level:
        to_lower = to_lower | (mine & (lax.rem(s - d, 4 * d) == 2 * d))

    @pl.when(to_lower)
    def _():
        sx[...] = -prod[32:64, 0:N]

    @pl.when(jnp.logical_not(to_lower))
    def _():
        sx[...] = -prod[0:32, N : 2 * N]

    x_sends(lambda c: c.start())

    lo, hi = means(v2, f1b, f2b, zb)
    gb[:, 0:H] = lo
    gb[:, H:N] = hi

    for k, d, mine in own_level:

        @pl.when(mine)
        def _():
            to(xown, xin.at[0], x_send.at[0], x_recv.at[0], s - d, j).wait_recv()

        @pl.when(mine & (s + d < 64))
        def _():
            to(xown, xin.at[1], x_send.at[0], x_recv.at[1], s + d, j).wait_recv()

        @pl.when(mine & (s + d >= 64))
        def _():
            xin[1] = jnp.zeros((8, N), F32)

    @pl.when(s == 0)
    def _():
        xown[...] = gb[2 * N : 2 * N + 8, :]

    @pl.when(s > 0)
    def _():
        xown[...] = gb[2 * N : 2 * N + 8, :] - (
            nn(xin[0], gb[0:N, :]) + nn(xin[1], gb[N : 2 * N, :])
        )

    def spread(act):
        for k in reversed(range(6)):
            d = 2**k

            @pl.when(divides(2 * d))
            def _():
                act(to(xown, xin.at[0], x_send.at[2 * k], x_recv.at[0], s + d, j))

            @pl.when(divides(2 * d) & (s > 0))
            def _():
                act(to(xown, xin.at[1], x_send.at[2 * k + 1], x_recv.at[1], s - d, j))

        @pl.when(jnp.logical_not(even))
        def _():
            act(to(xown, xin.at[2], x_send.at[12], x_recv.at[2], s - 1, j))

    spread(lambda c: c.start())

    lo, hi = means(v1, f1a, f2a, za)
    ga[:, 0:H] = lo
    ga[:, H:N] = hi
    part = ga[2 * N : 2 * N + 8, :] - nn(xown[...], ga[0:N, :])

    @pl.when(even)
    def _():
        to(xown, xin.at[2], x_send.at[12], x_recv.at[2], s + 1, j).wait_recv()

    @pl.when(jnp.logical_not(even))
    def _():
        xin[2] = xin[1]

    later = part - nn(xin[2], ga[N : 2 * N, :])
    both = jnp.concatenate([xown[0:1, :], later[0:1, :]], axis=0)
    for i in range(8):

        @pl.when(j == i)
        def _():
            out[...] = both[:, 32 * i : 32 * i + 32]

    for a, (src, dst) in enumerate(first):
        for r in range(1, 8):
            peer(src, dst, g1_send, g1_recv, a, r).wait_send()

    @pl.when(up0)
    def _():
        send_up0().wait_send()

    @pl.when(even)
    def _():
        send_x0().wait_send()

    each_peer(own_d, d2.at[rows], 0, lambda c: c.wait_send())

    @pl.when(s > 0)
    def _():
        each_peer(rxl, xl.at[rows], 1, lambda c: c.wait_send())
        each_peer(rxu, xu.at[rows], 2, lambda c: c.wait_send())

    sends(lambda c: c.wait_send())
    x_sends(lambda c: c.wait_send())
    spread(lambda c: c.wait_send())


def body(diagonal, coupling, info):
    offset = lax.axis_index("state") * 32
    placed = lax.dynamic_update_slice(jnp.zeros((8, N), F32), info, (0, offset))
    vmem = pltpu.VMEM
    dma = pltpu.SemaphoreType.DMA
    square = vmem((N, N), F32)
    half = vmem((H, H), F32)
    tall = vmem((2 * N + 8, N), F32)
    return pl.pallas_call(
        kernel,
        out_shape=jax.ShapeDtypeStruct((2, 32), F32),
        in_specs=[pl.BlockSpec(memory_space=vmem)] * 3,
        out_specs=pl.BlockSpec(memory_space=vmem),
        scratch_shapes=[
            square, square, square, vmem((64, N), F32), square, square, square, tall, tall, tall,
            half, half, half, half, half, half, tall, tall,
            vmem((32, N), F32), vmem((8, N), F32), vmem((13, 40, N), F32),
            vmem((32, N), F32), vmem((32, N), F32),
            vmem((40, N), F32), vmem((32, N), F32),
            vmem((40, N), F32), vmem((40, N), F32), vmem((32, N), F32),
            vmem((3, 8, N), F32), vmem((8, N), F32),
            dma((4, 8)), dma((4, 8)), dma((3, 8)), dma((3, 8)),
            dma((13,)), dma((2,)), dma((5,)), dma((13,)), dma((3,)),
        ],
        compiler_params=pltpu.CompilerParams(
            collective_id=0, has_side_effects=True, vmem_limit_bytes=32 * 1024 * 1024
        ),
    )(diagonal, coupling, placed)


def solution(mesh):
    placed = (P("tm", "state", None), P("tm", "state", None), P("tm", "state"))
    return jax.shard_map(
        body, mesh=mesh, in_specs=placed, out_specs=P("tm", "state"), check_vma=False
    )
```

```python
import jax
import jax.numpy as jnp
from jax import lax
from jax.experimental import pallas as pl
from jax.experimental.pallas import tpu as pltpu
from jax.sharding import PartitionSpec as P

N = 256
H = 128
F32 = jnp.float32
MESH = pl.DeviceIdType.MESH
EXACT = lax.Precision.HIGHEST


def nt(a, b):
    return lax.dot_general(
        a, b, (((1,), (1,)), ((), ())), precision=EXACT, preferred_element_type=F32
    )


def nn(a, b):
    return jnp.dot(a, b, precision=EXACT, preferred_element_type=F32)


def row_of(x, k):
    return jnp.broadcast_to(x[k : k + 1, :], x.shape)


def lane_of(x, l):
    return jnp.take_along_axis(x, jnp.full((8, H), l, jnp.int32), axis=1)


def sum8(t):
    return ((t[0] + t[1]) + (t[2] + t[3])) + ((t[4] + t[5]) + (t[6] + t[7]))


def pivot_block(w, b, sub, lane):
    at = 8 * b
    c = [lane_of(w[b], at + j) for j in range(8)]
    inside = (lane >= at) & (lane < at + 8)
    r = jnp.where(inside, (lane - at == sub).astype(F32), w[b])
    t = r
    pivots = jnp.ones((8, H), F32)
    inverses = []
    for k in range(0, 8, 2):
        first, second = sub == k, sub == k + 1
        p, q, o = row_of(c[k], k), row_of(c[k + 1], k), row_of(c[k + 1], k + 1)
        det = 1.0 / (p * o - q * q)
        m0 = jnp.where(first | second, 0.0, c[k])
        m1 = jnp.where(first | second, 0.0, c[k + 1])
        f0 = (m0 * o - m1 * q) * det
        f1 = (m1 * p - m0 * q) * det
        inverses.append((o * det, -q * det, p * det))
        ratio = q * (1.0 / p)
        r0, r1 = row_of(r, k), row_of(r, k + 1)
        t = jnp.where(first, r0, jnp.where(second, r1 - ratio * r0, t))
        pivots = jnp.where(first, p, jnp.where(second, o - ratio * q, pivots))
        for j in range(k + 2, 8):
            c[j] = c[j] - (f0 * row_of(c[j], k) + f1 * row_of(c[j], k + 1))
        r = r - (f0 * r0 + f1 * r1)
    if b < 15:
        rows = []
        for k in range(0, 8, 2):
            ia, ib, ic = inverses[k // 2]
            r0, r1 = row_of(r, k), row_of(r, k + 1)
            rows += [ia * r0 + ib * r1, ib * r0 + ic * r1]
        for i in range(b + 1, 16):
            cols = [lane_of(w[i], at + j) for j in range(8)]
            w[i] = jnp.where(inside, 0.0, w[i]) - sum8([cols[j] * rows[j] for j in range(8)])
    return jnp.where(lane < at + 8, t * lax.rsqrt(pivots), 0.0)


def factor_part(w, blocks):
    sub = lax.broadcasted_iota(jnp.int32, (8, H), 0)
    lane = lax.broadcasted_iota(jnp.int32, (8, H), 1)
    return [pivot_block(w, b, sub, lane) for b in blocks]


def groups(a):
    return [a[8 * r : 8 * r + 8, :] for r in range(16)]


def factor_start(block, f1):
    f1[...] = jnp.concatenate(factor_part(groups(block[0:H, 0:H]), range(16)), axis=0)


def factor_rest(block, fill, x, v, f1, f2, z):
    z[...] = nt(block[H:N, 0:H], f1[...])
    w = groups(block[H:N, H:N] - nt(z[...], z[...]))
    out = factor_part(w, range(8))
    fill()
    v[:, 0:H] = nt(x[:, 0:H], f1[...])
    y = x[:, H:N] - nt(v[:, 0:H], z[...])
    out += factor_part(w, range(8, 16))
    f2[...] = jnp.concatenate(out, axis=0)
    v[:, H:N] = nt(y, f2[...])


def means(v, f1, f2, z):
    hi = nn(v[:, H:N], f2[...])
    lo = nn(v[:, 0:H] - nn(hi, z[...]), f1[...])
    return lo, hi


def kernel(
    diag, coup, info, out,
    d1, c0, c1, hin, d2, xl, xu, xcat, v1, v2, f1a, f2a, za, f1b, f2b, zb, ga, gb,
    own_h, rc1, rc2, rxl, rxu, pu01, pu02, sx0, pl1, pl2, pu1, pu2, sx, xin, xown,
    g1_send, g1_recv, g2_send, g2_recv, r1_recv, r2_recv, rx_recv, s_send, x_send, x_recv, own_sem,
):
    s = lax.axis_index("tm")
    j = lax.axis_index("state")
    rows = pl.ds(pl.multiple_of(j * 32, 32), 32)

    def divides(d):
        return lax.rem(s, d) == 0

    even = divides(2)

    barrier = pltpu.get_barrier_semaphore()
    count = jnp.int32(7)
    for r in range(1, 8):
        pl.semaphore_signal(
            barrier, inc=1, device_id=(s, lax.rem(j + r, 8)), device_id_type=MESH
        )
    for k in range(6):
        d = 2**k
        down = divides(d) & (s >= d)
        up = divides(d) & (s + d < 64)
        count = count + down.astype(jnp.int32) + up.astype(jnp.int32)

        @pl.when(down)
        def _():
            pl.semaphore_signal(barrier, inc=1, device_id=(s - d, j), device_id_type=MESH)

        @pl.when(up)
        def _():
            pl.semaphore_signal(barrier, inc=1, device_id=(s + d, j), device_id_type=MESH)

    first = [
        (diag.at[1], d1.at[rows]),
        (coup.at[0], c0.at[rows]),
        (coup.at[1], c1.at[rows]),
        (info, hin.at[pl.ds(pl.multiple_of(j * 8, 8), 8)]),
        (diag.at[0], d2.at[rows]),
    ]
    local = [
        pltpu.make_async_copy(src, dst, own_sem.at[a]) for a, (src, dst) in enumerate(first)
    ]
    for c in local:
        c.start()

    pl.semaphore_wait(barrier, count)

    def to(src, dst, send, recv, tm, state):
        return pltpu.make_async_remote_copy(
            src_ref=src, dst_ref=dst, send_sem=send, recv_sem=recv,
            device_id=(tm, state), device_id_type=MESH,
        )

    def peer(src, dst, sends, recvs, a, r):
        return to(src, dst, sends.at[a, r], recvs.at[a, r], s, lax.rem(j + r, 8))

    for a, (src, dst) in enumerate(first):
        for r in range(1, 8):
            peer(src, dst, g1_send, g1_recv, a, r).start()

    def arrived(a):
        src, dst = first[a]
        local[a].wait()
        for r in range(1, 8):
            peer(src, dst, g1_send, g1_recv, a, r).wait_recv()

    arrived(0)
    factor_start(d1, f1a)

    def fill0():
        arrived(1)
        arrived(2)
        arrived(3)
        info_all = sum8([hin[8 * i : 8 * i + 8, :] for i in range(8)])
        own_h[...] = row_of(info_all, 0)
        xcat[0:N, :] = c0[...]
        xcat[N : 2 * N, :] = jnp.where(s == 63, 0.0, c1[...].T)
        xcat[2 * N : 2 * N + 8, :] = row_of(info_all, 1)

    factor_rest(d1, fill0, xcat, v1, f1a, f2a, za)

    start = pl.multiple_of(j * 32, 32)
    up0 = s < 63

    def up0_sends(act):
        @pl.when(up0)
        def _():
            act(to(pu01, rc1.at[0], s_send.at[0], r1_recv.at[0], s + 1, j))

    def up0_rest(act):
        @pl.when(up0)
        def _():
            act(to(pu02, rc2.at[0], s_send.at[1], r2_recv.at[0], s + 1, j))

    def up0_link(act):
        @pl.when(even)
        def _():
            act(to(sx0, rxl, s_send.at[2], rx_recv.at[0], s + 1, j))

    pu01[...] = nt(v1[N : N + H, :], v1[N : N + H, :])
    up0_sends(lambda c: c.start())
    sx0[...] = -nt(v1[pl.ds(start, 32), :], v1[N : 2 * N, :])
    up0_link(lambda c: c.start())
    pu02[0:H, :] = nt(v1[N + H : 2 * N, :], v1[N : 2 * N, :])
    back = nt(v1[2 * N : 2 * N + 8, :], v1[0 : 2 * N, :])
    pu02[H : H + 8, :] = back[:, N : 2 * N]
    up0_rest(lambda c: c.start())
    own_h[...] = own_h[...] - back[:, 0:N]
    arrived(4)
    d2[...] = d2[...] - nt(v1[0:N, :], v1[0:N, :])

    @pl.when(jnp.logical_not(even))
    def _():
        xu[...] = -nt(v1[N : 2 * N, :], v1[0:N, :])

    def take_lead(slot):
        to(pl1, rc1.at[slot], s_send.at[3], r1_recv.at[slot], s, j).wait_recv()
        d2[0:H, 0:H] = d2[0:H, 0:H] - rc1[slot]

    def take_rest(slot):
        to(pl2, rc2.at[slot], s_send.at[4], r2_recv.at[slot], s, j).wait_recv()
        d2[H:N, :] = d2[H:N, :] - rc2[slot, 0:H, :]
        own_h[...] = own_h[...] - rc2[slot, H : H + 8, :]

    @pl.when(even & (s > 0))
    def _():
        take_lead(0)
        take_rest(0)

    last = [jnp.logical_not(even)]
    for k in range(6):
        at_last = lax.rem(s, 4 * 2**k) == 2 * 2**k
        if k == 5:
            at_last = s == 0
        last.append(at_last)
        early = divides(4 * 2**k) & jnp.logical_not(at_last)

        @pl.when(early & (s > 0))
        def _():
            take_lead(1 + 2 * k)
            take_rest(1 + 2 * k)

        @pl.when(early)
        def _():
            take_lead(2 + 2 * k)
            take_rest(2 + 2 * k)

    def take_last(take):
        @pl.when(last[0])
        def _():
            take(0)

        for k in range(6):
            if k < 5:

                @pl.when(last[k + 1])
                def _():
                    take(1 + 2 * k)

            @pl.when(last[k + 1])
            def _():
                take(2 + 2 * k)

    take_last(take_lead)
    factor_start(d2, f1b)
    take_last(take_rest)

    def each_peer(src, dst, a, act):
        for r in range(1, 8):
            act(peer(src, dst, g2_send, g2_recv, a, r))

    @pl.when(s > 0)
    def _():
        to(sx0, rxl, s_send.at[2], rx_recv.at[0], s, j).wait_recv()
        each_peer(rxl, xl.at[rows], 0, lambda c: c.start())
        xl[rows, :] = rxl[...]

        @pl.when(even)
        def _():
            to(sx, rxu, s_send.at[7], rx_recv.at[1], s, j).wait_recv()
            each_peer(rxu, xu.at[rows], 1, lambda c: c.start())
            xu[rows, :] = rxu[...]

    def fill():
        @pl.when(s > 0)
        def _():
            each_peer(rxl, xl.at[rows], 0, lambda c: c.wait_recv())

            @pl.when(even)
            def _():
                each_peer(rxu, xu.at[rows], 1, lambda c: c.wait_recv())

            xcat[0:N, :] = xl[...]
            xcat[N : 2 * N, :] = xu[...]

        @pl.when(s == 0)
        def _():
            xcat[0 : 2 * N, :] = jnp.zeros((2 * N, N), F32)

        xcat[2 * N : 2 * N + 8, :] = own_h[...]

    factor_rest(d2, fill, xcat, v2, f1b, f2b, zb)

    own_level = []
    to_lower = jnp.bool_(False)
    for k in range(6):
        d = 2**k
        mine = lax.rem(s, 2 * d) == d
        own_level.append((k, d, mine))
        to_lower = to_lower | (mine & (lax.rem(s - d, 4 * d) == 2 * d))

    def sends(lower, upper, lower_dst, upper_dst, recv, at, act):
        for k, d, mine in own_level:

            @pl.when(mine)
            def _():
                slot = 2 + 2 * k
                act(to(lower, lower_dst.at[slot], s_send.at[at], recv.at[slot], s - d, j))

            @pl.when(mine & (s + d < 64))
            def _():
                slot = 1 + 2 * k
                act(to(upper, upper_dst.at[slot], s_send.at[at + 1], recv.at[slot], s + d, j))

    def lead_sends(act):
        sends(pl1, pu1, rc1, rc1, r1_recv, 3, act)

    def rest_sends(act):
        sends(pl2, pu2, rc2, rc2, r2_recv, 5, act)

    def link_sends(act):
        for k, d, mine in own_level[:5]:

            @pl.when(mine & (lax.rem(s - d, 4 * d) == 2 * d))
            def _():
                act(to(sx, rxu, s_send.at[7], rx_recv.at[1], s - d, j))

            @pl.when(mine & (s + d < 64) & (lax.rem(s + d, 4 * d) == 2 * d))
            def _():
                act(to(sx, rxl, s_send.at[7], rx_recv.at[0], s + d, j))

    @pl.when(s > 0)
    def _():
        pl1[...] = nt(v2[0:H, :], v2[0:H, :])
        pu1[...] = nt(v2[N : N + H, :], v2[N : N + H, :])

    lead_sends(lambda c: c.start())

    @pl.when(to_lower)
    def _():
        sx[...] = -nt(v2[pl.ds(start + N, 32), :], v2[0:N, :])

    @pl.when(jnp.logical_not(to_lower) & (s > 0))
    def _():
        sx[...] = -nt(v2[pl.ds(start, 32), :], v2[N : 2 * N, :])

    link_sends(lambda c: c.start())

    @pl.when(s > 0)
    def _():
        pl2[0:H, :] = nt(v2[H:N, :], v2[0:N, :])
        pu2[0:H, :] = nt(v2[N + H : 2 * N, :], v2[N : 2 * N, :])
        back = nt(v2[2 * N : 2 * N + 8, :], v2[0 : 2 * N, :])
        pl2[H : H + 8, :] = back[:, 0:N]
        pu2[H : H + 8, :] = back[:, N : 2 * N]

    rest_sends(lambda c: c.start())

    @pl.when(s > 0)
    def _():
        lo, hi = means(v2, f1b, f2b, zb)
        gb[:, 0:H] = lo
        gb[:, H:N] = hi

    for k, d, mine in own_level:

        @pl.when(mine)
        def _():
            to(xown, xin.at[0], x_send.at[0], x_recv.at[0], s, j).wait_recv()

        @pl.when(mine & (s + d < 64))
        def _():
            to(xown, xin.at[1], x_send.at[0], x_recv.at[1], s, j).wait_recv()

        @pl.when(mine & (s + d >= 64))
        def _():
            xin[1] = jnp.zeros((8, N), F32)

    @pl.when(s == 0)
    def _():
        lo, hi = means(v2[2 * N : 2 * N + 8, :], f1b, f2b, zb)
        xown[:, 0:H] = lo
        xown[:, H:N] = hi

    @pl.when(s > 0)
    def _():
        xown[...] = gb[2 * N : 2 * N + 8, :] - (
            nn(xin[0], gb[0:N, :]) + nn(xin[1], gb[N : 2 * N, :])
        )

    def spread(act):
        for k in reversed(range(6)):
            d = 2**k

            @pl.when(divides(2 * d))
            def _():
                act(to(xown, xin.at[0], x_send.at[2 * k], x_recv.at[0], s + d, j))

            @pl.when(divides(2 * d) & (s > 0))
            def _():
                act(to(xown, xin.at[1], x_send.at[2 * k + 1], x_recv.at[1], s - d, j))

        @pl.when(jnp.logical_not(even))
        def _():
            act(to(xown, xin.at[2], x_send.at[12], x_recv.at[2], s - 1, j))

    spread(lambda c: c.start())

    lo, hi = means(v1, f1a, f2a, za)
    ga[:, 0:H] = lo
    ga[:, H:N] = hi
    part = ga[2 * N : 2 * N + 8, :] - nn(xown[...], ga[0:N, :])

    @pl.when(even)
    def _():
        to(xown, xin.at[2], x_send.at[12], x_recv.at[2], s, j).wait_recv()

    @pl.when(jnp.logical_not(even))
    def _():
        xin[2] = xin[1]

    later = part - nn(xin[2], ga[N : 2 * N, :])
    both = jnp.concatenate([xown[0:1, :], later[0:1, :]], axis=0)
    for i in range(8):

        @pl.when(j == i)
        def _():
            out[...] = both[:, 32 * i : 32 * i + 32]

    for a, (src, dst) in enumerate(first):
        for r in range(1, 8):
            peer(src, dst, g1_send, g1_recv, a, r).wait_send()

    up0_sends(lambda c: c.wait_send())
    up0_link(lambda c: c.wait_send())
    up0_rest(lambda c: c.wait_send())

    @pl.when(s > 0)
    def _():
        each_peer(rxl, xl.at[rows], 0, lambda c: c.wait_send())

        @pl.when(even)
        def _():
            each_peer(rxu, xu.at[rows], 1, lambda c: c.wait_send())

    lead_sends(lambda c: c.wait_send())
    link_sends(lambda c: c.wait_send())
    rest_sends(lambda c: c.wait_send())
    spread(lambda c: c.wait_send())


def body(diagonal, coupling, info):
    offset = lax.axis_index("state") * 32
    placed = lax.dynamic_update_slice(jnp.zeros((8, N), F32), info, (0, offset))
    vmem = pltpu.VMEM
    dma = pltpu.SemaphoreType.DMA
    square = vmem((N, N), F32)
    half = vmem((H, H), F32)
    tall = vmem((2 * N + 8, N), F32)
    slab = vmem((H + 8, N), F32)
    slice_ = vmem((32, N), F32)
    return pl.pallas_call(
        kernel,
        out_shape=jax.ShapeDtypeStruct((2, 32), F32),
        in_specs=[pl.BlockSpec(memory_space=pl.ANY)] * 3,
        out_specs=pl.BlockSpec(memory_space=vmem),
        scratch_shapes=[
            square, square, square, vmem((64, N), F32), square, square, square, tall, tall, tall,
            half, half, half, half, half, half, tall, tall,
            vmem((8, N), F32), vmem((13, H, H), F32), vmem((13, H + 8, N), F32),
            slice_, slice_, half, slab, slice_, half, slab, half, slab, slice_,
            vmem((3, 8, N), F32), vmem((8, N), F32),
            dma((5, 8)), dma((5, 8)), dma((2, 8)), dma((2, 8)),
            dma((13,)), dma((13,)), dma((2,)), dma((8,)), dma((13,)), dma((3,)), dma((5,)),
        ],
        compiler_params=pltpu.CompilerParams(
            collective_id=0, has_side_effects=True, vmem_limit_bytes=32 * 1024 * 1024
        ),
    )(diagonal, coupling, placed)


def solution(mesh):
    placed = (P("tm", "state", None), P("tm", "state", None), P("tm", "state"))
    return jax.shard_map(
        body, mesh=mesh, in_specs=placed, out_specs=P("tm", "state"), check_vma=False
    )
```

```python
import jax
import jax.numpy as jnp
from jax import lax
from jax.experimental import pallas as pl
from jax.experimental.pallas import tpu as pltpu
from jax.sharding import PartitionSpec as P

N = 256
H = 128
F32 = jnp.float32
MESH = pl.DeviceIdType.MESH
EXACT = lax.Precision.HIGHEST


def nt(a, b):
    return lax.dot_general(
        a, b, (((1,), (1,)), ((), ())), precision=EXACT, preferred_element_type=F32
    )


def nn(a, b):
    return jnp.dot(a, b, precision=EXACT, preferred_element_type=F32)


def row_of(x, k):
    return jnp.broadcast_to(x[k : k + 1, :], x.shape)


def lane_of(x, l):
    return jnp.take_along_axis(x, jnp.full((8, H), l, jnp.int32), axis=1)


def sum8(t):
    return ((t[0] + t[1]) + (t[2] + t[3])) + ((t[4] + t[5]) + (t[6] + t[7]))


def pivot_block(w, b, sub, lane):
    at = 8 * b
    c = [lane_of(w[b], at + j) for j in range(8)]
    inside = (lane >= at) & (lane < at + 8)
    r = jnp.where(inside, (lane - at == sub).astype(F32), w[b])
    t = r
    pivots = jnp.ones((8, H), F32)
    inverses = []
    for k in range(0, 8, 2):
        first, second = sub == k, sub == k + 1
        p, q, o = row_of(c[k], k), row_of(c[k + 1], k), row_of(c[k + 1], k + 1)
        det = 1.0 / (p * o - q * q)
        m0 = jnp.where(first | second, 0.0, c[k])
        m1 = jnp.where(first | second, 0.0, c[k + 1])
        f0 = (m0 * o - m1 * q) * det
        f1 = (m1 * p - m0 * q) * det
        inverses.append((o * det, -q * det, p * det))
        ratio = q * (1.0 / p)
        r0, r1 = row_of(r, k), row_of(r, k + 1)
        t = jnp.where(first, r0, jnp.where(second, r1 - ratio * r0, t))
        pivots = jnp.where(first, p, jnp.where(second, o - ratio * q, pivots))
        for j in range(k + 2, 8):
            c[j] = c[j] - (f0 * row_of(c[j], k) + f1 * row_of(c[j], k + 1))
        r = r - (f0 * r0 + f1 * r1)
    if b < 15:
        rows = []
        for k in range(0, 8, 2):
            ia, ib, ic = inverses[k // 2]
            r0, r1 = row_of(r, k), row_of(r, k + 1)
            rows += [ia * r0 + ib * r1, ib * r0 + ic * r1]
        for i in range(b + 1, 16):
            cols = [lane_of(w[i], at + j) for j in range(8)]
            w[i] = jnp.where(inside, 0.0, w[i]) - sum8([cols[j] * rows[j] for j in range(8)])
    return jnp.where(lane < at + 8, t * lax.rsqrt(pivots), 0.0)


def factor_part(w, blocks):
    sub = lax.broadcasted_iota(jnp.int32, (8, H), 0)
    lane = lax.broadcasted_iota(jnp.int32, (8, H), 1)
    return [pivot_block(w, b, sub, lane) for b in blocks]


def groups(a):
    return [a[8 * r : 8 * r + 8, :] for r in range(16)]


def factor_start(block, begin, f1):
    w = groups(block[0:H, 0:H])
    out = factor_part(w, range(4))
    begin()
    out += factor_part(w, range(4, 16))
    f1[...] = jnp.concatenate(out, axis=0)


def factor_rest(block, fill, x, v, y, f1, f2, z, lead):
    z[...] = nt(block[H:N, 0:H], f1[...])
    w = groups(block[H:N, H:N] - nt(z[...], z[...]))
    out = factor_part(w, range(12))
    fill()
    v[:, 0:H] = nt(x[:, 0:H], f1[...])
    y[...] = x[:, H:N] - nt(v[:, 0:H], z[...])
    for at, to in lead:
        to[...] = nt(v[at : at + H, 0:H], v[at : at + H, 0:H])
    out += factor_part(w, range(12, 16))
    f2[...] = jnp.concatenate(out, axis=0)
    for at, to in lead:
        top = nt(y[at : at + H, :], f2[...])
        v[at : at + H, H:N] = top
        to[...] = to[...] + nt(top, top)


def finish_rows(v, y, f2, done):
    at = [r for r in (0, H, N, N + H) if r not in done]
    for r in at:
        v[r : r + H, H:N] = nt(y[r : r + H, :], f2[...])
    v[2 * N : 2 * N + 8, H:N] = nt(y[2 * N : 2 * N + 8, :], f2[...])


def means(v, f1, f2, z):
    hi = nn(v[:, H:N], f2[...])
    lo = nn(v[:, 0:H] - nn(hi, z[...]), f1[...])
    return lo, hi


def kernel(
    diag, coup, info, out,
    d1, c0, c1, hin, d2, xl, xu, xcat, ycat, v1, v2, f1a, f2a, za, f1b, f2b, zb, ga, gb,
    own_h, rc1, rc2, rxl, rxu, pu01, pu02, sx0, pl1, pl2, pu1, pu2, sx, xin, xown,
    g1_send, g1_recv, g2_send, g2_recv, r1_recv, r2_recv, rx_recv, s_send, x_send, x_recv, own_sem,
):
    s = lax.axis_index("tm")
    j = lax.axis_index("state")
    rows = pl.ds(pl.multiple_of(j * 32, 32), 32)

    def divides(d):
        return lax.rem(s, d) == 0

    even = divides(2)

    barrier = pltpu.get_barrier_semaphore()
    count = jnp.int32(7)
    for r in range(1, 8):
        pl.semaphore_signal(
            barrier, inc=1, device_id=(s, lax.rem(j + r, 8)), device_id_type=MESH
        )
    for k in range(6):
        d = 2**k
        down = divides(d) & (s >= d)
        up = divides(d) & (s + d < 64)
        count = count + down.astype(jnp.int32) + up.astype(jnp.int32)

        @pl.when(down)
        def _():
            pl.semaphore_signal(barrier, inc=1, device_id=(s - d, j), device_id_type=MESH)

        @pl.when(up)
        def _():
            pl.semaphore_signal(barrier, inc=1, device_id=(s + d, j), device_id_type=MESH)

    first = [
        (diag.at[1], d1.at[rows]),
        (coup.at[0], c0.at[rows]),
        (coup.at[1], c1.at[rows]),
        (info, hin.at[pl.ds(pl.multiple_of(j * 8, 8), 8)]),
        (diag.at[0], d2.at[rows]),
    ]
    local = [
        pltpu.make_async_copy(src, dst, own_sem.at[a]) for a, (src, dst) in enumerate(first)
    ]
    for c in local:
        c.start()

    pl.semaphore_wait(barrier, count)

    def to(src, dst, send, recv, tm, state):
        return pltpu.make_async_remote_copy(
            src_ref=src, dst_ref=dst, send_sem=send, recv_sem=recv,
            device_id=(tm, state), device_id_type=MESH,
        )

    def peer(src, dst, sends, recvs, a, r):
        return to(src, dst, sends.at[a, r], recvs.at[a, r], s, lax.rem(j + r, 8))

    def gather(a, act):
        src, dst = first[a]
        for r in range(1, 8):
            act(peer(src, dst, g1_send, g1_recv, a, r))

    gather(0, lambda c: c.start())
    gather(0, lambda c: c.wait_send())
    for a in range(1, 5):
        gather(a, lambda c: c.start())

    def arrived(a):
        local[a].wait()
        gather(a, lambda c: c.wait_recv())

    arrived(0)
    factor_start(d1, lambda: None, f1a)

    def fill0():
        arrived(1)
        arrived(2)
        arrived(3)
        info_all = sum8([hin[8 * i : 8 * i + 8, :] for i in range(8)])
        own_h[...] = row_of(info_all, 0)
        xcat[0:N, :] = c0[...]
        xcat[N : 2 * N, :] = jnp.where(s == 63, 0.0, c1[...].T)
        xcat[2 * N : 2 * N + 8, :] = row_of(info_all, 1)

    factor_rest(d1, fill0, xcat, v1, ycat, f1a, f2a, za, [(N, pu01)])

    start = pl.multiple_of(j * 32, 32)
    up0 = s < 63

    def up0_sends(act):
        @pl.when(up0)
        def _():
            act(to(pu01, rc1.at[0], s_send.at[0], r1_recv.at[0], s + 1, j))

    def up0_rest(act):
        @pl.when(up0)
        def _():
            act(to(pu02, rc2.at[0], s_send.at[1], r2_recv.at[0], s + 1, j))

    def up0_link(act):
        @pl.when(even)
        def _():
            act(to(sx0, rxl, s_send.at[2], rx_recv.at[0], s + 1, j))

    up0_sends(lambda c: c.start())
    finish_rows(v1, ycat, f2a, [N])
    sx0[...] = -nt(v1[pl.ds(start, 32), :], v1[N : 2 * N, :])
    up0_link(lambda c: c.start())
    pu02[0:H, :] = nt(v1[N + H : 2 * N, :], v1[N : 2 * N, :])
    back = nt(v1[2 * N : 2 * N + 8, :], v1[0 : 2 * N, :])
    pu02[H : H + 8, :] = back[:, N : 2 * N]
    up0_rest(lambda c: c.start())
    own_h[...] = own_h[...] - back[:, 0:N]
    arrived(4)
    d2[...] = d2[...] - nt(v1[0:N, :], v1[0:N, :])

    @pl.when(jnp.logical_not(even))
    def _():
        xu[...] = -nt(v1[N : 2 * N, :], v1[0:N, :])

    def take_lead(slot):
        to(pl1, rc1.at[slot], s_send.at[3], r1_recv.at[slot], s, j).wait_recv()
        d2[0:H, 0:H] = d2[0:H, 0:H] - rc1[slot]

    def take_rest(slot):
        to(pl2, rc2.at[slot], s_send.at[4], r2_recv.at[slot], s, j).wait_recv()
        d2[H:N, :] = d2[H:N, :] - rc2[slot, 0:H, :]
        own_h[...] = own_h[...] - rc2[slot, H : H + 8, :]

    @pl.when(even & (s > 0))
    def _():
        take_lead(0)
        take_rest(0)

    last = [jnp.logical_not(even)]
    for k in range(6):
        at_last = lax.rem(s, 4 * 2**k) == 2 * 2**k
        if k == 5:
            at_last = s == 0
        last.append(at_last)
        early = divides(4 * 2**k) & jnp.logical_not(at_last)

        @pl.when(early & (s > 0))
        def _():
            take_lead(1 + 2 * k)
            take_rest(1 + 2 * k)

        @pl.when(early)
        def _():
            take_lead(2 + 2 * k)
            take_rest(2 + 2 * k)

    def take_last(take):
        @pl.when(last[0])
        def _():
            take(0)

        for k in range(6):
            if k < 5:

                @pl.when(last[k + 1])
                def _():
                    take(1 + 2 * k)

            @pl.when(last[k + 1])
            def _():
                take(2 + 2 * k)

    take_last(take_lead)

    def each_peer(src, dst, a, act):
        for r in range(1, 8):
            act(peer(src, dst, g2_send, g2_recv, a, r))

    def begin():
        @pl.when(s > 0)
        def _():
            to(sx0, rxl, s_send.at[2], rx_recv.at[0], s, j).wait_recv()
            each_peer(rxl, xl.at[rows], 0, lambda c: c.start())
            xl[rows, :] = rxl[...]

            @pl.when(even)
            def _():
                to(sx, rxu, s_send.at[7], rx_recv.at[1], s, j).wait_recv()
                each_peer(rxu, xu.at[rows], 1, lambda c: c.start())
                xu[rows, :] = rxu[...]

    def fill():
        @pl.when(s > 0)
        def _():
            each_peer(rxl, xl.at[rows], 0, lambda c: c.wait_recv())

            @pl.when(even)
            def _():
                each_peer(rxu, xu.at[rows], 1, lambda c: c.wait_recv())

            xcat[0:N, :] = xl[...]
            xcat[N : 2 * N, :] = xu[...]

        @pl.when(s == 0)
        def _():
            xcat[0 : 2 * N, :] = jnp.zeros((2 * N, N), F32)

        xcat[2 * N : 2 * N + 8, :] = own_h[...]

    factor_start(d2, begin, f1b)
    take_last(take_rest)
    factor_rest(d2, fill, xcat, v2, ycat, f1b, f2b, zb, [(0, pl1), (N, pu1)])

    own_level = []
    to_lower = jnp.bool_(False)
    for k in range(6):
        d = 2**k
        mine = lax.rem(s, 2 * d) == d
        own_level.append((k, d, mine))
        to_lower = to_lower | (mine & (lax.rem(s - d, 4 * d) == 2 * d))

    def sends(lower, upper, lower_dst, upper_dst, recv, at, act):
        for k, d, mine in own_level:

            @pl.when(mine)
            def _():
                slot = 2 + 2 * k
                act(to(lower, lower_dst.at[slot], s_send.at[at], recv.at[slot], s - d, j))

            @pl.when(mine & (s + d < 64))
            def _():
                slot = 1 + 2 * k
                act(to(upper, upper_dst.at[slot], s_send.at[at + 1], recv.at[slot], s + d, j))

    def lead_sends(act):
        sends(pl1, pu1, rc1, rc1, r1_recv, 3, act)

    def rest_sends(act):
        sends(pl2, pu2, rc2, rc2, r2_recv, 5, act)

    def link_sends(act):
        for k, d, mine in own_level[:5]:

            @pl.when(mine & (lax.rem(s - d, 4 * d) == 2 * d))
            def _():
                act(to(sx, rxu, s_send.at[7], rx_recv.at[1], s - d, j))

            @pl.when(mine & (s + d < 64) & (lax.rem(s + d, 4 * d) == 2 * d))
            def _():
                act(to(sx, rxl, s_send.at[7], rx_recv.at[0], s + d, j))

    lead_sends(lambda c: c.start())
    finish_rows(v2, ycat, f2b, [0, N])

    @pl.when(to_lower)
    def _():
        sx[...] = -nt(v2[pl.ds(start + N, 32), :], v2[0:N, :])

    @pl.when(jnp.logical_not(to_lower) & (s > 0))
    def _():
        sx[...] = -nt(v2[pl.ds(start, 32), :], v2[N : 2 * N, :])

    link_sends(lambda c: c.start())

    @pl.when(s > 0)
    def _():
        pl2[0:H, :] = nt(v2[H:N, :], v2[0:N, :])
        pu2[0:H, :] = nt(v2[N + H : 2 * N, :], v2[N : 2 * N, :])
        back = nt(v2[2 * N : 2 * N + 8, :], v2[0 : 2 * N, :])
        pl2[H : H + 8, :] = back[:, 0:N]
        pu2[H : H + 8, :] = back[:, N : 2 * N]

    rest_sends(lambda c: c.start())

    @pl.when(s > 0)
    def _():
        lo, hi = means(v2, f1b, f2b, zb)
        gb[:, 0:H] = lo
        gb[:, H:N] = hi

    def early_means():
        lo, hi = means(v1, f1a, f2a, za)
        ga[:, 0:H] = lo
        ga[:, H:N] = hi

    @pl.when(s > 0)
    def _():
        early_means()

    for k, d, mine in own_level:

        @pl.when(mine)
        def _():
            to(xown, xin.at[0], x_send.at[0], x_recv.at[0], s, j).wait_recv()

        @pl.when(mine & (s + d < 64))
        def _():
            to(xown, xin.at[1], x_send.at[0], x_recv.at[1], s, j).wait_recv()

        @pl.when(mine & (s + d >= 64))
        def _():
            xin[1] = jnp.zeros((8, N), F32)

    @pl.when(s == 0)
    def _():
        lo, hi = means(v2[2 * N : 2 * N + 8, :], f1b, f2b, zb)
        xown[:, 0:H] = lo
        xown[:, H:N] = hi

    @pl.when(s > 0)
    def _():
        xown[...] = gb[2 * N : 2 * N + 8, :] - (
            nn(xin[0], gb[0:N, :]) + nn(xin[1], gb[N : 2 * N, :])
        )

    def spread(act):
        for k in reversed(range(6)):
            d = 2**k

            @pl.when(divides(2 * d))
            def _():
                act(to(xown, xin.at[0], x_send.at[2 * k], x_recv.at[0], s + d, j))

            @pl.when(divides(2 * d) & (s > 0))
            def _():
                act(to(xown, xin.at[1], x_send.at[2 * k + 1], x_recv.at[1], s - d, j))

        @pl.when(jnp.logical_not(even))
        def _():
            act(to(xown, xin.at[2], x_send.at[12], x_recv.at[2], s - 1, j))

    spread(lambda c: c.start())

    @pl.when(s == 0)
    def _():
        early_means()

    part = ga[2 * N : 2 * N + 8, :] - nn(xown[...], ga[0:N, :])

    @pl.when(even)
    def _():
        to(xown, xin.at[2], x_send.at[12], x_recv.at[2], s, j).wait_recv()

    @pl.when(jnp.logical_not(even))
    def _():
        xin[2] = xin[1]

    later = part - nn(xin[2], ga[N : 2 * N, :])
    both = jnp.concatenate([xown[0:1, :], later[0:1, :]], axis=0)
    for i in range(8):

        @pl.when(j == i)
        def _():
            out[...] = both[:, 32 * i : 32 * i + 32]

    for a in range(1, 5):
        gather(a, lambda c: c.wait_send())

    up0_sends(lambda c: c.wait_send())
    up0_link(lambda c: c.wait_send())
    up0_rest(lambda c: c.wait_send())

    @pl.when(s > 0)
    def _():
        each_peer(rxl, xl.at[rows], 0, lambda c: c.wait_send())

        @pl.when(even)
        def _():
            each_peer(rxu, xu.at[rows], 1, lambda c: c.wait_send())

    lead_sends(lambda c: c.wait_send())
    link_sends(lambda c: c.wait_send())
    rest_sends(lambda c: c.wait_send())
    spread(lambda c: c.wait_send())


def body(diagonal, coupling, info):
    offset = lax.axis_index("state") * 32
    placed = lax.dynamic_update_slice(jnp.zeros((8, N), F32), info, (0, offset))
    vmem = pltpu.VMEM
    dma = pltpu.SemaphoreType.DMA
    square = vmem((N, N), F32)
    half = vmem((H, H), F32)
    tall = vmem((2 * N + 8, N), F32)
    slab = vmem((H + 8, N), F32)
    slice_ = vmem((32, N), F32)
    return pl.pallas_call(
        kernel,
        out_shape=jax.ShapeDtypeStruct((2, 32), F32),
        in_specs=[pl.BlockSpec(memory_space=pltpu.HBM)] * 3,
        out_specs=pl.BlockSpec(memory_space=vmem),
        scratch_shapes=[
            square, square, square, vmem((64, N), F32), square, square, square, tall, vmem((2 * N + 8, H), F32), tall, tall,
            half, half, half, half, half, half, tall, tall,
            vmem((8, N), F32), vmem((13, H, H), F32), vmem((13, H + 8, N), F32),
            slice_, slice_, half, slab, slice_, half, slab, half, slab, slice_,
            vmem((3, 8, N), F32), vmem((8, N), F32),
            dma((5, 8)), dma((5, 8)), dma((2, 8)), dma((2, 8)),
            dma((13,)), dma((13,)), dma((2,)), dma((8,)), dma((13,)), dma((3,)), dma((5,)),
        ],
        compiler_params=pltpu.CompilerParams(
            collective_id=0, has_side_effects=True, vmem_limit_bytes=32 * 1024 * 1024
        ),
    )(diagonal, coupling, placed)


def solution(mesh):
    placed = (P("tm", "state", None), P("tm", "state", None), P("tm", "state"))
    return jax.shard_map(
        body, mesh=mesh, in_specs=placed, out_specs=P("tm", "state"), check_vma=False
    )
```

```python
import jax
import jax.numpy as jnp
from jax import lax
from jax.experimental import pallas as pl
from jax.experimental.pallas import tpu as pltpu
from jax.sharding import PartitionSpec as P

N = 256
H = 128
Q = 64
F32 = jnp.float32
MESH = pl.DeviceIdType.MESH
EXACT = lax.Precision.HIGHEST


def nt(a, b):
    return lax.dot_general(
        a, b, (((1,), (1,)), ((), ())), precision=EXACT, preferred_element_type=F32
    )


def nn(a, b):
    return jnp.dot(a, b, precision=EXACT, preferred_element_type=F32)


def row_of(x, k):
    return jnp.broadcast_to(x[k : k + 1, :], x.shape)


def lane_of(x, l):
    return jnp.take_along_axis(x, jnp.full((8, H), l, jnp.int32), axis=1)


def sum8(t):
    return ((t[0] + t[1]) + (t[2] + t[3])) + ((t[4] + t[5]) + (t[6] + t[7]))


def pivot_block(w, b, sub, lane):
    at = 8 * b
    c = [lane_of(w[b], at + j) for j in range(8)]
    inside = (lane >= at) & (lane < at + 8)
    r = jnp.where(inside, (lane - at == sub).astype(F32), w[b])
    t = r
    pivots = jnp.ones((8, H), F32)
    inverses = []
    for k in range(0, 8, 2):
        first, second = sub == k, sub == k + 1
        p, q, o = row_of(c[k], k), row_of(c[k + 1], k), row_of(c[k + 1], k + 1)
        det = 1.0 / (p * o - q * q)
        m0 = jnp.where(first | second, 0.0, c[k])
        m1 = jnp.where(first | second, 0.0, c[k + 1])
        f0 = (m0 * o - m1 * q) * det
        f1 = (m1 * p - m0 * q) * det
        inverses.append((o * det, -q * det, p * det))
        ratio = q * (1.0 / p)
        r0, r1 = row_of(r, k), row_of(r, k + 1)
        t = jnp.where(first, r0, jnp.where(second, r1 - ratio * r0, t))
        pivots = jnp.where(first, p, jnp.where(second, o - ratio * q, pivots))
        for j in range(k + 2, 8):
            c[j] = c[j] - (f0 * row_of(c[j], k) + f1 * row_of(c[j], k + 1))
        r = r - (f0 * r0 + f1 * r1)
    if b < 15:
        rows = []
        for k in range(0, 8, 2):
            ia, ib, ic = inverses[k // 2]
            r0, r1 = row_of(r, k), row_of(r, k + 1)
            rows += [ia * r0 + ib * r1, ib * r0 + ic * r1]
        for i in range(b + 1, 16):
            cols = [lane_of(w[i], at + j) for j in range(8)]
            w[i] = jnp.where(inside, 0.0, w[i]) - sum8([cols[j] * rows[j] for j in range(8)])
    return jnp.where(lane < at + 8, t * lax.rsqrt(pivots), 0.0)


def factor_part(w, blocks):
    sub = lax.broadcasted_iota(jnp.int32, (8, H), 0)
    lane = lax.broadcasted_iota(jnp.int32, (8, H), 1)
    return [pivot_block(w, b, sub, lane) for b in blocks]


def groups(a):
    return [a[8 * r : 8 * r + 8, :] for r in range(16)]


def factor_start(block, begin, f1):
    w = groups(block[0:H, 0:H])
    out = factor_part(w, range(8))
    begin()
    out += factor_part(w, range(8, 16))
    f1[...] = jnp.concatenate(out, axis=0)


def factor_rest(block, pass_on, fill, x, v, y, f1, f2, z, lead):
    z[...] = nt(block[H:N, 0:H], f1[...])
    w = groups(block[H:N, H:N] - nt(z[...], z[...]))
    out = factor_part(w, range(2))
    pass_on()
    out += factor_part(w, range(2, 12))
    fill()
    v[:, 0:H] = nt(x[:, 0:H], f1[...])
    y[...] = x[:, H:N] - nt(v[:, 0:H], z[...])
    for at, to in lead:
        to[...] = nt(v[at : at + H, 0:H], v[at : at + H, 0:H])
    out += factor_part(w, range(12, 16))
    f2[...] = jnp.concatenate(out, axis=0)
    for at, to in lead:
        top = nt(y[at : at + H, :], f2[...])
        v[at : at + H, H:N] = top
        to[...] = to[...] + nt(top, top)


def finish_rows(v, y, f2, done):
    at = [r for r in (0, H, N, N + H) if r not in done]
    for r in at:
        v[r : r + H, H:N] = nt(y[r : r + H, :], f2[...])
    v[2 * N : 2 * N + 8, H:N] = nt(y[2 * N : 2 * N + 8, :], f2[...])


def means(v, f1, f2, z):
    hi = nn(v[:, H:N], f2[...])
    lo = nn(v[:, 0:H] - nn(hi, z[...]), f1[...])
    return lo, hi


def kernel(
    diag, coup, info, out,
    d1, c0, c1, hin, d2, xl, xu, xcat, ycat, v1, v2, f1a, f2a, za, f1b, f2b, zb, ga, gb,
    own_h, rc1, rc2, dsib, pu01, pu02, sx0, pl1, pl2, pu1, pu2, sx, xin, xown,
    g1_send, g1_recv, sib_send, sib_recv, r1_recv, r2_recv, rx_recv, s_send, x_send, x_recv, own_sem,
):
    s = lax.axis_index("tm")
    j = lax.axis_index("state")
    core = lax.rem(j, 2)
    sibling = j + 1 - 2 * core
    rows = pl.ds(pl.multiple_of(j * 32, 32), 32)
    half_rows = pl.ds(pl.multiple_of(core * H, H), H)
    own_rows = pl.ds(pl.multiple_of(H + core * Q, Q), Q)
    other_rows = pl.ds(pl.multiple_of(H + Q - core * Q, Q), Q)

    def divides(d):
        return lax.rem(s, d) == 0

    even = divides(2)

    barrier = pltpu.get_barrier_semaphore()
    count = jnp.int32(7)
    for r in range(1, 8):
        pl.semaphore_signal(
            barrier, inc=1, device_id=(s, lax.rem(j + r, 8)), device_id_type=MESH
        )
    for k in range(6):
        d = 2**k
        down = divides(d) & (s >= d)
        up = divides(d) & (s + d < 64)
        count = count + down.astype(jnp.int32) + up.astype(jnp.int32)

        @pl.when(down)
        def _():
            pl.semaphore_signal(barrier, inc=1, device_id=(s - d, j), device_id_type=MESH)

        @pl.when(up)
        def _():
            pl.semaphore_signal(barrier, inc=1, device_id=(s + d, j), device_id_type=MESH)

    first = [
        (diag.at[1], d1.at[rows]),
        (coup.at[0], c0.at[rows]),
        (coup.at[1], c1.at[rows]),
        (info, hin.at[pl.ds(pl.multiple_of(j * 8, 8), 8)]),
        (diag.at[0], d2.at[rows]),
    ]
    local = [
        pltpu.make_async_copy(src, dst, own_sem.at[a]) for a, (src, dst) in enumerate(first)
    ]
    for c in local:
        c.start()

    pl.semaphore_wait(barrier, count)

    def to(src, dst, send, recv, tm, state):
        return pltpu.make_async_remote_copy(
            src_ref=src, dst_ref=dst, send_sem=send, recv_sem=recv,
            device_id=(tm, state), device_id_type=MESH,
        )

    def peer(src, dst, sends, recvs, a, r):
        return to(src, dst, sends.at[a, r], recvs.at[a, r], s, lax.rem(j + r, 8))

    def gather(a, act):
        src, dst = first[a]
        for r in range(1, 8):
            act(peer(src, dst, g1_send, g1_recv, a, r))

    def direct(a, act):
        src, dst = first[a]
        for r in (2, 4, 6):
            act(peer(src, dst, g1_send, g1_recv, a, r))
        act(to(src, dst, g1_send.at[a, 1], g1_recv.at[a, 1], s, sibling))

    def hand_on(a, act):
        whole = (None, c0, c1, None, d2)[a]
        for r in (2, 4, 6):
            at = pl.ds(pl.multiple_of(lax.rem(j + 8 - r, 8) * 32, 32), 32)
            piece = whole.at[at]
            act(to(piece, piece, g1_send.at[a, r + 1], g1_recv.at[a, r + 1], s, sibling))

    def direct_arrived(a):
        src, dst = first[a]
        for r in (2, 4, 6):
            peer(src, dst, g1_send, g1_recv, a, r).wait_recv()

    def arrived(a):
        src, dst = first[a]
        local[a].wait()
        to(src, dst, g1_send.at[a, 1], g1_recv.at[a, 1], s, sibling).wait_recv()
        hand_on(a, lambda c: c.wait_recv())

    gather(0, lambda c: c.start())
    gather(0, lambda c: c.wait_send())
    for a in (1, 2, 4):
        direct(a, lambda c: c.start())
    gather(3, lambda c: c.start())

    local[0].wait()
    gather(0, lambda c: c.wait_recv())
    factor_start(d1, lambda: None, f1a)

    def pass_on0():
        for a in (1, 2):
            direct_arrived(a)
            hand_on(a, lambda c: c.start())

    def fill0():
        direct_arrived(4)
        hand_on(4, lambda c: c.start())
        arrived(1)
        arrived(2)
        local[3].wait()
        gather(3, lambda c: c.wait_recv())
        info_all = sum8([hin[8 * i : 8 * i + 8, :] for i in range(8)])
        own_h[...] = row_of(info_all, 0)
        xcat[0:N, :] = c0[...]
        xcat[N : 2 * N, :] = jnp.where(s == 63, 0.0, c1[...].T)
        xcat[2 * N : 2 * N + 8, :] = row_of(info_all, 1)

    factor_rest(d1, pass_on0, fill0, xcat, v1, ycat, f1a, f2a, za, [(N, pu01)])

    half_at = pl.multiple_of(core * H, H)
    own_at = pl.multiple_of(H + core * Q, Q)
    up0 = s < 63

    def up0_sends(act):
        @pl.when(up0)
        def _():
            act(to(pu01, rc1.at[0], s_send.at[0], r1_recv.at[0], s + 1, j))

    def up0_rest(act):
        @pl.when(up0)
        def _():
            act(to(pu02, rc2.at[0], s_send.at[1], r2_recv.at[0], s + 1, j))

    def up0_link(act):
        @pl.when(even)
        def _():
            act(to(sx0, xl.at[half_rows], s_send.at[2], rx_recv.at[0], s + 1, j))

    up0_sends(lambda c: c.start())
    finish_rows(v1, ycat, f2a, [N])
    pu02[0:Q, :] = nt(v1[pl.ds(own_at + N, Q), :], v1[N : 2 * N, :])
    back = nt(v1[2 * N : 2 * N + 8, :], v1[0 : 2 * N, :])
    pu02[Q : Q + 8, :] = back[:, N : 2 * N]
    up0_rest(lambda c: c.start())
    sx0[...] = -nt(v1[pl.ds(half_at, H), :], v1[N : 2 * N, :])
    up0_link(lambda c: c.start())
    own_h[...] = own_h[...] - back[:, 0:N]
    arrived(4)
    hand_on(4, lambda c: c.wait_send())
    d2[0:H, 0:H] = d2[0:H, 0:H] - nt(v1[0:H, :], v1[0:H, :])
    d2[own_rows, :] = d2[own_rows, :] - nt(v1[own_rows, :], v1[0:N, :])

    @pl.when(jnp.logical_not(even))
    def _():
        xu[...] = -nt(v1[N : 2 * N, :], v1[0:N, :])

    def take_lead(slot):
        to(pl1, rc1.at[slot], s_send.at[3], r1_recv.at[slot], s, j).wait_recv()
        d2[0:H, 0:H] = d2[0:H, 0:H] - rc1[slot]

    def take_rest(slot):
        to(pl2, rc2.at[slot], s_send.at[4], r2_recv.at[slot], s, j).wait_recv()
        d2[own_rows, :] = d2[own_rows, :] - rc2[slot, 0:Q, :]
        own_h[...] = own_h[...] - rc2[slot, Q : Q + 8, :]

    @pl.when(even & (s > 0))
    def _():
        take_lead(0)
        take_rest(0)

    last = [jnp.logical_not(even)]
    for k in range(6):
        at_last = lax.rem(s, 4 * 2**k) == 2 * 2**k
        if k == 5:
            at_last = s == 0
        last.append(at_last)
        early = divides(4 * 2**k) & jnp.logical_not(at_last)

        @pl.when(early & (s > 0))
        def _():
            take_lead(1 + 2 * k)
            take_rest(1 + 2 * k)

        @pl.when(early)
        def _():
            take_lead(2 + 2 * k)
            take_rest(2 + 2 * k)

    def take_last(take):
        @pl.when(last[0])
        def _():
            take(0)

        for k in range(6):
            if k < 5:

                @pl.when(last[k + 1])
                def _():
                    take(1 + 2 * k)

            @pl.when(last[k + 1])
            def _():
                take(2 + 2 * k)

    take_last(take_lead)

    def hand(ref_rows, dst, a):
        return to(ref_rows, dst, sib_send.at[a], sib_recv.at[a], s, sibling)

    def hand_rest():
        return hand(d2.at[own_rows], dsib, 0)

    def hand_xl():
        return hand(xl.at[half_rows], xl.at[half_rows], 1)

    def hand_xu():
        return hand(xu.at[half_rows], xu.at[half_rows], 2)

    def begin():
        take_last(take_rest)
        hand_rest().start()

    def pass_on():
        @pl.when(s > 0)
        def _():
            to(sx0, xl.at[half_rows], s_send.at[2], rx_recv.at[0], s, j).wait_recv()
            hand_xl().start()

        @pl.when(even & (s > 0))
        def _():
            to(sx, xu.at[half_rows], s_send.at[7], rx_recv.at[1], s, j).wait_recv()
            hand_xu().start()

    def fill():
        @pl.when(s > 0)
        def _():
            hand_xl().wait_recv()

            @pl.when(even)
            def _():
                hand_xu().wait_recv()

            xcat[0:N, :] = xl[...]
            xcat[N : 2 * N, :] = xu[...]

        @pl.when(s == 0)
        def _():
            xcat[0 : 2 * N, :] = jnp.zeros((2 * N, N), F32)

        xcat[2 * N : 2 * N + 8, :] = own_h[...]

    factor_start(d2, begin, f1b)
    hand_rest().wait_recv()
    d2[other_rows, :] = dsib[...]
    factor_rest(d2, pass_on, fill, xcat, v2, ycat, f1b, f2b, zb, [(0, pl1), (N, pu1)])

    own_level = []
    to_lower = jnp.bool_(False)
    for k in range(6):
        d = 2**k
        mine = lax.rem(s, 2 * d) == d
        own_level.append((k, d, mine))
        to_lower = to_lower | (mine & (lax.rem(s - d, 4 * d) == 2 * d))

    def sends(lower, upper, lower_dst, upper_dst, recv, at, act):
        for k, d, mine in own_level:

            @pl.when(mine)
            def _():
                slot = 2 + 2 * k
                act(to(lower, lower_dst.at[slot], s_send.at[at], recv.at[slot], s - d, j))

            @pl.when(mine & (s + d < 64))
            def _():
                slot = 1 + 2 * k
                act(to(upper, upper_dst.at[slot], s_send.at[at + 1], recv.at[slot], s + d, j))

    def lead_sends(act):
        sends(pl1, pu1, rc1, rc1, r1_recv, 3, act)

    def rest_sends(act):
        sends(pl2, pu2, rc2, rc2, r2_recv, 5, act)

    def link_sends(act):
        for k, d, mine in own_level[:5]:

            @pl.when(mine & (lax.rem(s - d, 4 * d) == 2 * d))
            def _():
                act(to(sx, xu.at[half_rows], s_send.at[7], rx_recv.at[1], s - d, j))

            @pl.when(mine & (s + d < 64) & (lax.rem(s + d, 4 * d) == 2 * d))
            def _():
                act(to(sx, xl.at[half_rows], s_send.at[7], rx_recv.at[0], s + d, j))

    lead_sends(lambda c: c.start())
    finish_rows(v2, ycat, f2b, [0, N])

    @pl.when(s > 0)
    def _():
        pl2[0:Q, :] = nt(v2[own_rows, :], v2[0:N, :])
        pu2[0:Q, :] = nt(v2[pl.ds(own_at + N, Q), :], v2[N : 2 * N, :])
        back = nt(v2[2 * N : 2 * N + 8, :], v2[0 : 2 * N, :])
        pl2[Q : Q + 8, :] = back[:, 0:N]
        pu2[Q : Q + 8, :] = back[:, N : 2 * N]

    rest_sends(lambda c: c.start())

    @pl.when(to_lower)
    def _():
        sx[...] = -nt(v2[pl.ds(half_at + N, H), :], v2[0:N, :])

    @pl.when(jnp.logical_not(to_lower) & (s > 0))
    def _():
        sx[...] = -nt(v2[pl.ds(half_at, H), :], v2[N : 2 * N, :])

    link_sends(lambda c: c.start())

    @pl.when(s > 0)
    def _():
        lo, hi = means(v2, f1b, f2b, zb)
        gb[:, 0:H] = lo
        gb[:, H:N] = hi

    def early_means():
        lo, hi = means(v1, f1a, f2a, za)
        ga[:, 0:H] = lo
        ga[:, H:N] = hi

    @pl.when(s > 0)
    def _():
        early_means()

    for k, d, mine in own_level:

        @pl.when(mine)
        def _():
            to(xown, xin.at[0], x_send.at[0], x_recv.at[0], s, j).wait_recv()

        @pl.when(mine & (s + d < 64))
        def _():
            to(xown, xin.at[1], x_send.at[0], x_recv.at[1], s, j).wait_recv()

        @pl.when(mine & (s + d >= 64))
        def _():
            xin[1] = jnp.zeros((8, N), F32)

    @pl.when(s == 0)
    def _():
        lo, hi = means(v2[2 * N : 2 * N + 8, :], f1b, f2b, zb)
        xown[:, 0:H] = lo
        xown[:, H:N] = hi

    @pl.when(s > 0)
    def _():
        xown[...] = gb[2 * N : 2 * N + 8, :] - (
            nn(xin[0], gb[0:N, :]) + nn(xin[1], gb[N : 2 * N, :])
        )

    def spread(act):
        for k in reversed(range(6)):
            d = 2**k

            @pl.when(divides(2 * d))
            def _():
                act(to(xown, xin.at[0], x_send.at[2 * k], x_recv.at[0], s + d, j))

            @pl.when(divides(2 * d) & (s > 0))
            def _():
                act(to(xown, xin.at[1], x_send.at[2 * k + 1], x_recv.at[1], s - d, j))

        @pl.when(jnp.logical_not(even))
        def _():
            act(to(xown, xin.at[2], x_send.at[12], x_recv.at[2], s - 1, j))

    spread(lambda c: c.start())

    @pl.when(s == 0)
    def _():
        early_means()

    part = ga[2 * N : 2 * N + 8, :] - nn(xown[...], ga[0:N, :])

    @pl.when(even)
    def _():
        to(xown, xin.at[2], x_send.at[12], x_recv.at[2], s, j).wait_recv()

    @pl.when(jnp.logical_not(even))
    def _():
        xin[2] = xin[1]

    later = part - nn(xin[2], ga[N : 2 * N, :])
    both = jnp.concatenate([xown[0:1, :], later[0:1, :]], axis=0)
    for i in range(8):

        @pl.when(j == i)
        def _():
            out[...] = both[:, 32 * i : 32 * i + 32]

    gather(3, lambda c: c.wait_send())
    for a in (1, 2, 4):
        direct(a, lambda c: c.wait_send())
    for a in (1, 2):
        hand_on(a, lambda c: c.wait_send())

    up0_sends(lambda c: c.wait_send())
    up0_link(lambda c: c.wait_send())
    up0_rest(lambda c: c.wait_send())

    hand_rest().wait_send()

    @pl.when(s > 0)
    def _():
        hand_xl().wait_send()

    @pl.when(even & (s > 0))
    def _():
        hand_xu().wait_send()

    lead_sends(lambda c: c.wait_send())
    link_sends(lambda c: c.wait_send())
    rest_sends(lambda c: c.wait_send())
    spread(lambda c: c.wait_send())


def body(diagonal, coupling, info):
    offset = lax.axis_index("state") * 32
    placed = lax.dynamic_update_slice(jnp.zeros((8, N), F32), info, (0, offset))
    vmem = pltpu.VMEM
    dma = pltpu.SemaphoreType.DMA
    square = vmem((N, N), F32)
    half = vmem((H, H), F32)
    tall = vmem((2 * N + 8, N), F32)
    slab = vmem((Q + 8, N), F32)
    wide = vmem((H, N), F32)
    return pl.pallas_call(
        kernel,
        out_shape=jax.ShapeDtypeStruct((2, 32), F32),
        in_specs=[pl.BlockSpec(memory_space=pltpu.HBM)] * 3,
        out_specs=pl.BlockSpec(memory_space=vmem),
        scratch_shapes=[
            square, square, square, vmem((64, N), F32), square, square, square, tall, vmem((2 * N + 8, H), F32), tall, tall,
            half, half, half, half, half, half, tall, tall,
            vmem((8, N), F32), vmem((13, H, H), F32), vmem((13, Q + 8, N), F32), vmem((Q, N), F32),
            half, slab, wide, half, slab, half, slab, wide,
            vmem((3, 8, N), F32), vmem((8, N), F32),
            dma((5, 8)), dma((5, 8)), dma((3,)), dma((3,)),
            dma((13,)), dma((13,)), dma((2,)), dma((8,)), dma((13,)), dma((3,)), dma((5,)),
        ],
        compiler_params=pltpu.CompilerParams(
            collective_id=0, has_side_effects=True, vmem_limit_bytes=32 * 1024 * 1024
        ),
    )(diagonal, coupling, placed)


def solution(mesh):
    placed = (P("tm", "state", None), P("tm", "state", None), P("tm", "state"))
    return jax.shard_map(
        body, mesh=mesh, in_specs=placed, out_specs=P("tm", "state"), check_vma=False
    )
```

```python
import jax
import jax.numpy as jnp
from jax import lax
from jax.experimental import pallas as pl
from jax.experimental.pallas import tpu as pltpu
from jax.sharding import PartitionSpec as P

N = 256
H = 128
Q = 64
F32 = jnp.float32
MESH = pl.DeviceIdType.MESH
EXACT = lax.Precision.HIGHEST


def nt(a, b):
    return lax.dot_general(
        a, b, (((1,), (1,)), ((), ())), precision=EXACT, preferred_element_type=F32
    )


def nn(a, b):
    return jnp.dot(a, b, precision=EXACT, preferred_element_type=F32)


def row_of(x, k):
    return jnp.broadcast_to(x[k : k + 1, :], x.shape)


def lane_of(x, l):
    return jnp.take_along_axis(x, jnp.full((8, H), l, jnp.int32), axis=1)


def sum8(t):
    return ((t[0] + t[1]) + (t[2] + t[3])) + ((t[4] + t[5]) + (t[6] + t[7]))


def pivot_block(w, b, sub, lane):
    at = 8 * b
    c = [lane_of(w[b], at + j) for j in range(8)]
    inside = (lane >= at) & (lane < at + 8)
    r = jnp.where(inside, (lane - at == sub).astype(F32), w[b])
    t = r
    pivots = jnp.ones((8, H), F32)
    inverses = []
    for k in range(0, 8, 2):
        first, second = sub == k, sub == k + 1
        p, q, o = row_of(c[k], k), row_of(c[k + 1], k), row_of(c[k + 1], k + 1)
        det = 1.0 / (p * o - q * q)
        m0 = jnp.where(first | second, 0.0, c[k])
        m1 = jnp.where(first | second, 0.0, c[k + 1])
        f0 = (m0 * o - m1 * q) * det
        f1 = (m1 * p - m0 * q) * det
        inverses.append((o * det, -q * det, p * det))
        ratio = q * (1.0 / p)
        r0, r1 = row_of(r, k), row_of(r, k + 1)
        t = jnp.where(first, r0, jnp.where(second, r1 - ratio * r0, t))
        pivots = jnp.where(first, p, jnp.where(second, o - ratio * q, pivots))
        for j in range(k + 2, 8):
            c[j] = c[j] - (f0 * row_of(c[j], k) + f1 * row_of(c[j], k + 1))
        r = r - (f0 * r0 + f1 * r1)
    if b < 15:
        rows = []
        for k in range(0, 8, 2):
            ia, ib, ic = inverses[k // 2]
            r0, r1 = row_of(r, k), row_of(r, k + 1)
            rows += [ia * r0 + ib * r1, ib * r0 + ic * r1]
        for i in range(b + 1, 16):
            cols = [lane_of(w[i], at + j) for j in range(8)]
            w[i] = jnp.where(inside, 0.0, w[i]) - sum8([cols[j] * rows[j] for j in range(8)])
    return jnp.where(lane < at + 8, t * lax.rsqrt(pivots), 0.0)


def factor_part(w, blocks):
    sub = lax.broadcasted_iota(jnp.int32, (8, H), 0)
    lane = lax.broadcasted_iota(jnp.int32, (8, H), 1)
    return [pivot_block(w, b, sub, lane) for b in blocks]


def groups(a):
    return [a[8 * r : 8 * r + 8, :] for r in range(16)]


def factor_start(block, begin, f1):
    w = groups(block[0:H, 0:H])
    out = factor_part(w, range(8))
    begin()
    out += factor_part(w, range(8, 16))
    f1[...] = jnp.concatenate(out, axis=0)


def factor_rest(block, steps, f1, f2, z):
    z[...] = nt(block[H:N, 0:H], f1[...])
    w = groups(block[H:N, H:N] - nt(z[...], z[...]))
    out = []
    for b in range(16):
        if b in steps:
            steps[b]()
        out += factor_part(w, [b])
    f2[...] = jnp.concatenate(out, axis=0)


def project(x, at, v, y, to, n, f1, z):
    v[to : to + n, 0:H] = nt(x[at : at + n, 0:H], f1[...])
    y[to : to + n, :] = x[at : at + n, H:N] - nt(v[to : to + n, 0:H], z[...])


def lead_start(v, to, at):
    to[...] = nt(v[at : at + H, 0:H], v[at : at + H, 0:H])


def lead_end(v, y, f2, to, at):
    top = nt(y[at : at + H, :], f2[...])
    v[at : at + H, H:N] = top
    to[...] = to[...] + nt(top, top)


def rest_rows(v, own, cols):
    return jnp.concatenate([v[own, cols], v[2 * N : 2 * N + 8, cols]], axis=0)


def rest_start(v, to, own, at):
    c = slice(0, H)
    to[...] = nt(rest_rows(v, own, c), v[at : at + N, c])


def rest_end(v, to, own, at):
    c = slice(H, N)
    to[...] = to[...] + nt(rest_rows(v, own, c), v[at : at + N, c])


def finish_rows(v, y, f2, at, n):
    v[at : at + n, H:N] = nt(y[at : at + n, :], f2[...])


def means(v, f1, f2, z):
    hi = nn(v[:, H:N], f2[...])
    lo = nn(v[:, 0:H] - nn(hi, z[...]), f1[...])
    return lo, hi


def kernel(
    diag, coup, info, out,
    d1, c0, c1, hin, d2, xl, xu, c1t, h1, ycat, v1, v2, f1a, f2a, za, f1b, f2b, zb, ga, gb,
    own_h, rc1, rc2, dsib, pu01, pu02, sx0, pl1, pl2, pu1, pu2, sx, xin, xown,
    g1_send, g1_recv, sib_send, sib_recv, r1_recv, r2_recv, rx_recv, s_send, x_send, x_recv, own_sem,
):
    s = lax.axis_index("tm")
    j = lax.axis_index("state")
    core = lax.rem(j, 2)
    sibling = j + 1 - 2 * core
    rows = pl.ds(pl.multiple_of(j * 32, 32), 32)
    own_rows = pl.ds(pl.multiple_of(H + core * Q, Q), Q)
    other_rows = pl.ds(pl.multiple_of(H + Q - core * Q, Q), Q)

    even = lax.rem(s, 2) == 0

    level, dist = jnp.int32(6), jnp.int32(64)
    to_lower, to_upper = jnp.bool_(False), jnp.bool_(False)
    for k in range(6):
        d = 2**k
        mine = lax.rem(s, 2 * d) == d
        level, dist = jnp.where(mine, k, level), jnp.where(mine, d, dist)
        if k < 5:
            to_lower = to_lower | (mine & (lax.rem(s - d, 4 * d) == 2 * d))
            to_upper = to_upper | (mine & (s + d < 64) & (lax.rem(s + d, 4 * d) == 2 * d))
    inner = s > 0
    upper = s + dist < 64

    barrier = pltpu.get_barrier_semaphore()
    for r in range(1, 8):
        pl.semaphore_signal(
            barrier, inc=1, device_id=(s, lax.rem(j + r, 8)), device_id_type=MESH
        )

    def greet(k, carry):
        d, count = carry
        up = s + d < 64

        @pl.when(inner)
        def _():
            pl.semaphore_signal(barrier, inc=1, device_id=(s - d, j), device_id_type=MESH)

        @pl.when(up)
        def _():
            pl.semaphore_signal(barrier, inc=1, device_id=(s + d, j), device_id_type=MESH)

        return 2 * d, count + inner.astype(jnp.int32) + up.astype(jnp.int32)

    _, count = lax.fori_loop(0, level + 1, greet, (jnp.int32(1), jnp.int32(7)))

    first = [
        (diag.at[1], d1.at[rows]),
        (coup.at[0], c0.at[rows]),
        (coup.at[1], c1.at[rows]),
        (info, hin.at[pl.ds(pl.multiple_of(j * 8, 8), 8)]),
        (diag.at[0], d2.at[rows]),
    ]
    local = [
        pltpu.make_async_copy(src, dst, own_sem.at[a]) for a, (src, dst) in enumerate(first)
    ]
    for c in local:
        c.start()

    @pl.when(s == 0)
    def _():
        xl[...] = jnp.zeros((N, N), F32)
        xu[...] = jnp.zeros((N, N), F32)

    pl.semaphore_wait(barrier, count)

    def to(src, dst, send, recv, tm, state):
        return pltpu.make_async_remote_copy(
            src_ref=src, dst_ref=dst, send_sem=send, recv_sem=recv,
            device_id=(tm, state), device_id_type=MESH,
        )

    def peer(src, dst, sends, recvs, a, r):
        return to(src, dst, sends.at[a, r], recvs.at[a, r], s, lax.rem(j + r, 8))

    def gather(a, act):
        src, dst = first[a]
        for r in range(1, 8):
            act(peer(src, dst, g1_send, g1_recv, a, r))

    def direct(a, act):
        src, dst = first[a]
        for r in (2, 4, 6):
            act(peer(src, dst, g1_send, g1_recv, a, r))
        act(to(src, dst, g1_send.at[a, 1], g1_recv.at[a, 1], s, sibling))

    def hand_on(a, act):
        whole = (None, c0, c1, None, d2)[a]
        for r in (2, 4, 6):
            at = pl.ds(pl.multiple_of(lax.rem(j + 8 - r, 8) * 32, 32), 32)
            piece = whole.at[at]
            act(to(piece, piece, g1_send.at[a, r + 1], g1_recv.at[a, r + 1], s, sibling))

    def direct_arrived(a):
        src, dst = first[a]
        for r in (2, 4, 6):
            peer(src, dst, g1_send, g1_recv, a, r).wait_recv()

    def arrived(a):
        src, dst = first[a]
        local[a].wait()
        to(src, dst, g1_send.at[a, 1], g1_recv.at[a, 1], s, sibling).wait_recv()
        hand_on(a, lambda c: c.wait_recv())

    gather(0, lambda c: c.start())
    gather(0, lambda c: c.wait_send())
    for a in (1, 2, 4):
        direct(a, lambda c: c.start())
    gather(3, lambda c: c.start())

    local[0].wait()
    gather(0, lambda c: c.wait_recv())
    factor_start(d1, lambda: None, f1a)

    def pass_on0():
        for a in (1, 2):
            direct_arrived(a)
            hand_on(a, lambda c: c.start())

    def fill0():
        direct_arrived(4)
        hand_on(4, lambda c: c.start())
        arrived(1)
        arrived(2)
        local[3].wait()
        gather(3, lambda c: c.wait_recv())
        info_all = sum8([hin[8 * i : 8 * i + 8, :] for i in range(8)])
        own_h[...] = row_of(info_all, 0)
        h1[...] = row_of(info_all, 1)
        c1t[...] = jnp.where(s == 63, 0.0, c1[...].T)
        project(c1t, 0, v1, ycat, N, H, f1a, za)
        lead_start(v1, pu01, N)
        project(c1t, H, v1, ycat, N + H, H, f1a, za)
        project(h1, 0, v1, ycat, 2 * N, 8, f1a, za)
        rest_start(v1, pu02, up_rows, N)
        project(c0, 0, v1, ycat, 0, N, f1a, za)

    up_rows = pl.ds(pl.multiple_of(N + H + core * Q, Q), Q)
    factor_rest(d1, {2: pass_on0, 12: fill0}, f1a, f2a, za)
    lead_end(v1, ycat, f2a, pu01, N)

    up0 = s < 63

    def up0_sends(act):
        @pl.when(up0)
        def _():
            act(to(pu01, rc1.at[0], s_send.at[0], r1_recv.at[0], s + 1, j))

    def up0_rest(act):
        @pl.when(up0)
        def _():
            act(to(pu02, rc2.at[0], s_send.at[1], r2_recv.at[0], s + 1, j))

    def part_rows(part):
        return pl.ds(pl.multiple_of(part * H + core * Q, Q), Q)

    def part_of(v, part, base):
        return v[pl.ds(pl.multiple_of(base + part * H + core * Q, Q), Q), :]

    def up0_link(act):
        @pl.when(even)
        def _():
            for part in range(2):
                act(to(sx0.at[part], xl.at[part_rows(part)], s_send.at[2 + part], rx_recv.at[0, part], s + 1, j))

    up0_sends(lambda c: c.start())
    finish_rows(v1, ycat, f2a, N + H, H)
    finish_rows(v1, ycat, f2a, 2 * N, 8)
    rest_end(v1, pu02, up_rows, N)
    up0_rest(lambda c: c.start())
    finish_rows(v1, ycat, f2a, 0, N)
    for part in range(2):
        sx0[part] = -nt(part_of(v1, part, 0), v1[N : 2 * N, :])
    up0_link(lambda c: c.start())
    back = nt(v1[2 * N : 2 * N + 8, :], v1[0:N, :])
    own_h[...] = own_h[...] - back
    arrived(4)
    hand_on(4, lambda c: c.wait_send())
    d2[0:H, 0:H] = d2[0:H, 0:H] - nt(v1[0:H, :], v1[0:H, :])
    d2[own_rows, :] = d2[own_rows, :] - nt(v1[own_rows, :], v1[0:N, :])

    @pl.when(jnp.logical_not(even))
    def _():
        xu[...] = -nt(v1[N : 2 * N, :], v1[0:N, :])

    def take_lead(slot):
        to(pl1, rc1.at[slot], s_send.at[4], r1_recv.at[slot], s, j).wait_recv()
        d2[0:H, 0:H] = d2[0:H, 0:H] - rc1[slot]

    def take_rest(slot):
        to(pl2, rc2.at[slot], s_send.at[5], r2_recv.at[slot], s, j).wait_recv()
        d2[own_rows, :] = d2[own_rows, :] - rc2[slot, 0:Q, :]
        own_h[...] = own_h[...] - rc2[slot, Q : Q + 8, :]

    @pl.when(even & inner)
    def _():
        take_lead(0)
        take_rest(0)

    def early(k, carry):
        @pl.when(inner)
        def _():
            take_lead(1 + 2 * k)
            take_rest(1 + 2 * k)

        take_lead(2 + 2 * k)
        take_rest(2 + 2 * k)
        return carry

    lax.fori_loop(0, jnp.maximum(level - 1, 0), early, 0)

    left_slot = jnp.where(even, 2 * level - 1, 0)

    def take_last(take):
        @pl.when(inner)
        def _():
            take(left_slot)

        @pl.when(even)
        def _():
            take(2 * level)

    take_last(take_lead)

    def hand(ref_rows, dst, a):
        return to(ref_rows, dst, sib_send.at[a], sib_recv.at[a], s, sibling)

    def hand_rest():
        return hand(d2.at[own_rows], dsib, 0)

    def hand_link(x, part, a):
        return hand(x.at[part_rows(part)], x.at[part_rows(part)], 1 + 2 * a + part)

    def begin():
        take_last(take_rest)
        hand_rest().start()

    def pass_on(part):
        @pl.when(inner)
        def _():
            to(sx0.at[0], xl.at[part_rows(part)], s_send.at[2], rx_recv.at[0, part], s, j).wait_recv()
            hand_link(xl, part, 0).start()

        @pl.when(even & inner)
        def _():
            to(sx0.at[0], xu.at[part_rows(part)], s_send.at[2], rx_recv.at[1, part], s, j).wait_recv()
            hand_link(xu, part, 1).start()

    def handed(part, act):
        @pl.when(inner)
        def _():
            act(hand_link(xl, part, 0))

        @pl.when(even & inner)
        def _():
            act(hand_link(xu, part, 1))

    def fill_lead():
        handed(0, lambda c: c.wait_recv())
        for x, at, to_ in ((xl, 0, pl1), (xu, N, pu1)):
            project(x, 0, v2, ycat, at, H, f1b, zb)
            lead_start(v2, to_, at)

    def fill_rest():
        handed(1, lambda c: c.wait_recv())
        project(own_h, 0, v2, ycat, 2 * N, 8, f1b, zb)
        for x, at, to_, own in ((xl, 0, pl2, own_rows), (xu, N, pu2, up_rows)):
            project(x, H, v2, ycat, at + H, H, f1b, zb)
            rest_start(v2, to_, own, at)

    factor_start(d2, begin, f1b)
    hand_rest().wait_recv()
    d2[other_rows, :] = dsib[...]
    steps = {1: lambda: pass_on(0), 3: lambda: pass_on(1), 6: fill_lead, 12: fill_rest}
    factor_rest(d2, steps, f1b, f2b, zb)
    lead_end(v2, ycat, f2b, pl1, 0)
    lead_end(v2, ycat, f2b, pu1, N)

    lower_slot, upper_slot = 2 + 2 * level, 1 + 2 * level

    def lead_sends(act):
        @pl.when(inner)
        def _():
            act(to(pl1, rc1.at[lower_slot], s_send.at[4], r1_recv.at[lower_slot], s - dist, j))

        @pl.when(upper)
        def _():
            act(to(pu1, rc1.at[upper_slot], s_send.at[5], r1_recv.at[upper_slot], s + dist, j))

    def rest_sends(act):
        @pl.when(inner)
        def _():
            act(to(pl2, rc2.at[lower_slot], s_send.at[6], r2_recv.at[lower_slot], s - dist, j))

        @pl.when(upper)
        def _():
            act(to(pu2, rc2.at[upper_slot], s_send.at[7], r2_recv.at[upper_slot], s + dist, j))

    def link_send(part, act):
        at = part_rows(part)

        @pl.when(to_lower)
        def _():
            act(to(sx.at[part], xu.at[at], s_send.at[8 + part], rx_recv.at[1, part], s - dist, j))

        @pl.when(to_upper)
        def _():
            act(to(sx.at[part], xl.at[at], s_send.at[8 + part], rx_recv.at[0, part], s + dist, j))

    lead_sends(lambda c: c.start())
    for at in (H, N + H):
        finish_rows(v2, ycat, f2b, at, H)
    finish_rows(v2, ycat, f2b, 2 * N, 8)
    rest_end(v2, pl2, own_rows, 0)
    rest_end(v2, pu2, up_rows, N)
    rest_sends(lambda c: c.start())

    for part in range(2):

        @pl.when(to_lower)
        def _():
            sx[part] = -nt(part_of(v2, part, N), v2[0:N, :])

        @pl.when(to_upper)
        def _():
            sx[part] = -nt(part_of(v2, part, 0), v2[N : 2 * N, :])

        link_send(part, lambda c: c.start())

    @pl.when(inner)
    def _():
        lo, hi = means(v2, f1b, f2b, zb)
        gb[:, 0:H] = lo
        gb[:, H:N] = hi

    def early_means():
        lo, hi = means(v1, f1a, f2a, za)
        ga[:, 0:H] = lo
        ga[:, H:N] = hi

    @pl.when(s > 0)
    def _():
        early_means()

    @pl.when(inner)
    def _():
        to(xown, xin.at[0], x_send.at[0], x_recv.at[0], s, j).wait_recv()

    @pl.when(upper)
    def _():
        to(xown, xin.at[1], x_send.at[0], x_recv.at[1], s, j).wait_recv()

    @pl.when(jnp.logical_not(upper))
    def _():
        xin[1] = jnp.zeros((8, N), F32)

    @pl.when(s == 0)
    def _():
        lo, hi = means(v2[2 * N : 2 * N + 8, :], f1b, f2b, zb)
        xown[:, 0:H] = lo
        xown[:, H:N] = hi

    @pl.when(s > 0)
    def _():
        xown[...] = gb[2 * N : 2 * N + 8, :] - (
            nn(xin[0], gb[0:N, :]) + nn(xin[1], gb[N : 2 * N, :])
        )

    def spread(act):
        def step(i, d):
            k = level - 1 - i
            act(to(xown, xin.at[0], x_send.at[2 * k], x_recv.at[0], s + d, j))

            @pl.when(inner)
            def _():
                act(to(xown, xin.at[1], x_send.at[2 * k + 1], x_recv.at[1], s - d, j))

            return d // 2

        lax.fori_loop(0, level, step, dist // 2)

        @pl.when(jnp.logical_not(even))
        def _():
            act(to(xown, xin.at[2], x_send.at[12], x_recv.at[2], s - 1, j))

    spread(lambda c: c.start())

    @pl.when(s == 0)
    def _():
        early_means()

    part = ga[2 * N : 2 * N + 8, :] - nn(xown[...], ga[0:N, :])

    @pl.when(even)
    def _():
        to(xown, xin.at[2], x_send.at[12], x_recv.at[2], s, j).wait_recv()

    @pl.when(jnp.logical_not(even))
    def _():
        xin[2] = xin[1]

    later = part - nn(xin[2], ga[N : 2 * N, :])
    both = jnp.concatenate([xown[0:1, :], later[0:1, :]], axis=0)
    for i in range(8):

        @pl.when(j == i)
        def _():
            out[...] = both[:, 32 * i : 32 * i + 32]

    gather(3, lambda c: c.wait_send())
    for a in (1, 2, 4):
        direct(a, lambda c: c.wait_send())
    for a in (1, 2):
        hand_on(a, lambda c: c.wait_send())

    up0_sends(lambda c: c.wait_send())
    up0_link(lambda c: c.wait_send())
    up0_rest(lambda c: c.wait_send())

    hand_rest().wait_send()

    for part in range(2):
        handed(part, lambda c: c.wait_send())

    lead_sends(lambda c: c.wait_send())
    for part in range(2):
        link_send(part, lambda c: c.wait_send())
    rest_sends(lambda c: c.wait_send())
    spread(lambda c: c.wait_send())


def body(diagonal, coupling, info):
    offset = lax.axis_index("state") * 32
    placed = lax.dynamic_update_slice(jnp.zeros((8, N), F32), info, (0, offset))
    vmem = pltpu.VMEM
    dma = pltpu.SemaphoreType.DMA
    square = vmem((N, N), F32)
    half = vmem((H, H), F32)
    tall = vmem((2 * N + 8, N), F32)
    slab = vmem((Q + 8, N), F32)
    pair = vmem((2, Q, N), F32)
    return pl.pallas_call(
        kernel,
        out_shape=jax.ShapeDtypeStruct((2, 32), F32),
        in_specs=[pl.BlockSpec(memory_space=pltpu.HBM)] * 3,
        out_specs=pl.BlockSpec(memory_space=vmem),
        scratch_shapes=[
            square, square, square, vmem((64, N), F32), square, square, square, square, vmem((8, N), F32), vmem((2 * N + 8, H), F32), tall, tall,
            half, half, half, half, half, half, tall, tall,
            vmem((8, N), F32), vmem((13, H, H), F32), vmem((13, Q + 8, N), F32), vmem((Q, N), F32),
            half, slab, pair, half, slab, half, slab, pair,
            vmem((3, 8, N), F32), vmem((8, N), F32),
            dma((5, 8)), dma((5, 8)), dma((5,)), dma((5,)),
            dma((13,)), dma((13,)), dma((2, 2)), dma((10,)), dma((13,)), dma((3,)), dma((5,)),
        ],
        compiler_params=pltpu.CompilerParams(
            collective_id=0, has_side_effects=True, vmem_limit_bytes=32 * 1024 * 1024
        ),
    )(diagonal, coupling, placed)


def solution(mesh):
    placed = (P("tm", "state", None), P("tm", "state", None), P("tm", "state"))
    return jax.shard_map(
        body, mesh=mesh, in_specs=placed, out_specs=P("tm", "state"), check_vma=False
    )
```

```python
import jax
import jax.numpy as jnp
from jax import lax
from jax.experimental import pallas as pl
from jax.experimental.pallas import tpu as pltpu
from jax.sharding import PartitionSpec as P

N = 256
H = 128
F32 = jnp.float32
MESH = pl.DeviceIdType.MESH
EXACT = lax.Precision.HIGHEST


def nt(a, b):
    return lax.dot_general(
        a, b, (((1,), (1,)), ((), ())), precision=EXACT, preferred_element_type=F32
    )


def nn(a, b):
    return jnp.dot(a, b, precision=EXACT, preferred_element_type=F32)


def row_of(x, k):
    return jnp.broadcast_to(x[k : k + 1, :], x.shape)


def lane_of(x, l):
    return jnp.take_along_axis(x, jnp.full((8, H), l, jnp.int32), axis=1)


def sum8(t):
    return ((t[0] + t[1]) + (t[2] + t[3])) + ((t[4] + t[5]) + (t[6] + t[7]))


def pivot_block(w, b, sub, lane):
    at = 8 * b
    c = [lane_of(w[b], at + j) for j in range(8)]
    inside = (lane >= at) & (lane < at + 8)
    r = jnp.where(inside, (lane - at == sub).astype(F32), w[b])
    t = r
    pivots = jnp.ones((8, H), F32)
    inverses = []
    for k in range(0, 8, 2):
        first, second = sub == k, sub == k + 1
        p, q, o = row_of(c[k], k), row_of(c[k + 1], k), row_of(c[k + 1], k + 1)
        det = 1.0 / (p * o - q * q)
        m0 = jnp.where(first | second, 0.0, c[k])
        m1 = jnp.where(first | second, 0.0, c[k + 1])
        f0 = (m0 * o - m1 * q) * det
        f1 = (m1 * p - m0 * q) * det
        inverses.append((o * det, -q * det, p * det))
        ratio = q * (1.0 / p)
        r0, r1 = row_of(r, k), row_of(r, k + 1)
        t = jnp.where(first, r0, jnp.where(second, r1 - ratio * r0, t))
        pivots = jnp.where(first, p, jnp.where(second, o - ratio * q, pivots))
        for j in range(k + 2, 8):
            c[j] = c[j] - (f0 * row_of(c[j], k) + f1 * row_of(c[j], k + 1))
        r = r - (f0 * r0 + f1 * r1)
    if b < 15:
        rows = []
        for k in range(0, 8, 2):
            ia, ib, ic = inverses[k // 2]
            r0, r1 = row_of(r, k), row_of(r, k + 1)
            rows += [ia * r0 + ib * r1, ib * r0 + ic * r1]
        for i in range(b + 1, 16):
            cols = [lane_of(w[i], at + j) for j in range(8)]
            w[i] = jnp.where(inside, 0.0, w[i]) - sum8([cols[j] * rows[j] for j in range(8)])
    return jnp.where(lane < at + 8, t * lax.rsqrt(pivots), 0.0)


def factor_part(w, blocks):
    sub = lax.broadcasted_iota(jnp.int32, (8, H), 0)
    lane = lax.broadcasted_iota(jnp.int32, (8, H), 1)
    return [pivot_block(w, b, sub, lane) for b in blocks]


def groups(a):
    return [a[8 * r : 8 * r + 8, :] for r in range(16)]


def factor_start(block, f1):
    f1[...] = jnp.concatenate(factor_part(groups(block[0:H, 0:H]), range(16)), axis=0)


def factor_rest(block, steps, f1, f2, z):
    z[...] = nt(block[H:N, 0:H], f1[...])
    w = groups(block[H:N, H:N] - nt(z[...], z[...]))
    out = []
    for b in range(16):
        if b in steps:
            steps[b]()
        out += factor_part(w, [b])
    f2[...] = jnp.concatenate(out, axis=0)


def project(x, at, v, y, to, n, f1, z):
    v[to : to + n, 0:H] = nt(x[at : at + n, 0:H], f1[...])
    y[to : to + n, :] = x[at : at + n, H:N] - nt(v[to : to + n, 0:H], z[...])


def lead_start(v, to, at):
    to[...] = nt(v[at : at + H, 0:H], v[at : at + H, 0:H])


def lead_end(v, y, f2, to, at):
    top = nt(y[at : at + H, :], f2[...])
    v[at : at + H, H:N] = top
    to[...] = to[...] + nt(top, top)


def rest_products(v, to, at):
    to[0:H, :] = nt(v[at + H : at + N, :], v[at : at + N, :])
    to[H : H + 8, :] = nt(v[2 * N : 2 * N + 8, :], v[at : at + N, :])


def finish_rows(v, y, f2, at, n):
    v[at : at + n, H:N] = nt(y[at : at + n, :], f2[...])


def means(v, f1, f2, z):
    hi = nn(v[:, H:N], f2[...])
    lo = nn(v[:, 0:H] - nn(hi, z[...]), f1[...])
    return lo, hi


def kernel(
    diag, coup, info, out,
    d1, c0, c1, hin, d2, xl, xu, c1t, h1, ycat, v1, v2, f1a, f2a, za, f1b, f2b, zb, ga, gb,
    own_h, rc1, rc2, pu01, pu02, sx0, pl1, pl2, pu1, pu2, sx, xin, xown,
    g1_send, g1_recv, r1_recv, r2_recv, rx_recv, s_send, x_send, x_recv, own_sem,
):
    s = lax.axis_index("tm")
    j = lax.axis_index("state")
    core = lax.rem(j, 2)
    sibling = j + 1 - 2 * core
    rows = pl.ds(pl.multiple_of(j * 32, 32), 32)

    even = lax.rem(s, 2) == 0

    level, dist = jnp.int32(6), jnp.int32(64)
    to_lower, to_upper = jnp.bool_(False), jnp.bool_(False)
    for k in range(6):
        d = 2**k
        mine = lax.rem(s, 2 * d) == d
        level, dist = jnp.where(mine, k, level), jnp.where(mine, d, dist)
        if k < 5:
            to_lower = to_lower | (mine & (lax.rem(s - d, 4 * d) == 2 * d))
            to_upper = to_upper | (mine & (s + d < 64) & (lax.rem(s + d, 4 * d) == 2 * d))
    inner = s > 0
    upper = s + dist < 64

    barrier = pltpu.get_barrier_semaphore()
    for r in range(1, 8):
        pl.semaphore_signal(
            barrier, inc=1, device_id=(s, lax.rem(j + r, 8)), device_id_type=MESH
        )

    def greet(k, carry):
        d, count = carry
        up = s + d < 64

        @pl.when(inner)
        def _():
            pl.semaphore_signal(barrier, inc=1, device_id=(s - d, j), device_id_type=MESH)

        @pl.when(up)
        def _():
            pl.semaphore_signal(barrier, inc=1, device_id=(s + d, j), device_id_type=MESH)

        return 2 * d, count + inner.astype(jnp.int32) + up.astype(jnp.int32)

    _, count = lax.fori_loop(0, level + 1, greet, (jnp.int32(1), jnp.int32(7)))

    first = [
        (diag.at[1, :, 0:H], d1.at[rows, 0:H]),
        (coup.at[0], c0.at[rows]),
        (coup.at[1], c1.at[rows]),
        (info, hin.at[pl.ds(pl.multiple_of(j * 8, 8), 8)]),
        (diag.at[0], d2.at[rows]),
        (diag.at[1, :, H:N], d1.at[rows, H:N]),
    ]
    local = [
        pltpu.make_async_copy(src, dst, own_sem.at[a]) for a, (src, dst) in enumerate(first)
    ]
    for c in local:
        c.start()

    @pl.when(s == 0)
    def _():
        xl[...] = jnp.zeros((N, N), F32)
        xu[...] = jnp.zeros((N, N), F32)

    pl.semaphore_wait(barrier, count)

    def to(src, dst, send, recv, tm, state):
        return pltpu.make_async_remote_copy(
            src_ref=src, dst_ref=dst, send_sem=send, recv_sem=recv,
            device_id=(tm, state), device_id_type=MESH,
        )

    def peer(src, dst, sends, recvs, a, r):
        return to(src, dst, sends.at[a, r], recvs.at[a, r], s, lax.rem(j + r, 8))

    def gather(a, act):
        src, dst = first[a]
        for r in range(1, 8):
            act(peer(src, dst, g1_send, g1_recv, a, r))

    def direct(a, act):
        src, dst = first[a]
        for r in (2, 4, 6):
            act(peer(src, dst, g1_send, g1_recv, a, r))
        act(to(src, dst, g1_send.at[a, 1], g1_recv.at[a, 1], s, sibling))

    def hand_on(a, act):
        whole = (None, c0, c1, None, d2)[a]
        for r in (2, 4, 6):
            at = pl.ds(pl.multiple_of(lax.rem(j + 8 - r, 8) * 32, 32), 32)
            piece = whole.at[at]
            act(to(piece, piece, g1_send.at[a, r + 1], g1_recv.at[a, r + 1], s, sibling))

    def direct_arrived(a):
        src, dst = first[a]
        for r in (2, 4, 6):
            peer(src, dst, g1_send, g1_recv, a, r).wait_recv()

    def arrived(a):
        src, dst = first[a]
        local[a].wait()
        to(src, dst, g1_send.at[a, 1], g1_recv.at[a, 1], s, sibling).wait_recv()
        hand_on(a, lambda c: c.wait_recv())

    gather(0, lambda c: c.start())
    gather(5, lambda c: c.start())
    gather(0, lambda c: c.wait_send())
    gather(5, lambda c: c.wait_send())
    for a in (2, 1, 4):
        direct(a, lambda c: c.start())
    gather(3, lambda c: c.start())

    def gathered(a):
        local[a].wait()
        gather(a, lambda c: c.wait_recv())

    gathered(0)
    factor_start(d1, f1a)
    gathered(5)

    for a in (2, 1):
        direct_arrived(a)
        hand_on(a, lambda c: c.start())

    def fill0():
        arrived(2)
        arrived(1)
        gathered(3)
        info_all = sum8([hin[8 * i : 8 * i + 8, :] for i in range(8)])
        own_h[...] = row_of(info_all, 0)
        h1[...] = row_of(info_all, 1)
        c1t[...] = jnp.where(s == 63, 0.0, c1[...].T)
        project(c1t, 0, v1, ycat, N, H, f1a, za)
        lead_start(v1, pu01, N)
        project(c1t, H, v1, ycat, N + H, H, f1a, za)
        project(h1, 0, v1, ycat, 2 * N, 8, f1a, za)
        project(c0, 0, v1, ycat, 0, N, f1a, za)

    factor_rest(d1, {12: fill0}, f1a, f2a, za)
    lead_end(v1, ycat, f2a, pu01, N)

    up0 = s < 63

    def up0_sends(act):
        @pl.when(up0)
        def _():
            act(to(pu01, rc1.at[0], s_send.at[0], r1_recv.at[0], s + 1, j))

    def up0_rest(act):
        @pl.when(up0)
        def _():
            act(to(pu02, rc2.at[0], s_send.at[1], r2_recv.at[0], s + 1, j))

    def part_rows(part):
        return pl.ds(part * H, H)

    def up0_link(act):
        @pl.when(even)
        def _():
            for part in range(2):
                act(to(sx0.at[part], xl.at[part_rows(part)], s_send.at[2 + part], rx_recv.at[0, part], s + 1, j))

    up0_sends(lambda c: c.start())
    finish_rows(v1, ycat, f2a, N + H, H)
    finish_rows(v1, ycat, f2a, 2 * N, 8)
    rest_products(v1, pu02, N)
    up0_rest(lambda c: c.start())
    finish_rows(v1, ycat, f2a, 0, N)
    for part in range(2):
        sx0[part] = -nt(v1[part * H : part * H + H, :], v1[N : 2 * N, :])
    up0_link(lambda c: c.start())
    direct_arrived(4)
    hand_on(4, lambda c: c.start())
    back = nt(v1[2 * N : 2 * N + 8, :], v1[0:N, :])
    own_h[...] = own_h[...] - back
    arrived(4)
    hand_on(4, lambda c: c.wait_send())
    d2[0:H, 0:H] = d2[0:H, 0:H] - nt(v1[0:H, :], v1[0:H, :])
    d2[H:N, :] = d2[H:N, :] - nt(v1[H:N, :], v1[0:N, :])

    @pl.when(jnp.logical_not(even))
    def _():
        xu[...] = -nt(v1[N : 2 * N, :], v1[0:N, :])

    def take_lead(slot):
        to(pl1, rc1.at[slot], s_send.at[4], r1_recv.at[slot], s, j).wait_recv()
        d2[0:H, 0:H] = d2[0:H, 0:H] - rc1[slot]

    def take_rest(slot):
        to(pl2, rc2.at[slot], s_send.at[5], r2_recv.at[slot], s, j).wait_recv()
        d2[H:N, :] = d2[H:N, :] - rc2[slot, 0:H, :]
        own_h[...] = own_h[...] - rc2[slot, H : H + 8, :]

    @pl.when(even & inner)
    def _():
        take_lead(0)
        take_rest(0)

    def early(k, carry):
        @pl.when(inner)
        def _():
            take_lead(1 + 2 * k)
            take_rest(1 + 2 * k)

        take_lead(2 + 2 * k)
        take_rest(2 + 2 * k)
        return carry

    lax.fori_loop(0, jnp.maximum(level - 1, 0), early, 0)

    left_slot = jnp.where(even, 2 * level - 1, 0)

    def take_last(take):
        @pl.when(inner)
        def _():
            take(left_slot)

        @pl.when(even)
        def _():
            take(2 * level)

    take_last(take_lead)

    def take_link(part):
        @pl.when(inner)
        def _():
            to(sx0.at[0], xl.at[part_rows(part)], s_send.at[2], rx_recv.at[0, part], s, j).wait_recv()

        @pl.when(even & inner)
        def _():
            to(sx0.at[0], xu.at[part_rows(part)], s_send.at[2], rx_recv.at[1, part], s, j).wait_recv()

    factor_start(d2, f1b)
    take_last(take_rest)
    take_link(0)

    def fill():
        project(own_h, 0, v2, ycat, 2 * N, 8, f1b, zb)
        for x, at, to_ in ((xl, 0, pl1), (xu, N, pu1)):
            project(x, 0, v2, ycat, at, H, f1b, zb)
            lead_start(v2, to_, at)

    factor_rest(d2, {6: fill}, f1b, f2b, zb)
    lead_end(v2, ycat, f2b, pl1, 0)
    lead_end(v2, ycat, f2b, pu1, N)

    lower_slot, upper_slot = 2 + 2 * level, 1 + 2 * level

    def lead_sends(act):
        @pl.when(inner)
        def _():
            act(to(pl1, rc1.at[lower_slot], s_send.at[4], r1_recv.at[lower_slot], s - dist, j))

        @pl.when(upper)
        def _():
            act(to(pu1, rc1.at[upper_slot], s_send.at[5], r1_recv.at[upper_slot], s + dist, j))

    def rest_sends(act):
        @pl.when(inner)
        def _():
            act(to(pl2, rc2.at[lower_slot], s_send.at[6], r2_recv.at[lower_slot], s - dist, j))

        @pl.when(upper)
        def _():
            act(to(pu2, rc2.at[upper_slot], s_send.at[7], r2_recv.at[upper_slot], s + dist, j))

    def link_send(part, act):
        at = part_rows(part)

        @pl.when(to_lower)
        def _():
            act(to(sx.at[part], xu.at[at], s_send.at[8 + part], rx_recv.at[1, part], s - dist, j))

        @pl.when(to_upper)
        def _():
            act(to(sx.at[part], xl.at[at], s_send.at[8 + part], rx_recv.at[0, part], s + dist, j))

    lead_sends(lambda c: c.start())
    take_link(1)
    for x, at in ((xl, H), (xu, N + H)):
        project(x, H, v2, ycat, at, H, f1b, zb)
        finish_rows(v2, ycat, f2b, at, H)
    finish_rows(v2, ycat, f2b, 2 * N, 8)
    rest_products(v2, pl2, 0)
    rest_products(v2, pu2, N)
    rest_sends(lambda c: c.start())

    for part in range(2):

        @pl.when(to_lower)
        def _():
            sx[part] = -nt(v2[N + part * H : N + part * H + H, :], v2[0:N, :])

        @pl.when(to_upper)
        def _():
            sx[part] = -nt(v2[part * H : part * H + H, :], v2[N : 2 * N, :])

        link_send(part, lambda c: c.start())

    @pl.when(inner)
    def _():
        lo, hi = means(v2, f1b, f2b, zb)
        gb[:, 0:H] = lo
        gb[:, H:N] = hi

    def early_means():
        lo, hi = means(v1, f1a, f2a, za)
        ga[:, 0:H] = lo
        ga[:, H:N] = hi

    @pl.when(s > 0)
    def _():
        early_means()

    @pl.when(inner)
    def _():
        to(xown, xin.at[0], x_send.at[0], x_recv.at[0], s, j).wait_recv()

    @pl.when(upper)
    def _():
        to(xown, xin.at[1], x_send.at[0], x_recv.at[1], s, j).wait_recv()

    @pl.when(jnp.logical_not(upper))
    def _():
        xin[1] = jnp.zeros((8, N), F32)

    @pl.when(s == 0)
    def _():
        lo, hi = means(v2[2 * N : 2 * N + 8, :], f1b, f2b, zb)
        xown[:, 0:H] = lo
        xown[:, H:N] = hi

    @pl.when(s > 0)
    def _():
        xown[...] = gb[2 * N : 2 * N + 8, :] - (
            nn(xin[0], gb[0:N, :]) + nn(xin[1], gb[N : 2 * N, :])
        )

    def spread(act):
        def step(i, d):
            k = level - 1 - i
            act(to(xown, xin.at[0], x_send.at[2 * k], x_recv.at[0], s + d, j))

            @pl.when(inner)
            def _():
                act(to(xown, xin.at[1], x_send.at[2 * k + 1], x_recv.at[1], s - d, j))

            return d // 2

        lax.fori_loop(0, level, step, dist // 2)

        @pl.when(jnp.logical_not(even))
        def _():
            act(to(xown, xin.at[2], x_send.at[12], x_recv.at[2], s - 1, j))

    spread(lambda c: c.start())

    @pl.when(s == 0)
    def _():
        early_means()

    part = ga[2 * N : 2 * N + 8, :] - nn(xown[...], ga[0:N, :])

    @pl.when(even)
    def _():
        to(xown, xin.at[2], x_send.at[12], x_recv.at[2], s, j).wait_recv()

    @pl.when(jnp.logical_not(even))
    def _():
        xin[2] = xin[1]

    later = part - nn(xin[2], ga[N : 2 * N, :])
    both = jnp.concatenate([xown[0:1, :], later[0:1, :]], axis=0)
    for i in range(8):

        @pl.when(j == i)
        def _():
            out[...] = both[:, 32 * i : 32 * i + 32]

    gather(3, lambda c: c.wait_send())
    for a in (1, 2, 4):
        direct(a, lambda c: c.wait_send())
    for a in (1, 2):
        hand_on(a, lambda c: c.wait_send())

    up0_sends(lambda c: c.wait_send())
    up0_link(lambda c: c.wait_send())
    up0_rest(lambda c: c.wait_send())


    lead_sends(lambda c: c.wait_send())
    for part in range(2):
        link_send(part, lambda c: c.wait_send())
    rest_sends(lambda c: c.wait_send())
    spread(lambda c: c.wait_send())


def body(diagonal, coupling, info):
    offset = lax.axis_index("state") * 32
    placed = lax.dynamic_update_slice(jnp.zeros((8, N), F32), info, (0, offset))
    vmem = pltpu.VMEM
    dma = pltpu.SemaphoreType.DMA
    square = vmem((N, N), F32)
    half = vmem((H, H), F32)
    tall = vmem((2 * N + 8, N), F32)
    slab = vmem((H + 8, N), F32)
    pair = vmem((2, H, N), F32)
    return pl.pallas_call(
        kernel,
        out_shape=jax.ShapeDtypeStruct((2, 32), F32),
        in_specs=[pl.BlockSpec(memory_space=pltpu.HBM)] * 3,
        out_specs=pl.BlockSpec(memory_space=vmem),
        scratch_shapes=[
            square, square, square, vmem((64, N), F32), square, square, square, square, vmem((8, N), F32), vmem((2 * N + 8, H), F32), tall, tall,
            half, half, half, half, half, half, tall, tall,
            vmem((8, N), F32), vmem((13, H, H), F32), vmem((13, H + 8, N), F32),
            half, slab, pair, half, slab, half, slab, pair,
            vmem((3, 8, N), F32), vmem((8, N), F32),
            dma((6, 8)), dma((6, 8)),
            dma((13,)), dma((13,)), dma((2, 2)), dma((10,)), dma((13,)), dma((3,)), dma((6,)),
        ],
        compiler_params=pltpu.CompilerParams(
            collective_id=0, has_side_effects=True, vmem_limit_bytes=32 * 1024 * 1024
        ),
    )(diagonal, coupling, placed)


def solution(mesh):
    placed = (P("tm", "state", None), P("tm", "state", None), P("tm", "state"))
    return jax.shard_map(
        body, mesh=mesh, in_specs=placed, out_specs=P("tm", "state"), check_vma=False
    )
```

```python
import jax
import jax.numpy as jnp
from jax import lax
from jax.experimental import pallas as pl
from jax.experimental.pallas import tpu as pltpu
from jax.sharding import PartitionSpec as P

N = 256
H = 128
F32 = jnp.float32
MESH = pl.DeviceIdType.MESH
EXACT = lax.Precision.HIGHEST


def nt(a, b):
    return lax.dot_general(
        a, b, (((1,), (1,)), ((), ())), precision=EXACT, preferred_element_type=F32
    )


def nn(a, b):
    return jnp.dot(a, b, precision=EXACT, preferred_element_type=F32)


def row_of(x, k):
    return jnp.broadcast_to(x[k : k + 1, :], x.shape)


def lane_of(x, l):
    return jnp.take_along_axis(x, jnp.full((8, H), l, jnp.int32), axis=1)


def sum8(t):
    return ((t[0] + t[1]) + (t[2] + t[3])) + ((t[4] + t[5]) + (t[6] + t[7]))


def pivot_block(w, b, sub, lane):
    at = 8 * b
    c = [lane_of(w[b], at + j) for j in range(8)]
    inside = (lane >= at) & (lane < at + 8)
    r = jnp.where(inside, (lane - at == sub).astype(F32), w[b])
    t = r
    pivots = jnp.ones((8, H), F32)
    inverses = []
    for k in range(0, 8, 2):
        first, second = sub == k, sub == k + 1
        p, q, o = row_of(c[k], k), row_of(c[k + 1], k), row_of(c[k + 1], k + 1)
        det = 1.0 / (p * o - q * q)
        m0 = jnp.where(first | second, 0.0, c[k])
        m1 = jnp.where(first | second, 0.0, c[k + 1])
        f0 = (m0 * o - m1 * q) * det
        f1 = (m1 * p - m0 * q) * det
        inverses.append((o * det, -q * det, p * det))
        ratio = q * (1.0 / p)
        r0, r1 = row_of(r, k), row_of(r, k + 1)
        t = jnp.where(first, r0, jnp.where(second, r1 - ratio * r0, t))
        pivots = jnp.where(first, p, jnp.where(second, o - ratio * q, pivots))
        for j in range(k + 2, 8):
            c[j] = c[j] - (f0 * row_of(c[j], k) + f1 * row_of(c[j], k + 1))
        r = r - (f0 * r0 + f1 * r1)
    if b < 15:
        rows = []
        for k in range(0, 8, 2):
            ia, ib, ic = inverses[k // 2]
            r0, r1 = row_of(r, k), row_of(r, k + 1)
            rows += [ia * r0 + ib * r1, ib * r0 + ic * r1]
        for i in range(b + 1, 16):
            cols = [lane_of(w[i], at + j) for j in range(8)]
            w[i] = jnp.where(inside, 0.0, w[i]) - sum8([cols[j] * rows[j] for j in range(8)])
    return jnp.where(lane < at + 8, t * lax.rsqrt(pivots), 0.0)


def factor_part(w, blocks):
    sub = lax.broadcasted_iota(jnp.int32, (8, H), 0)
    lane = lax.broadcasted_iota(jnp.int32, (8, H), 1)
    return [pivot_block(w, b, sub, lane) for b in blocks]


def groups(a):
    return [a[8 * r : 8 * r + 8, :] for r in range(16)]


def factor_start(block, f1):
    f1[...] = jnp.concatenate(factor_part(groups(block[0:H, 0:H]), range(16)), axis=0)


def factor_rest(block, steps, f1, f2, z):
    z[...] = nt(block[H:N, 0:H], f1[...])
    w = groups(block[H:N, H:N] - nt(z[...], z[...]))
    out = []
    for b in range(16):
        if b in steps:
            steps[b]()
        out += factor_part(w, [b])
    f2[...] = jnp.concatenate(out, axis=0)


def project(x, at, v, y, to, n, f1, z):
    v[to : to + n, 0:H] = nt(x[at : at + n, 0:H], f1[...])
    y[to : to + n, :] = x[at : at + n, H:N] - nt(v[to : to + n, 0:H], z[...])


def lead_start(v, to, at):
    to[...] = nt(v[at : at + H, 0:H], v[at : at + H, 0:H])


def lead_end(v, y, f2, to, at):
    top = nt(y[at : at + H, :], f2[...])
    v[at : at + H, H:N] = top
    to[...] = to[...] + nt(top, top)


def rest_products(v, to, at):
    to[0:H, :] = nt(v[at + H : at + N, :], v[at : at + N, :])
    to[H : H + 8, :] = nt(v[2 * N : 2 * N + 8, :], v[at : at + N, :])


def finish_rows(v, y, f2, at, n):
    v[at : at + n, H:N] = nt(y[at : at + n, :], f2[...])


def means(v, f1, f2, z):
    hi = nn(v[:, H:N], f2[...])
    lo = nn(v[:, 0:H] - nn(hi, z[...]), f1[...])
    return lo, hi


def kernel(
    diag, coup, info, out,
    d1, c0, c1, hin, d2, xl, xu, c1t, h1, ycat, v1, v2, f1a, f2a, za, f1b, f2b, zb, f1c, f2c, zc, hv, hy, xfirst, ga, gb,
    own_h, rc1, rc2, pu01, pu02, sx0, pl1, pl2, pu1, pu2, sx, xin, xown,
    g1_send, g1_recv, r1_recv, r2_recv, rx_recv, s_send, x_send, x_recv, own_sem,
):
    s = lax.axis_index("tm")
    j = lax.axis_index("state")
    core = lax.rem(j, 2)
    sibling = j + 1 - 2 * core
    rows = pl.ds(pl.multiple_of(j * 32, 32), 32)

    even = lax.rem(s, 2) == 0

    level, dist = jnp.int32(6), jnp.int32(64)
    to_lower, to_upper = jnp.bool_(False), jnp.bool_(False)
    for k in range(6):
        d = 2**k
        mine = lax.rem(s, 2 * d) == d
        level, dist = jnp.where(mine, k, level), jnp.where(mine, d, dist)
        if k < 5:
            to_lower = to_lower | (mine & (lax.rem(s - d, 4 * d) == 2 * d))
            to_upper = to_upper | (mine & (s + d < 64) & (lax.rem(s + d, 4 * d) == 2 * d))
    inner = s > 0
    upper = s + dist < 64

    barrier = pltpu.get_barrier_semaphore()
    for r in range(1, 8):
        pl.semaphore_signal(
            barrier, inc=1, device_id=(s, lax.rem(j + r, 8)), device_id_type=MESH
        )

    def greet(k, carry):
        d, count = carry
        up = s + d < 64

        @pl.when(inner)
        def _():
            pl.semaphore_signal(barrier, inc=1, device_id=(s - d, j), device_id_type=MESH)

        @pl.when(up)
        def _():
            pl.semaphore_signal(barrier, inc=1, device_id=(s + d, j), device_id_type=MESH)

        return 2 * d, count + inner.astype(jnp.int32) + up.astype(jnp.int32)

    _, count = lax.fori_loop(0, level + 1, greet, (jnp.int32(1), jnp.int32(7)))

    root = s == 32
    reads_first = (s == 1) | (s == 2) | (s == 4) | (s == 8)
    count = count + reads_first.astype(jnp.int32) + 4 * root.astype(jnp.int32)

    @pl.when(reads_first)
    def _():
        pl.semaphore_signal(barrier, inc=1, device_id=(32, j), device_id_type=MESH)

    @pl.when(root)
    def _():
        for k in range(4):
            pl.semaphore_signal(barrier, inc=1, device_id=(2**k, j), device_id_type=MESH)

    first = [
        (diag.at[1, :, 0:H], d1.at[rows, 0:H]),
        (coup.at[0], c0.at[rows]),
        (coup.at[1], c1.at[rows]),
        (info, hin.at[pl.ds(pl.multiple_of(j * 8, 8), 8)]),
        (diag.at[0], d2.at[rows]),
        (diag.at[1, :, H:N], d1.at[rows, H:N]),
    ]
    local = [
        pltpu.make_async_copy(src, dst, own_sem.at[a]) for a, (src, dst) in enumerate(first)
    ]
    for c in local:
        c.start()

    pl.semaphore_wait(barrier, count)

    def to(src, dst, send, recv, tm, state):
        return pltpu.make_async_remote_copy(
            src_ref=src, dst_ref=dst, send_sem=send, recv_sem=recv,
            device_id=(tm, state), device_id_type=MESH,
        )

    def peer(src, dst, sends, recvs, a, r):
        return to(src, dst, sends.at[a, r], recvs.at[a, r], s, lax.rem(j + r, 8))

    def gather(a, act):
        src, dst = first[a]
        for r in range(1, 8):
            act(peer(src, dst, g1_send, g1_recv, a, r))

    def direct(a, act):
        src, dst = first[a]
        for r in (2, 4, 6):
            act(peer(src, dst, g1_send, g1_recv, a, r))
        act(to(src, dst, g1_send.at[a, 1], g1_recv.at[a, 1], s, sibling))

    def hand_on(a, act):
        whole = (None, c0, c1, None, d2)[a]
        for r in (2, 4, 6):
            at = pl.ds(pl.multiple_of(lax.rem(j + 8 - r, 8) * 32, 32), 32)
            piece = whole.at[at]
            act(to(piece, piece, g1_send.at[a, r + 1], g1_recv.at[a, r + 1], s, sibling))

    def direct_arrived(a):
        src, dst = first[a]
        for r in (2, 4, 6):
            peer(src, dst, g1_send, g1_recv, a, r).wait_recv()

    def arrived(a):
        src, dst = first[a]
        local[a].wait()
        to(src, dst, g1_send.at[a, 1], g1_recv.at[a, 1], s, sibling).wait_recv()
        hand_on(a, lambda c: c.wait_recv())

    gather(0, lambda c: c.start())
    gather(5, lambda c: c.start())
    gather(0, lambda c: c.wait_send())
    gather(5, lambda c: c.wait_send())
    for a in (2, 1, 4):
        direct(a, lambda c: c.start())
    gather(3, lambda c: c.start())

    def gathered(a):
        local[a].wait()
        gather(a, lambda c: c.wait_recv())

    gathered(0)
    factor_start(d1, f1a)
    gathered(5)

    for a in (2, 1):
        direct_arrived(a)
        hand_on(a, lambda c: c.start())

    def fill0():
        arrived(2)
        arrived(1)
        gathered(3)
        info_all = sum8([hin[8 * i : 8 * i + 8, :] for i in range(8)])
        own_h[...] = row_of(info_all, 0)
        h1[...] = row_of(info_all, 1)
        c1t[...] = jnp.where(s == 63, 0.0, c1[...].T)
        project(c1t, 0, v1, ycat, N, H, f1a, za)
        lead_start(v1, pu01, N)
        project(c1t, H, v1, ycat, N + H, H, f1a, za)
        project(h1, 0, v1, ycat, 2 * N, 8, f1a, za)
        project(c0, 0, v1, ycat, 0, N, f1a, za)

    factor_rest(d1, {12: fill0}, f1a, f2a, za)
    lead_end(v1, ycat, f2a, pu01, N)

    up0 = s < 63

    def up0_sends(act):
        @pl.when(up0)
        def _():
            act(to(pu01, rc1.at[0], s_send.at[0], r1_recv.at[0], s + 1, j))

    def up0_rest(act):
        @pl.when(up0)
        def _():
            act(to(pu02, rc2.at[0], s_send.at[1], r2_recv.at[0], s + 1, j))

    def part_rows(part):
        return pl.ds(part * H, H)

    def up0_link(act):
        @pl.when(even)
        def _():
            for part in range(2):
                act(to(sx0.at[part], xl.at[part_rows(part)], s_send.at[2 + part], rx_recv.at[0, part], s + 1, j))

    up0_sends(lambda c: c.start())
    finish_rows(v1, ycat, f2a, N + H, H)
    finish_rows(v1, ycat, f2a, 2 * N, 8)
    rest_products(v1, pu02, N)
    up0_rest(lambda c: c.start())
    finish_rows(v1, ycat, f2a, 0, N)
    for part in range(2):
        sx0[part] = -nt(v1[part * H : part * H + H, :], v1[N : 2 * N, :])
    up0_link(lambda c: c.start())
    direct_arrived(4)
    hand_on(4, lambda c: c.start())
    back = nt(v1[2 * N : 2 * N + 8, :], v1[0:N, :])
    own_h[...] = own_h[...] - back
    arrived(4)
    hand_on(4, lambda c: c.wait_send())
    d2[0:H, 0:H] = d2[0:H, 0:H] - nt(v1[0:H, :], v1[0:H, :])
    d2[H:N, :] = d2[H:N, :] - nt(v1[H:N, :], v1[0:N, :])

    @pl.when(jnp.logical_not(even))
    def _():
        xu[...] = -nt(v1[N : 2 * N, :], v1[0:N, :])

    def take_lead(slot):
        to(pl1, rc1.at[slot], s_send.at[4], r1_recv.at[slot], s, j).wait_recv()
        d2[0:H, 0:H] = d2[0:H, 0:H] - rc1[slot]

    def take_rest(slot):
        to(pl2, rc2.at[slot], s_send.at[5], r2_recv.at[slot], s, j).wait_recv()
        d2[H:N, :] = d2[H:N, :] - rc2[slot, 0:H, :]
        own_h[...] = own_h[...] - rc2[slot, H : H + 8, :]

    @pl.when(even & inner)
    def _():
        take_lead(0)
        take_rest(0)

    def early(k, carry):
        @pl.when(inner)
        def _():
            take_lead(1 + 2 * k)
            take_rest(1 + 2 * k)

        take_lead(2 + 2 * k)
        take_rest(2 + 2 * k)
        return carry

    below = jnp.minimum(level, 5)
    lax.fori_loop(0, jnp.maximum(below - 1, 0), early, 0)

    left_slot = jnp.where(even, 2 * level - 1, 0)

    def take_last(take):
        @pl.when(inner)
        def _():
            take(left_slot)

        @pl.when(even)
        def _():
            take(2 * below)

    take_last(take_lead)

    def take_link(part):
        @pl.when(inner)
        def _():
            to(sx0.at[0], xl.at[part_rows(part)], s_send.at[2], rx_recv.at[0, part], s, j).wait_recv()

        @pl.when(even & inner)
        def _():
            to(sx0.at[0], xu.at[part_rows(part)], s_send.at[2], rx_recv.at[1, part], s, j).wait_recv()

    def first_lead():
        return to(pl1, rc1.at[12], s_send.at[4], r1_recv.at[12], 32, j)

    def first_rest():
        return to(pl2, rc2.at[12], s_send.at[6], r2_recv.at[12], 32, j)

    @pl.when(s == 0)
    def _():
        pl1[...] = d2[0:H, 0:H]
        first_lead().start()
        take_last(take_rest)
        pl2[0:H, :] = d2[H:N, :]
        pl2[H : H + 8, :] = own_h[...]
        first_rest().start()

    @pl.when(inner)
    def _():
        factor_start(d2, f1b)
        take_last(take_rest)
        take_link(0)

        def fill():
            project(own_h, 0, v2, ycat, 2 * N, 8, f1b, zb)
            for x, at, to_ in ((xl, 0, pl1), (xu, N, pu1)):
                project(x, 0, v2, ycat, at, H, f1b, zb)
                lead_start(v2, to_, at)

        factor_rest(d2, {6: fill}, f1b, f2b, zb)
        lead_end(v2, ycat, f2b, pl1, 0)
        lead_end(v2, ycat, f2b, pu1, N)

    sending = inner & jnp.logical_not(root)

    lower_slot, upper_slot = 2 + 2 * level, 1 + 2 * level

    def lead_sends(act):
        @pl.when(sending)
        def _():
            act(to(pl1, rc1.at[lower_slot], s_send.at[4], r1_recv.at[lower_slot], s - dist, j))

        @pl.when(upper)
        def _():
            act(to(pu1, rc1.at[upper_slot], s_send.at[5], r1_recv.at[upper_slot], s + dist, j))

    def rest_sends(act):
        @pl.when(sending)
        def _():
            act(to(pl2, rc2.at[lower_slot], s_send.at[6], r2_recv.at[lower_slot], s - dist, j))

        @pl.when(upper)
        def _():
            act(to(pu2, rc2.at[upper_slot], s_send.at[7], r2_recv.at[upper_slot], s + dist, j))

    def link_send(part, act):
        at = part_rows(part)

        @pl.when(to_lower)
        def _():
            act(to(sx.at[part], xu.at[at], s_send.at[8 + part], rx_recv.at[1, part], s - dist, j))

        @pl.when(to_upper)
        def _():
            act(to(sx.at[part], xl.at[at], s_send.at[8 + part], rx_recv.at[0, part], s + dist, j))

    lead_sends(lambda c: c.start())
    take_link(1)

    @pl.when(inner)
    def _():
        for x, at in ((xl, H), (xu, N + H)):
            project(x, H, v2, ycat, at, H, f1b, zb)
            finish_rows(v2, ycat, f2b, at, H)
        finish_rows(v2, ycat, f2b, 2 * N, 8)
        rest_products(v2, pl2, 0)
        rest_products(v2, pu2, N)

    rest_sends(lambda c: c.start())

    for part in range(2):

        @pl.when(to_lower)
        def _():
            sx[part] = -nt(v2[N + part * H : N + part * H + H, :], v2[0:N, :])

        @pl.when(to_upper)
        def _():
            sx[part] = -nt(v2[part * H : part * H + H, :], v2[N : 2 * N, :])

        link_send(part, lambda c: c.start())

    def own_means():
        lo, hi = means(v2, f1b, f2b, zb)
        gb[:, 0:H] = lo
        gb[:, H:N] = hi

    def early_means():
        lo, hi = means(v1, f1a, f2a, za)
        ga[:, 0:H] = lo
        ga[:, H:N] = hi

    def spread_first(act):
        for a, seg in enumerate((16, 8, 4, 2, 1, 0)):
            act(to(xfirst, xin.at[0], x_send.at[13 + a], x_recv.at[0], seg, j))

    @pl.when(root)
    def _():
        to(pl1, rc1.at[12], s_send.at[4], r1_recv.at[12], s, j).wait_recv()
        to(pl2, rc2.at[12], s_send.at[6], r2_recv.at[12], s, j).wait_recv()
        d1[0:H, 0:H] = rc1[12] - pl1[...]
        d1[H:N, :] = rc2[12, 0:H, :] - pl2[0:H, :]
        h1[...] = rc2[12, H : H + 8, :] - pl2[H : H + 8, :]
        factor_start(d1, f1c)

        def fill():
            project(h1, 0, hv, hy, 0, 8, f1c, zc)
            own_means()

        factor_rest(d1, {2: fill}, f1c, f2c, zc)
        finish_rows(hv, hy, f2c, 0, 8)
        lo, hi = means(hv, f1c, f2c, zc)
        xfirst[:, 0:H] = lo
        xfirst[:, H:N] = hi
        spread_first(lambda c: c.start())
        xown[...] = gb[2 * N : 2 * N + 8, :] - nn(xfirst[...], gb[0:N, :])

    @pl.when(jnp.logical_not(root))
    def _():
        @pl.when(inner)
        def _():
            own_means()

        early_means()
        to(xown, xin.at[0], x_send.at[0], x_recv.at[0], s, j).wait_recv()

    @pl.when(upper)
    def _():
        to(xown, xin.at[1], x_send.at[0], x_recv.at[1], s, j).wait_recv()

    @pl.when(jnp.logical_not(upper))
    def _():
        xin[1] = jnp.zeros((8, N), F32)

    @pl.when(s == 0)
    def _():
        xown[...] = xin[0]

    @pl.when(sending)
    def _():
        xown[...] = gb[2 * N : 2 * N + 8, :] - (
            nn(xin[0], gb[0:N, :]) + nn(xin[1], gb[N : 2 * N, :])
        )

    def spread(act):
        def step(i, d):
            k = level - 1 - i
            act(to(xown, xin.at[0], x_send.at[2 * k], x_recv.at[0], s + d, j))
            act(to(xown, xin.at[1], x_send.at[2 * k + 1], x_recv.at[1], s - d, j))
            return d // 2

        lax.fori_loop(0, jnp.where(inner, level, 0), step, dist // 2)

        @pl.when(jnp.logical_not(even))
        def _():
            act(to(xown, xin.at[2], x_send.at[12], x_recv.at[2], s - 1, j))

    spread(lambda c: c.start())

    @pl.when(root)
    def _():
        early_means()

    part = ga[2 * N : 2 * N + 8, :] - nn(xown[...], ga[0:N, :])

    @pl.when(even)
    def _():
        to(xown, xin.at[2], x_send.at[12], x_recv.at[2], s, j).wait_recv()

    @pl.when(jnp.logical_not(even))
    def _():
        xin[2] = xin[1]

    later = part - nn(xin[2], ga[N : 2 * N, :])
    both = jnp.concatenate([xown[0:1, :], later[0:1, :]], axis=0)
    for i in range(8):

        @pl.when(j == i)
        def _():
            out[...] = both[:, 32 * i : 32 * i + 32]

    gather(3, lambda c: c.wait_send())
    for a in (1, 2, 4):
        direct(a, lambda c: c.wait_send())
    for a in (1, 2):
        hand_on(a, lambda c: c.wait_send())

    up0_sends(lambda c: c.wait_send())
    up0_link(lambda c: c.wait_send())
    up0_rest(lambda c: c.wait_send())


    @pl.when(s == 0)
    def _():
        first_lead().wait_send()
        first_rest().wait_send()

    @pl.when(root)
    def _():
        spread_first(lambda c: c.wait_send())

    lead_sends(lambda c: c.wait_send())
    for part in range(2):
        link_send(part, lambda c: c.wait_send())
    rest_sends(lambda c: c.wait_send())
    spread(lambda c: c.wait_send())


def body(diagonal, coupling, info):
    offset = lax.axis_index("state") * 32
    placed = lax.dynamic_update_slice(jnp.zeros((8, N), F32), info, (0, offset))
    vmem = pltpu.VMEM
    dma = pltpu.SemaphoreType.DMA
    square = vmem((N, N), F32)
    half = vmem((H, H), F32)
    tall = vmem((2 * N + 8, N), F32)
    slab = vmem((H + 8, N), F32)
    pair = vmem((2, H, N), F32)
    return pl.pallas_call(
        kernel,
        out_shape=jax.ShapeDtypeStruct((2, 32), F32),
        in_specs=[pl.BlockSpec(memory_space=pltpu.HBM)] * 3,
        out_specs=pl.BlockSpec(memory_space=vmem),
        scratch_shapes=[
            square, square, square, vmem((64, N), F32), square, square, square, square, vmem((8, N), F32), vmem((2 * N + 8, H), F32), tall, tall,
            half, half, half, half, half, half, half, half, half,
            vmem((8, N), F32), vmem((8, H), F32), vmem((8, N), F32), tall, tall,
            vmem((8, N), F32), vmem((13, H, H), F32), vmem((13, H + 8, N), F32),
            half, slab, pair, half, slab, half, slab, pair,
            vmem((3, 8, N), F32), vmem((8, N), F32),
            dma((6, 8)), dma((6, 8)),
            dma((13,)), dma((13,)), dma((2, 2)), dma((10,)), dma((19,)), dma((3,)), dma((6,)),
        ],
        compiler_params=pltpu.CompilerParams(
            collective_id=0, has_side_effects=True, vmem_limit_bytes=32 * 1024 * 1024
        ),
    )(diagonal, coupling, placed)


def solution(mesh):
    placed = (P("tm", "state", None), P("tm", "state", None), P("tm", "state"))
    return jax.shard_map(
        body, mesh=mesh, in_specs=placed, out_specs=P("tm", "state"), check_vma=False
    )
```

```python
import jax
import jax.numpy as jnp
from jax import lax
from jax.experimental import pallas as pl
from jax.experimental.pallas import tpu as pltpu
from jax.sharding import PartitionSpec as P

N = 256
H = 128
F32 = jnp.float32
MESH = pl.DeviceIdType.MESH
EXACT = lax.Precision.HIGHEST


def nt(a, b):
    return lax.dot_general(
        a, b, (((1,), (1,)), ((), ())), precision=EXACT, preferred_element_type=F32
    )


def nn(a, b):
    return jnp.dot(a, b, precision=EXACT, preferred_element_type=F32)


def row_of(x, k):
    return jnp.broadcast_to(x[k : k + 1, :], x.shape)


def lane_of(x, l):
    return jnp.take_along_axis(x, jnp.full((8, H), l, jnp.int32), axis=1)


def sum8(t):
    return ((t[0] + t[1]) + (t[2] + t[3])) + ((t[4] + t[5]) + (t[6] + t[7]))


def pivot_block(w, b, sub, lane):
    at = 8 * b
    c = [lane_of(w[b], at + j) for j in range(8)]
    inside = (lane >= at) & (lane < at + 8)
    r = jnp.where(inside, (lane - at == sub).astype(F32), w[b])
    t = r
    pivots = jnp.ones((8, H), F32)
    inverses = []
    for k in range(0, 8, 2):
        first, second = sub == k, sub == k + 1
        p, q, o = row_of(c[k], k), row_of(c[k + 1], k), row_of(c[k + 1], k + 1)
        det = 1.0 / (p * o - q * q)
        m0 = jnp.where(first | second, 0.0, c[k])
        m1 = jnp.where(first | second, 0.0, c[k + 1])
        f0 = (m0 * o - m1 * q) * det
        f1 = (m1 * p - m0 * q) * det
        inverses.append((o * det, -q * det, p * det))
        ratio = q * (1.0 / p)
        r0, r1 = row_of(r, k), row_of(r, k + 1)
        t = jnp.where(first, r0, jnp.where(second, r1 - ratio * r0, t))
        pivots = jnp.where(first, p, jnp.where(second, o - ratio * q, pivots))
        for j in range(k + 2, 8):
            c[j] = c[j] - (f0 * row_of(c[j], k) + f1 * row_of(c[j], k + 1))
        r = r - (f0 * r0 + f1 * r1)
    if b < 15:
        rows = []
        for k in range(0, 8, 2):
            ia, ib, ic = inverses[k // 2]
            r0, r1 = row_of(r, k), row_of(r, k + 1)
            rows += [ia * r0 + ib * r1, ib * r0 + ic * r1]
        for i in range(b + 1, 16):
            cols = [lane_of(w[i], at + j) for j in range(8)]
            w[i] = jnp.where(inside, 0.0, w[i]) - sum8([cols[j] * rows[j] for j in range(8)])
    return jnp.where(lane < at + 8, t * lax.rsqrt(pivots), 0.0)


def factor_part(w, blocks):
    sub = lax.broadcasted_iota(jnp.int32, (8, H), 0)
    lane = lax.broadcasted_iota(jnp.int32, (8, H), 1)
    return [pivot_block(w, b, sub, lane) for b in blocks]


def groups(a):
    return [a[8 * r : 8 * r + 8, :] for r in range(16)]


def factor_start(block, f1):
    f1[...] = jnp.concatenate(factor_part(groups(block[0:H, 0:H]), range(16)), axis=0)


def factor_rest(block, steps, f1, f2, z):
    z[...] = nt(block[H:N, 0:H], f1[...])
    w = groups(block[H:N, H:N] - nt(z[...], z[...]))
    out = []
    for b in range(16):
        if b in steps:
            steps[b]()
        out += factor_part(w, [b])
    f2[...] = jnp.concatenate(out, axis=0)


def project(x, at, v, y, to, n, f1, z):
    v[to : to + n, 0:H] = nt(x[at : at + n, 0:H], f1[...])
    y[to : to + n, :] = x[at : at + n, H:N] - nt(v[to : to + n, 0:H], z[...])


def lead_start(v, to, at):
    to[...] = nt(v[at : at + H, 0:H], v[at : at + H, 0:H])


def lead_end(v, y, f2, to, at):
    top = nt(y[at : at + H, :], f2[...])
    v[at : at + H, H:N] = top
    to[...] = to[...] + nt(top, top)


def rest_products(v, to, at):
    to[0:H, :] = nt(v[at + H : at + N, :], v[at : at + N, :])
    to[H : H + 8, :] = nt(v[2 * N : 2 * N + 8, :], v[at : at + N, :])


def rest_rows(v, at, cols):
    return jnp.concatenate([v[at + H : at + N, cols], v[2 * N : 2 * N + 8, cols]], axis=0)


def rest_start(v, to, at):
    c = slice(0, H)
    to[...] = nt(rest_rows(v, at, c), v[at : at + N, c])


def rest_end(v, to, at):
    c = slice(H, N)
    to[...] = to[...] + nt(rest_rows(v, at, c), v[at : at + N, c])


def finish_rows(v, y, f2, at, n):
    v[at : at + n, H:N] = nt(y[at : at + n, :], f2[...])


def means(v, f1, f2, z):
    hi = nn(v[:, H:N], f2[...])
    lo = nn(v[:, 0:H] - nn(hi, z[...]), f1[...])
    return lo, hi


def kernel(
    diag, coup, info, out,
    d1, c0, c1, hin, d2, xl, xu, c1t, h1, ycat, v1, v2, f1a, f2a, za, f1b, f2b, zb, f1c, f2c, zc, hv, hy, xfirst, placed, ga, gb,
    own_h, rc1, rc2, pu01, pu02, sx0, pl1, pl2, pu1, pu2, sx, xin, xown,
    g1_send, g1_recv, r1_recv, r2_recv, rx_recv, s_send, x_send, x_recv, own_sem,
):
    s = lax.axis_index("tm")
    j = lax.axis_index("state")
    core = lax.rem(j, 2)
    sibling = j + 1 - 2 * core
    rows = pl.ds(pl.multiple_of(j * 32, 32), 32)

    even = lax.rem(s, 2) == 0

    level, dist = jnp.int32(6), jnp.int32(64)
    to_lower, to_upper = jnp.bool_(False), jnp.bool_(False)
    for k in range(6):
        d = 2**k
        mine = lax.rem(s, 2 * d) == d
        level, dist = jnp.where(mine, k, level), jnp.where(mine, d, dist)
        if k < 5:
            to_lower = to_lower | (mine & (lax.rem(s - d, 4 * d) == 2 * d))
            to_upper = to_upper | (mine & (s + d < 64) & (lax.rem(s + d, 4 * d) == 2 * d))
    inner = s > 0
    upper = s + dist < 64

    barrier = pltpu.get_barrier_semaphore()
    for r in range(1, 8):
        pl.semaphore_signal(
            barrier, inc=1, device_id=(s, lax.rem(j + r, 8)), device_id_type=MESH
        )

    def greet(k, carry):
        d, count = carry
        up = s + d < 64

        @pl.when(inner)
        def _():
            pl.semaphore_signal(barrier, inc=1, device_id=(s - d, j), device_id_type=MESH)

        @pl.when(up)
        def _():
            pl.semaphore_signal(barrier, inc=1, device_id=(s + d, j), device_id_type=MESH)

        return 2 * d, count + inner.astype(jnp.int32) + up.astype(jnp.int32)

    _, count = lax.fori_loop(0, level + 1, greet, (jnp.int32(1), jnp.int32(7)))

    root = s == 32
    reads_first = (s == 1) | (s == 2) | (s == 4) | (s == 8)
    count = count + reads_first.astype(jnp.int32) + 4 * root.astype(jnp.int32)

    @pl.when(reads_first)
    def _():
        pl.semaphore_signal(barrier, inc=1, device_id=(32, j), device_id_type=MESH)

    @pl.when(root)
    def _():
        for k in range(4):
            pl.semaphore_signal(barrier, inc=1, device_id=(2**k, j), device_id_type=MESH)

    first = [
        (diag.at[1, :, 0:H], d1.at[rows, 0:H]),
        (coup.at[0], c0.at[rows]),
        (coup.at[1], c1.at[rows]),
        (placed, hin.at[pl.ds(pl.multiple_of(j * 8, 8), 8)]),
        (diag.at[0], d2.at[rows]),
        (diag.at[1, :, H:N], d1.at[rows, H:N]),
    ]
    placed[...] = jnp.zeros((8, N), F32)
    for i in range(8):

        @pl.when(j == i)
        def _():
            placed[0:2, 32 * i : 32 * i + 32] = info[...]

    local = [
        pltpu.make_async_copy(src, dst, own_sem.at[a]) for a, (src, dst) in enumerate(first)
    ]
    for c in local:
        c.start()

    pl.semaphore_wait(barrier, count)

    def to(src, dst, send, recv, tm, state):
        return pltpu.make_async_remote_copy(
            src_ref=src, dst_ref=dst, send_sem=send, recv_sem=recv,
            device_id=(tm, state), device_id_type=MESH,
        )

    def peer(src, dst, sends, recvs, a, r):
        return to(src, dst, sends.at[a, r], recvs.at[a, r], s, lax.rem(j + r, 8))

    def gather(a, act):
        src, dst = first[a]
        for r in range(1, 8):
            act(peer(src, dst, g1_send, g1_recv, a, r))

    def direct(a, act):
        src, dst = first[a]
        for r in (2, 4, 6):
            act(peer(src, dst, g1_send, g1_recv, a, r))
        act(to(src, dst, g1_send.at[a, 1], g1_recv.at[a, 1], s, sibling))

    def hand_on(a, act):
        whole = (None, c0, c1, None, d2)[a]
        for r in (2, 4, 6):
            at = pl.ds(pl.multiple_of(lax.rem(j + 8 - r, 8) * 32, 32), 32)
            piece = whole.at[at]
            act(to(piece, piece, g1_send.at[a, r + 1], g1_recv.at[a, r + 1], s, sibling))

    def direct_arrived(a):
        src, dst = first[a]
        for r in (2, 4, 6):
            peer(src, dst, g1_send, g1_recv, a, r).wait_recv()

    def arrived(a):
        src, dst = first[a]
        local[a].wait()
        to(src, dst, g1_send.at[a, 1], g1_recv.at[a, 1], s, sibling).wait_recv()
        hand_on(a, lambda c: c.wait_recv())

    gather(0, lambda c: c.start())
    gather(5, lambda c: c.start())
    gather(0, lambda c: c.wait_send())
    gather(5, lambda c: c.wait_send())
    for a in (2, 1, 4):
        direct(a, lambda c: c.start())
    gather(3, lambda c: c.start())

    def gathered(a):
        local[a].wait()
        gather(a, lambda c: c.wait_recv())

    gathered(0)
    factor_start(d1, f1a)
    gathered(5)

    for a in (2, 1):
        direct_arrived(a)
        hand_on(a, lambda c: c.start())

    def fill0():
        arrived(2)
        arrived(1)
        gathered(3)
        info_all = sum8([hin[8 * i : 8 * i + 8, :] for i in range(8)])
        own_h[...] = row_of(info_all, 0)
        h1[...] = row_of(info_all, 1)
        c1t[...] = jnp.where(s == 63, 0.0, c1[...].T)
        project(c1t, 0, v1, ycat, N, H, f1a, za)
        lead_start(v1, pu01, N)
        project(c1t, H, v1, ycat, N + H, H, f1a, za)
        project(h1, 0, v1, ycat, 2 * N, 8, f1a, za)
        project(c0, 0, v1, ycat, 0, N, f1a, za)

    factor_rest(d1, {12: fill0}, f1a, f2a, za)
    lead_end(v1, ycat, f2a, pu01, N)

    up0 = s < 63

    def up0_sends(act):
        @pl.when(up0)
        def _():
            act(to(pu01, rc1.at[0], s_send.at[0], r1_recv.at[0], s + 1, j))

    def up0_rest(act):
        @pl.when(up0)
        def _():
            act(to(pu02, rc2.at[0], s_send.at[1], r2_recv.at[0], s + 1, j))

    def part_rows(part):
        return pl.ds(part * H, H)

    def up0_link(act):
        @pl.when(even)
        def _():
            for part in range(2):
                act(to(sx0.at[part], xl.at[part_rows(part)], s_send.at[2 + part], rx_recv.at[0, part], s + 1, j))

    up0_sends(lambda c: c.start())
    finish_rows(v1, ycat, f2a, N + H, H)
    finish_rows(v1, ycat, f2a, 2 * N, 8)
    rest_products(v1, pu02, N)
    up0_rest(lambda c: c.start())
    finish_rows(v1, ycat, f2a, 0, N)
    for part in range(2):
        sx0[part] = -nt(v1[part * H : part * H + H, :], v1[N : 2 * N, :])
    up0_link(lambda c: c.start())
    direct_arrived(4)
    hand_on(4, lambda c: c.start())
    back = nt(v1[2 * N : 2 * N + 8, :], v1[0:N, :])
    own_h[...] = own_h[...] - back
    arrived(4)
    hand_on(4, lambda c: c.wait_send())
    d2[0:H, 0:H] = d2[0:H, 0:H] - nt(v1[0:H, :], v1[0:H, :])
    d2[H:N, :] = d2[H:N, :] - nt(v1[H:N, :], v1[0:N, :])

    @pl.when(jnp.logical_not(even))
    def _():
        xu[...] = -nt(v1[N : 2 * N, :], v1[0:N, :])

    def take_lead(slot):
        to(pl1, rc1.at[slot], s_send.at[4], r1_recv.at[slot], s, j).wait_recv()
        d2[0:H, 0:H] = d2[0:H, 0:H] - rc1[slot]

    def take_rest(slot):
        to(pl2, rc2.at[slot], s_send.at[5], r2_recv.at[slot], s, j).wait_recv()
        d2[H:N, :] = d2[H:N, :] - rc2[slot, 0:H, :]
        own_h[...] = own_h[...] - rc2[slot, H : H + 8, :]

    @pl.when(even & inner)
    def _():
        take_lead(0)
        take_rest(0)

    def early(k, carry):
        @pl.when(inner)
        def _():
            take_lead(1 + 2 * k)
            take_rest(1 + 2 * k)

        take_lead(2 + 2 * k)
        take_rest(2 + 2 * k)
        return carry

    below = jnp.minimum(level, 5)
    lax.fori_loop(0, jnp.maximum(below - 1, 0), early, 0)

    left_slot = jnp.where(even, 2 * level - 1, 0)

    def take_last(take):
        @pl.when(inner)
        def _():
            take(left_slot)

        @pl.when(even)
        def _():
            take(2 * below)

    take_last(take_lead)

    def take_link(part):
        @pl.when(inner)
        def _():
            to(sx0.at[0], xl.at[part_rows(part)], s_send.at[2], rx_recv.at[0, part], s, j).wait_recv()

        @pl.when(even & inner)
        def _():
            to(sx0.at[0], xu.at[part_rows(part)], s_send.at[2], rx_recv.at[1, part], s, j).wait_recv()

    def first_lead():
        return to(pl1, rc1.at[12], s_send.at[4], r1_recv.at[12], 32, j)

    def first_rest():
        return to(pl2, rc2.at[12], s_send.at[6], r2_recv.at[12], 32, j)

    @pl.when(s == 0)
    def _():
        pl1[...] = d2[0:H, 0:H]
        first_lead().start()
        take_last(take_rest)
        pl2[0:H, :] = d2[H:N, :]
        pl2[H : H + 8, :] = own_h[...]
        first_rest().start()

    @pl.when(inner)
    def _():
        factor_start(d2, f1b)
        take_last(take_rest)
        take_link(0)
        take_link(1)

        def fill():
            project(own_h, 0, v2, ycat, 2 * N, 8, f1b, zb)
            for x, at, to_ in ((xl, 0, pl1), (xu, N, pu1)):
                project(x, 0, v2, ycat, at, N, f1b, zb)
                lead_start(v2, to_, at)

        def fill_rest():
            rest_start(v2, pl2, 0)
            rest_start(v2, pu2, N)

        factor_rest(d2, {2: fill, 9: fill_rest}, f1b, f2b, zb)
        lead_end(v2, ycat, f2b, pl1, 0)
        lead_end(v2, ycat, f2b, pu1, N)

    sending = inner & jnp.logical_not(root)

    lower_slot, upper_slot = 2 + 2 * level, 1 + 2 * level

    def lead_sends(act):
        @pl.when(sending)
        def _():
            act(to(pl1, rc1.at[lower_slot], s_send.at[4], r1_recv.at[lower_slot], s - dist, j))

        @pl.when(upper)
        def _():
            act(to(pu1, rc1.at[upper_slot], s_send.at[5], r1_recv.at[upper_slot], s + dist, j))

    def rest_sends(act):
        @pl.when(sending)
        def _():
            act(to(pl2, rc2.at[lower_slot], s_send.at[6], r2_recv.at[lower_slot], s - dist, j))

        @pl.when(upper)
        def _():
            act(to(pu2, rc2.at[upper_slot], s_send.at[7], r2_recv.at[upper_slot], s + dist, j))

    def link_send(part, act):
        at = part_rows(part)

        @pl.when(to_lower)
        def _():
            act(to(sx.at[part], xu.at[at], s_send.at[8 + part], rx_recv.at[1, part], s - dist, j))

        @pl.when(to_upper)
        def _():
            act(to(sx.at[part], xl.at[at], s_send.at[8 + part], rx_recv.at[0, part], s + dist, j))

    lead_sends(lambda c: c.start())
    @pl.when(inner)
    def _():
        for at in (H, N + H):
            finish_rows(v2, ycat, f2b, at, H)
        finish_rows(v2, ycat, f2b, 2 * N, 8)
        rest_end(v2, pl2, 0)
        rest_end(v2, pu2, N)

    rest_sends(lambda c: c.start())

    for part in range(2):

        @pl.when(to_lower)
        def _():
            sx[part] = -nt(v2[N + part * H : N + part * H + H, :], v2[0:N, :])

        @pl.when(to_upper)
        def _():
            sx[part] = -nt(v2[part * H : part * H + H, :], v2[N : 2 * N, :])

        link_send(part, lambda c: c.start())

    def own_means():
        lo, hi = means(v2, f1b, f2b, zb)
        gb[:, 0:H] = lo
        gb[:, H:N] = hi

    def early_means():
        lo, hi = means(v1, f1a, f2a, za)
        ga[:, 0:H] = lo
        ga[:, H:N] = hi

    def spread_first(act):
        for a, seg in enumerate((16, 8, 4, 2, 1, 0)):
            act(to(xfirst, xin.at[0], x_send.at[13 + a], x_recv.at[0], seg, j))

    @pl.when(root)
    def _():
        to(pl1, rc1.at[12], s_send.at[4], r1_recv.at[12], s, j).wait_recv()
        to(pl2, rc2.at[12], s_send.at[6], r2_recv.at[12], s, j).wait_recv()
        d1[0:H, 0:H] = rc1[12] - pl1[...]
        d1[H:N, :] = rc2[12, 0:H, :] - pl2[0:H, :]
        h1[...] = rc2[12, H : H + 8, :] - pl2[H : H + 8, :]
        factor_start(d1, f1c)

        def fill():
            project(h1, 0, hv, hy, 0, 8, f1c, zc)
            own_means()

        factor_rest(d1, {2: fill}, f1c, f2c, zc)
        finish_rows(hv, hy, f2c, 0, 8)
        lo, hi = means(hv, f1c, f2c, zc)
        xfirst[:, 0:H] = lo
        xfirst[:, H:N] = hi
        spread_first(lambda c: c.start())
        xown[...] = gb[2 * N : 2 * N + 8, :] - nn(xfirst[...], gb[0:N, :])

    @pl.when(jnp.logical_not(root))
    def _():
        @pl.when(inner)
        def _():
            own_means()

        early_means()

    def wait_mean(a):
        to(xown, xin.at[a], x_send.at[0], x_recv.at[a], s, j).wait_recv()

    @pl.when(s == 0)
    def _():
        wait_mean(0)
        xown[...] = xin[0]
        xin[1] = jnp.zeros((8, N), F32)

    @pl.when(to_lower)
    def _():
        @pl.when(upper)
        def _():
            wait_mean(1)

        @pl.when(jnp.logical_not(upper))
        def _():
            xin[1] = jnp.zeros((8, N), F32)

        xown[...] = gb[2 * N : 2 * N + 8, :] - nn(xin[1], gb[N : 2 * N, :])
        wait_mean(0)
        xown[...] = xown[...] - nn(xin[0], gb[0:N, :])

    @pl.when(to_upper)
    def _():
        wait_mean(0)
        xown[...] = gb[2 * N : 2 * N + 8, :] - nn(xin[0], gb[0:N, :])
        wait_mean(1)
        xown[...] = xown[...] - nn(xin[1], gb[N : 2 * N, :])

    def spread(act):
        def step(i, d):
            k = level - 1 - i
            act(to(xown, xin.at[0], x_send.at[2 * k], x_recv.at[0], s + d, j))
            act(to(xown, xin.at[1], x_send.at[2 * k + 1], x_recv.at[1], s - d, j))
            return d // 2

        lax.fori_loop(0, jnp.where(inner, level, 0), step, dist // 2)

        @pl.when(jnp.logical_not(even))
        def _():
            act(to(xown, xin.at[2], x_send.at[12], x_recv.at[2], s - 1, j))

    spread(lambda c: c.start())

    @pl.when(root)
    def _():
        early_means()

    part = ga[2 * N : 2 * N + 8, :] - nn(xown[...], ga[0:N, :])

    @pl.when(even)
    def _():
        to(xown, xin.at[2], x_send.at[12], x_recv.at[2], s, j).wait_recv()

    @pl.when(jnp.logical_not(even))
    def _():
        xin[2] = xin[1]

    later = part - nn(xin[2], ga[N : 2 * N, :])
    both = jnp.concatenate([xown[0:1, :], later[0:1, :]], axis=0)
    for i in range(8):

        @pl.when(j == i)
        def _():
            out[...] = both[:, 32 * i : 32 * i + 32]

    gather(3, lambda c: c.wait_send())
    for a in (1, 2, 4):
        direct(a, lambda c: c.wait_send())
    for a in (1, 2):
        hand_on(a, lambda c: c.wait_send())

    up0_sends(lambda c: c.wait_send())
    up0_link(lambda c: c.wait_send())
    up0_rest(lambda c: c.wait_send())


    @pl.when(s == 0)
    def _():
        first_lead().wait_send()
        first_rest().wait_send()

    @pl.when(root)
    def _():
        spread_first(lambda c: c.wait_send())

    lead_sends(lambda c: c.wait_send())
    for part in range(2):
        link_send(part, lambda c: c.wait_send())
    rest_sends(lambda c: c.wait_send())
    spread(lambda c: c.wait_send())


def body(diagonal, coupling, info):
    vmem = pltpu.VMEM
    dma = pltpu.SemaphoreType.DMA
    square = vmem((N, N), F32)
    half = vmem((H, H), F32)
    tall = vmem((2 * N + 8, N), F32)
    slab = vmem((H + 8, N), F32)
    pair = vmem((2, H, N), F32)
    return pl.pallas_call(
        kernel,
        out_shape=jax.ShapeDtypeStruct((2, 32), F32),
        in_specs=[pl.BlockSpec(memory_space=m) for m in (pltpu.HBM, pltpu.HBM, vmem)],
        out_specs=pl.BlockSpec(memory_space=vmem),
        scratch_shapes=[
            square, square, square, vmem((64, N), F32), square, square, square, square, vmem((8, N), F32), vmem((2 * N + 8, H), F32), tall, tall,
            half, half, half, half, half, half, half, half, half,
            vmem((8, N), F32), vmem((8, H), F32), vmem((8, N), F32), vmem((8, N), F32), tall, tall,
            vmem((8, N), F32), vmem((13, H, H), F32), vmem((13, H + 8, N), F32),
            half, slab, pair, half, slab, half, slab, pair,
            vmem((3, 8, N), F32), vmem((8, N), F32),
            dma((6, 8)), dma((6, 8)),
            dma((13,)), dma((13,)), dma((2, 2)), dma((10,)), dma((19,)), dma((3,)), dma((6,)),
        ],
        compiler_params=pltpu.CompilerParams(
            collective_id=0, has_side_effects=True, vmem_limit_bytes=32 * 1024 * 1024
        ),
    )(diagonal, coupling, info)


def solution(mesh):
    placed = (P("tm", "state", None), P("tm", "state", None), P("tm", "state"))
    return jax.shard_map(
        body, mesh=mesh, in_specs=placed, out_specs=P("tm", "state"), check_vma=False
    )
```

```python
import jax
import jax.numpy as jnp
from jax import lax
from jax.experimental import pallas as pl
from jax.experimental.pallas import tpu as pltpu
from jax.sharding import PartitionSpec as P

N = 256
H = 128
F32 = jnp.float32
MESH = pl.DeviceIdType.MESH
EXACT = lax.Precision.HIGHEST


def nt(a, b):
    return lax.dot_general(
        a, b, (((1,), (1,)), ((), ())), precision=EXACT, preferred_element_type=F32
    )


def nn(a, b):
    return jnp.dot(a, b, precision=EXACT, preferred_element_type=F32)


def row_of(x, k):
    return jnp.broadcast_to(x[k : k + 1, :], x.shape)


def lane_of(x, l):
    return jnp.take_along_axis(x, jnp.full((8, H), l, jnp.int32), axis=1)


def sum8(t):
    return ((t[0] + t[1]) + (t[2] + t[3])) + ((t[4] + t[5]) + (t[6] + t[7]))


def pivot_block(w, b, sub, lane):
    at = 8 * b
    c = [lane_of(w[b], at + j) for j in range(8)]
    inside = (lane >= at) & (lane < at + 8)
    r = jnp.where(inside, (lane - at == sub).astype(F32), w[b])
    t = r
    pivots = jnp.ones((8, H), F32)
    inverses = []
    for k in range(0, 8, 2):
        first, second = sub == k, sub == k + 1
        p, q, o = row_of(c[k], k), row_of(c[k + 1], k), row_of(c[k + 1], k + 1)
        det = 1.0 / (p * o - q * q)
        m0 = jnp.where(first | second, 0.0, c[k])
        m1 = jnp.where(first | second, 0.0, c[k + 1])
        f0 = (m0 * o - m1 * q) * det
        f1 = (m1 * p - m0 * q) * det
        inverses.append((o * det, -q * det, p * det))
        ratio = q * (1.0 / p)
        r0, r1 = row_of(r, k), row_of(r, k + 1)
        t = jnp.where(first, r0, jnp.where(second, r1 - ratio * r0, t))
        pivots = jnp.where(first, p, jnp.where(second, o - ratio * q, pivots))
        for j in range(k + 2, 8):
            c[j] = c[j] - (f0 * row_of(c[j], k) + f1 * row_of(c[j], k + 1))
        r = r - (f0 * r0 + f1 * r1)
    if b < 15:
        rows = []
        for k in range(0, 8, 2):
            ia, ib, ic = inverses[k // 2]
            r0, r1 = row_of(r, k), row_of(r, k + 1)
            rows += [ia * r0 + ib * r1, ib * r0 + ic * r1]
        for i in range(b + 1, 16):
            cols = [lane_of(w[i], at + j) for j in range(8)]
            w[i] = jnp.where(inside, 0.0, w[i]) - sum8([cols[j] * rows[j] for j in range(8)])
    return jnp.where(lane < at + 8, t * lax.rsqrt(pivots), 0.0)


def factor_part(w, blocks):
    sub = lax.broadcasted_iota(jnp.int32, (8, H), 0)
    lane = lax.broadcasted_iota(jnp.int32, (8, H), 1)
    return [pivot_block(w, b, sub, lane) for b in blocks]


def groups(a):
    return [a[8 * r : 8 * r + 8, :] for r in range(16)]


def factor_start(block, f1):
    f1[...] = jnp.concatenate(factor_part(groups(block[0:H, 0:H]), range(16)), axis=0)


def factor_rest(block, steps, f1, f2, z):
    z[...] = nt(block[H:N, 0:H], f1[...])
    w = groups(block[H:N, H:N] - nt(z[...], z[...]))
    out = []
    for b in range(16):
        if b in steps:
            steps[b]()
        out += factor_part(w, [b])
    f2[...] = jnp.concatenate(out, axis=0)


def project(x, at, v, y, to, n, f1, z):
    v[to : to + n, 0:H] = nt(x[at : at + n, 0:H], f1[...])
    y[to : to + n, :] = x[at : at + n, H:N] - nt(v[to : to + n, 0:H], z[...])


def lead_start(v, to, at):
    to[...] = nt(v[at : at + H, 0:H], v[at : at + H, 0:H])


def lead_end(v, y, f2, to, at):
    top = nt(y[at : at + H, :], f2[...])
    v[at : at + H, H:N] = top
    to[...] = to[...] + nt(top, top)


def rest_products(v, to, at):
    to[0:H, :] = nt(v[at + H : at + N, :], v[at : at + N, :])
    to[H : H + 8, :] = nt(v[2 * N : 2 * N + 8, :], v[at : at + N, :])


def rest_rows(v, at, cols):
    return jnp.concatenate([v[at + H : at + N, cols], v[2 * N : 2 * N + 8, cols]], axis=0)


def rest_start(v, to, at):
    c = slice(0, H)
    to[...] = nt(rest_rows(v, at, c), v[at : at + N, c])


def rest_end(v, to, at):
    c = slice(H, N)
    to[...] = to[...] + nt(rest_rows(v, at, c), v[at : at + N, c])


def finish_rows(v, y, f2, at, n):
    v[at : at + n, H:N] = nt(y[at : at + n, :], f2[...])


def means(v, f1, f2, z):
    hi = nn(v[:, H:N], f2[...])
    lo = nn(v[:, 0:H] - nn(hi, z[...]), f1[...])
    return lo, hi


def kernel(
    diag, coup, info, out,
    d1, c0, c1, hin, d2, xl, xu, c1t, h1, ycat, v1, v2, f1a, f2a, za, f1b, f2b, zb, f1c, f2c, zc, hv, hy, xfirst, placed, ga, gb,
    own_h, rc1, rc2, pu01, pu02, sx0, pl1, pl2, pu1, pu2, sx, xin, xown,
    g1_send, g1_recv, r1_recv, r2_recv, rx_recv, s_send, x_send, x_recv, own_sem,
):
    s = lax.axis_index("tm")
    j = lax.axis_index("state")
    core = lax.rem(j, 2)
    sibling = j + 1 - 2 * core
    rows = pl.ds(pl.multiple_of(j * 32, 32), 32)

    even = lax.rem(s, 2) == 0

    level, dist = jnp.int32(6), jnp.int32(64)
    to_lower, to_upper = jnp.bool_(False), jnp.bool_(False)
    for k in range(6):
        d = 2**k
        mine = lax.rem(s, 2 * d) == d
        level, dist = jnp.where(mine, k, level), jnp.where(mine, d, dist)
        if k < 5:
            to_lower = to_lower | (mine & (lax.rem(s - d, 4 * d) == 2 * d))
            to_upper = to_upper | (mine & (s + d < 64) & (lax.rem(s + d, 4 * d) == 2 * d))
    inner = s > 0
    upper = s + dist < 64

    barrier = pltpu.get_barrier_semaphore()
    for r in range(1, 8):
        pl.semaphore_signal(
            barrier, inc=1, device_id=(s, lax.rem(j + r, 8)), device_id_type=MESH
        )

    def greet(k, carry):
        d, count = carry
        up = s + d < 64

        @pl.when(inner)
        def _():
            pl.semaphore_signal(barrier, inc=1, device_id=(s - d, j), device_id_type=MESH)

        @pl.when(up)
        def _():
            pl.semaphore_signal(barrier, inc=1, device_id=(s + d, j), device_id_type=MESH)

        return 2 * d, count + inner.astype(jnp.int32) + up.astype(jnp.int32)

    _, count = lax.fori_loop(0, level + 1, greet, (jnp.int32(1), jnp.int32(7)))

    root = s == 32
    reads_first = (s == 1) | (s == 2) | (s == 4) | (s == 8)
    count = count + reads_first.astype(jnp.int32) + 4 * root.astype(jnp.int32)

    @pl.when(reads_first)
    def _():
        pl.semaphore_signal(barrier, inc=1, device_id=(32, j), device_id_type=MESH)

    @pl.when(root)
    def _():
        for k in range(4):
            pl.semaphore_signal(barrier, inc=1, device_id=(2**k, j), device_id_type=MESH)

    first = [
        (diag.at[1, :, 0:H], d1.at[rows, 0:H]),
        (coup.at[0], c0.at[rows]),
        (coup.at[1], c1.at[rows]),
        (placed, hin.at[pl.ds(pl.multiple_of(j * 8, 8), 8)]),
        (diag.at[0], d2.at[rows]),
        (diag.at[1, :, H:N], d1.at[rows, H:N]),
    ]
    placed[...] = jnp.zeros((8, N), F32)
    for i in range(8):

        @pl.when(j == i)
        def _():
            placed[0:2, 32 * i : 32 * i + 32] = info[...]

    local = [
        pltpu.make_async_copy(src, dst, own_sem.at[a]) for a, (src, dst) in enumerate(first)
    ]
    for c in local:
        c.start()

    pl.semaphore_wait(barrier, count)

    def to(src, dst, send, recv, tm, state):
        return pltpu.make_async_remote_copy(
            src_ref=src, dst_ref=dst, send_sem=send, recv_sem=recv,
            device_id=(tm, state), device_id_type=MESH,
        )

    def peer(src, dst, sends, recvs, a, r):
        return to(src, dst, sends.at[a, r], recvs.at[a, r], s, lax.rem(j + r, 8))

    def gather(a, act):
        src, dst = first[a]
        for r in range(1, 8):
            act(peer(src, dst, g1_send, g1_recv, a, r))

    def direct(a, act):
        src, dst = first[a]
        for r in (2, 4, 6):
            act(peer(src, dst, g1_send, g1_recv, a, r))
        act(to(src, dst, g1_send.at[a, 1], g1_recv.at[a, 1], s, sibling))

    def hand_on(a, act):
        whole = (None, c0, c1, None, d2)[a]
        for r in (2, 4, 6):
            at = pl.ds(pl.multiple_of(lax.rem(j + 8 - r, 8) * 32, 32), 32)
            piece = whole.at[at]
            act(to(piece, piece, g1_send.at[a, r + 1], g1_recv.at[a, r + 1], s, sibling))

    def direct_arrived(a):
        src, dst = first[a]
        for r in (2, 4, 6):
            peer(src, dst, g1_send, g1_recv, a, r).wait_recv()

    def arrived(a):
        src, dst = first[a]
        local[a].wait()
        to(src, dst, g1_send.at[a, 1], g1_recv.at[a, 1], s, sibling).wait_recv()
        hand_on(a, lambda c: c.wait_recv())

    gather(0, lambda c: c.start())
    gather(5, lambda c: c.start())
    gather(0, lambda c: c.wait_send())
    gather(5, lambda c: c.wait_send())
    for a in (2, 1, 4):
        direct(a, lambda c: c.start())
    gather(3, lambda c: c.start())

    def gathered(a):
        local[a].wait()
        gather(a, lambda c: c.wait_recv())

    gathered(0)
    factor_start(d1, f1a)
    gathered(5)

    for a in (2, 1):
        direct_arrived(a)
        hand_on(a, lambda c: c.start())

    def fill0():
        arrived(2)
        arrived(1)
        gathered(3)
        info_all = sum8([hin[8 * i : 8 * i + 8, :] for i in range(8)])
        own_h[...] = row_of(info_all, 0)
        h1[...] = row_of(info_all, 1)
        c1t[...] = jnp.where(s == 63, 0.0, c1[...].T)
        project(c1t, 0, v1, ycat, N, H, f1a, za)
        lead_start(v1, pu01, N)
        project(c1t, H, v1, ycat, N + H, H, f1a, za)
        project(h1, 0, v1, ycat, 2 * N, 8, f1a, za)
        project(c0, 0, v1, ycat, 0, N, f1a, za)

    factor_rest(d1, {12: fill0}, f1a, f2a, za)
    lead_end(v1, ycat, f2a, pu01, N)

    up0 = s < 63

    def up0_sends(act):
        @pl.when(up0)
        def _():
            act(to(pu01, rc1.at[0], s_send.at[0], r1_recv.at[0], s + 1, j))

    def up0_rest(act):
        @pl.when(up0)
        def _():
            act(to(pu02, rc2.at[0], s_send.at[1], r2_recv.at[0], s + 1, j))

    def part_rows(part):
        return pl.ds(part * H, H)

    def up0_link(act):
        @pl.when(even)
        def _():
            for part in range(2):
                act(to(sx0.at[part], xl.at[part_rows(part)], s_send.at[2 + part], rx_recv.at[0, part], s + 1, j))

    up0_sends(lambda c: c.start())
    finish_rows(v1, ycat, f2a, N + H, H)
    finish_rows(v1, ycat, f2a, 2 * N, 8)
    rest_products(v1, pu02, N)
    up0_rest(lambda c: c.start())
    finish_rows(v1, ycat, f2a, 0, N)
    for part in range(2):
        sx0[part] = -nt(v1[part * H : part * H + H, :], v1[N : 2 * N, :])
    up0_link(lambda c: c.start())
    direct_arrived(4)
    hand_on(4, lambda c: c.start())
    back = nt(v1[2 * N : 2 * N + 8, :], v1[0:N, :])
    own_h[...] = own_h[...] - back
    arrived(4)
    hand_on(4, lambda c: c.wait_send())
    d2[0:H, 0:H] = d2[0:H, 0:H] - nt(v1[0:H, :], v1[0:H, :])
    d2[H:N, :] = d2[H:N, :] - nt(v1[H:N, :], v1[0:N, :])

    @pl.when(jnp.logical_not(even))
    def _():
        xu[...] = -nt(v1[N : 2 * N, :], v1[0:N, :])

    def take_lead(slot):
        to(pl1, rc1.at[slot], s_send.at[4], r1_recv.at[slot], s, j).wait_recv()
        d2[0:H, 0:H] = d2[0:H, 0:H] - rc1[slot]

    def take_rest(slot):
        to(pl2, rc2.at[slot], s_send.at[5], r2_recv.at[slot], s, j).wait_recv()
        d2[H:N, :] = d2[H:N, :] - rc2[slot, 0:H, :]
        own_h[...] = own_h[...] - rc2[slot, H : H + 8, :]

    @pl.when(even & inner)
    def _():
        take_lead(0)
        take_rest(0)

    def early(k, carry):
        @pl.when(inner)
        def _():
            take_lead(1 + 2 * k)
            take_rest(1 + 2 * k)

        take_lead(2 + 2 * k)
        take_rest(2 + 2 * k)
        return carry

    below = jnp.minimum(level, 5)
    lax.fori_loop(0, jnp.maximum(below - 1, 0), early, 0)

    left_slot = jnp.where(even, 2 * level - 1, 0)

    def take_last(take):
        @pl.when(inner)
        def _():
            take(left_slot)

        @pl.when(even)
        def _():
            take(2 * below)

    take_last(take_lead)

    def take_link(part):
        @pl.when(inner)
        def _():
            to(sx0.at[0], xl.at[part_rows(part)], s_send.at[2], rx_recv.at[0, part], s, j).wait_recv()

        @pl.when(even & inner)
        def _():
            to(sx0.at[0], xu.at[part_rows(part)], s_send.at[2], rx_recv.at[1, part], s, j).wait_recv()

    def first_lead():
        return to(pl1, rc1.at[12], s_send.at[4], r1_recv.at[12], 32, j)

    def first_rest():
        return to(pl2, rc2.at[12], s_send.at[6], r2_recv.at[12], 32, j)

    @pl.when(s == 0)
    def _():
        pl1[...] = d2[0:H, 0:H]
        first_lead().start()
        take_last(take_rest)
        pl2[0:H, :] = d2[H:N, :]
        pl2[H : H + 8, :] = own_h[...]
        first_rest().start()

    @pl.when(inner)
    def _():
        factor_start(d2, f1b)
        take_last(take_rest)
        take_link(0)

        def fill():
            project(own_h, 0, v2, ycat, 2 * N, 8, f1b, zb)
            for x, at, to_ in ((xl, 0, pl1), (xu, N, pu1)):
                project(x, 0, v2, ycat, at, H, f1b, zb)
                lead_start(v2, to_, at)

        def fill_rest():
            take_link(1)
            for x, at in ((xl, H), (xu, N + H)):
                project(x, H, v2, ycat, at, H, f1b, zb)
            rest_start(v2, pl2, 0)
            rest_start(v2, pu2, N)

        factor_rest(d2, {2: fill, 8: fill_rest}, f1b, f2b, zb)
        lead_end(v2, ycat, f2b, pl1, 0)
        lead_end(v2, ycat, f2b, pu1, N)

    sending = inner & jnp.logical_not(root)

    lower_slot, upper_slot = 2 + 2 * level, 1 + 2 * level

    def lead_sends(act):
        @pl.when(sending)
        def _():
            act(to(pl1, rc1.at[lower_slot], s_send.at[4], r1_recv.at[lower_slot], s - dist, j))

        @pl.when(upper)
        def _():
            act(to(pu1, rc1.at[upper_slot], s_send.at[5], r1_recv.at[upper_slot], s + dist, j))

    def rest_sends(act):
        @pl.when(sending)
        def _():
            act(to(pl2, rc2.at[lower_slot], s_send.at[6], r2_recv.at[lower_slot], s - dist, j))

        @pl.when(upper)
        def _():
            act(to(pu2, rc2.at[upper_slot], s_send.at[7], r2_recv.at[upper_slot], s + dist, j))

    def link_send(part, act):
        at = part_rows(part)

        @pl.when(to_lower)
        def _():
            act(to(sx.at[part], xu.at[at], s_send.at[8 + part], rx_recv.at[1, part], s - dist, j))

        @pl.when(to_upper)
        def _():
            act(to(sx.at[part], xl.at[at], s_send.at[8 + part], rx_recv.at[0, part], s + dist, j))

    lead_sends(lambda c: c.start())
    @pl.when(inner)
    def _():
        for at in (H, N + H):
            finish_rows(v2, ycat, f2b, at, H)
        finish_rows(v2, ycat, f2b, 2 * N, 8)
        rest_end(v2, pl2, 0)
        rest_end(v2, pu2, N)

    rest_sends(lambda c: c.start())

    for part in range(2):

        @pl.when(to_lower)
        def _():
            sx[part] = -nt(v2[N + part * H : N + part * H + H, :], v2[0:N, :])

        @pl.when(to_upper)
        def _():
            sx[part] = -nt(v2[part * H : part * H + H, :], v2[N : 2 * N, :])

        link_send(part, lambda c: c.start())

    def own_means():
        lo, hi = means(v2, f1b, f2b, zb)
        gb[:, 0:H] = lo
        gb[:, H:N] = hi

    def early_means():
        lo, hi = means(v1, f1a, f2a, za)
        ga[:, 0:H] = lo
        ga[:, H:N] = hi

    def spread_first(act):
        for a, seg in enumerate((16, 8, 4, 2, 1, 0)):
            act(to(xfirst, xin.at[0], x_send.at[13 + a], x_recv.at[0], seg, j))

    @pl.when(root)
    def _():
        to(pl1, rc1.at[12], s_send.at[4], r1_recv.at[12], s, j).wait_recv()
        to(pl2, rc2.at[12], s_send.at[6], r2_recv.at[12], s, j).wait_recv()
        d1[0:H, 0:H] = rc1[12] - pl1[...]
        d1[H:N, :] = rc2[12, 0:H, :] - pl2[0:H, :]
        h1[...] = rc2[12, H : H + 8, :] - pl2[H : H + 8, :]
        factor_start(d1, f1c)

        def fill():
            project(h1, 0, hv, hy, 0, 8, f1c, zc)
            own_means()

        factor_rest(d1, {2: fill}, f1c, f2c, zc)
        finish_rows(hv, hy, f2c, 0, 8)
        lo, hi = means(hv, f1c, f2c, zc)
        xfirst[:, 0:H] = lo
        xfirst[:, H:N] = hi
        spread_first(lambda c: c.start())
        xown[...] = gb[2 * N : 2 * N + 8, :] - nn(xfirst[...], gb[0:N, :])

    @pl.when(jnp.logical_not(root))
    def _():
        @pl.when(inner)
        def _():
            own_means()

        early_means()

    def wait_mean(a):
        to(xown, xin.at[a], x_send.at[0], x_recv.at[a], s, j).wait_recv()

    @pl.when(s == 0)
    def _():
        wait_mean(0)
        xown[...] = xin[0]
        xin[1] = jnp.zeros((8, N), F32)

    @pl.when(to_lower)
    def _():
        @pl.when(upper)
        def _():
            wait_mean(1)

        @pl.when(jnp.logical_not(upper))
        def _():
            xin[1] = jnp.zeros((8, N), F32)

        xown[...] = gb[2 * N : 2 * N + 8, :] - nn(xin[1], gb[N : 2 * N, :])
        wait_mean(0)
        xown[...] = xown[...] - nn(xin[0], gb[0:N, :])

    @pl.when(to_upper)
    def _():
        wait_mean(0)
        xown[...] = gb[2 * N : 2 * N + 8, :] - nn(xin[0], gb[0:N, :])
        wait_mean(1)
        xown[...] = xown[...] - nn(xin[1], gb[N : 2 * N, :])

    def spread(act):
        def step(i, d):
            k = level - 1 - i
            act(to(xown, xin.at[0], x_send.at[2 * k], x_recv.at[0], s + d, j))
            act(to(xown, xin.at[1], x_send.at[2 * k + 1], x_recv.at[1], s - d, j))
            return d // 2

        lax.fori_loop(0, jnp.where(inner, level, 0), step, dist // 2)

        @pl.when(jnp.logical_not(even))
        def _():
            act(to(xown, xin.at[2], x_send.at[12], x_recv.at[2], s - 1, j))

    spread(lambda c: c.start())

    @pl.when(root)
    def _():
        early_means()

    part = ga[2 * N : 2 * N + 8, :] - nn(xown[...], ga[0:N, :])

    @pl.when(even)
    def _():
        to(xown, xin.at[2], x_send.at[12], x_recv.at[2], s, j).wait_recv()

    @pl.when(jnp.logical_not(even))
    def _():
        xin[2] = xin[1]

    later = part - nn(xin[2], ga[N : 2 * N, :])
    both = jnp.concatenate([xown[0:1, :], later[0:1, :]], axis=0)
    for i in range(8):

        @pl.when(j == i)
        def _():
            out[...] = both[:, 32 * i : 32 * i + 32]

    gather(3, lambda c: c.wait_send())
    for a in (1, 2, 4):
        direct(a, lambda c: c.wait_send())
    for a in (1, 2):
        hand_on(a, lambda c: c.wait_send())

    up0_sends(lambda c: c.wait_send())
    up0_link(lambda c: c.wait_send())
    up0_rest(lambda c: c.wait_send())


    @pl.when(s == 0)
    def _():
        first_lead().wait_send()
        first_rest().wait_send()

    @pl.when(root)
    def _():
        spread_first(lambda c: c.wait_send())

    lead_sends(lambda c: c.wait_send())
    for part in range(2):
        link_send(part, lambda c: c.wait_send())
    rest_sends(lambda c: c.wait_send())
    spread(lambda c: c.wait_send())


def body(diagonal, coupling, info):
    vmem = pltpu.VMEM
    dma = pltpu.SemaphoreType.DMA
    square = vmem((N, N), F32)
    half = vmem((H, H), F32)
    tall = vmem((2 * N + 8, N), F32)
    slab = vmem((H + 8, N), F32)
    pair = vmem((2, H, N), F32)
    return pl.pallas_call(
        kernel,
        out_shape=jax.ShapeDtypeStruct((2, 32), F32),
        in_specs=[pl.BlockSpec(memory_space=m) for m in (pltpu.HBM, pltpu.HBM, vmem)],
        out_specs=pl.BlockSpec(memory_space=vmem),
        scratch_shapes=[
            square, square, square, vmem((64, N), F32), square, square, square, square, vmem((8, N), F32), vmem((2 * N + 8, H), F32), tall, tall,
            half, half, half, half, half, half, half, half, half,
            vmem((8, N), F32), vmem((8, H), F32), vmem((8, N), F32), vmem((8, N), F32), tall, tall,
            vmem((8, N), F32), vmem((13, H, H), F32), vmem((13, H + 8, N), F32),
            half, slab, pair, half, slab, half, slab, pair,
            vmem((3, 8, N), F32), vmem((8, N), F32),
            dma((6, 8)), dma((6, 8)),
            dma((13,)), dma((13,)), dma((2, 2)), dma((10,)), dma((19,)), dma((3,)), dma((6,)),
        ],
        compiler_params=pltpu.CompilerParams(
            collective_id=0, has_side_effects=True, vmem_limit_bytes=32 * 1024 * 1024
        ),
    )(diagonal, coupling, info)


def solution(mesh):
    placed = (P("tm", "state", None), P("tm", "state", None), P("tm", "state"))
    return jax.shard_map(
        body, mesh=mesh, in_specs=placed, out_specs=P("tm", "state"), check_vma=False
    )
```

```python
import jax
import jax.numpy as jnp
from jax import lax
from jax.experimental import pallas as pl
from jax.experimental.pallas import tpu as pltpu
from jax.sharding import PartitionSpec as P

N = 256
H = 128
F32 = jnp.float32
MESH = pl.DeviceIdType.MESH
EXACT = lax.Precision.HIGHEST


def nt(a, b):
    return lax.dot_general(
        a, b, (((1,), (1,)), ((), ())), precision=EXACT, preferred_element_type=F32
    )


def nn(a, b):
    return jnp.dot(a, b, precision=EXACT, preferred_element_type=F32)


def row_of(x, k):
    return jnp.broadcast_to(x[k : k + 1, :], x.shape)


def lane_of(x, l):
    return jnp.take_along_axis(x, jnp.full((8, H), l, jnp.int32), axis=1)


def sum8(t):
    return ((t[0] + t[1]) + (t[2] + t[3])) + ((t[4] + t[5]) + (t[6] + t[7]))


def pivot_block(w, b, sub, lane):
    at = 8 * b
    c = [lane_of(w[b], at + j) for j in range(8)]
    inside = (lane >= at) & (lane < at + 8)
    r = jnp.where(inside, (lane - at == sub).astype(F32), w[b])
    t = r
    pivots = jnp.ones((8, H), F32)
    inverses = []
    for k in range(0, 8, 2):
        first, second = sub == k, sub == k + 1
        p, q, o = row_of(c[k], k), row_of(c[k + 1], k), row_of(c[k + 1], k + 1)
        det = 1.0 / (p * o - q * q)
        m0 = jnp.where(first | second, 0.0, c[k])
        m1 = jnp.where(first | second, 0.0, c[k + 1])
        f0 = (m0 * o - m1 * q) * det
        f1 = (m1 * p - m0 * q) * det
        inverses.append((o * det, -q * det, p * det))
        ratio = q * (1.0 / p)
        r0, r1 = row_of(r, k), row_of(r, k + 1)
        t = jnp.where(first, r0, jnp.where(second, r1 - ratio * r0, t))
        pivots = jnp.where(first, p, jnp.where(second, o - ratio * q, pivots))
        for j in range(k + 2, 8):
            c[j] = c[j] - (f0 * row_of(c[j], k) + f1 * row_of(c[j], k + 1))
        r = r - (f0 * r0 + f1 * r1)
    if b < 15:
        rows = []
        for k in range(0, 8, 2):
            ia, ib, ic = inverses[k // 2]
            r0, r1 = row_of(r, k), row_of(r, k + 1)
            rows += [ia * r0 + ib * r1, ib * r0 + ic * r1]
        for i in range(b + 1, 16):
            cols = [lane_of(w[i], at + j) for j in range(8)]
            w[i] = jnp.where(inside, 0.0, w[i]) - sum8([cols[j] * rows[j] for j in range(8)])
    return jnp.where(lane < at + 8, t * lax.rsqrt(pivots), 0.0)


def factor_part(w, blocks):
    sub = lax.broadcasted_iota(jnp.int32, (8, H), 0)
    lane = lax.broadcasted_iota(jnp.int32, (8, H), 1)
    return [pivot_block(w, b, sub, lane) for b in blocks]


def groups(a):
    return [a[8 * r : 8 * r + 8, :] for r in range(16)]


def factor_start(block, f1):
    f1[...] = jnp.concatenate(factor_part(groups(block[0:H, 0:H]), range(16)), axis=0)


def factor_rest(block, steps, f1, f2, z):
    z[...] = nt(block[H:N, 0:H], f1[...])
    w = groups(block[H:N, H:N] - nt(z[...], z[...]))
    out = []
    for b in range(16):
        if b in steps:
            steps[b]()
        out += factor_part(w, [b])
    f2[...] = jnp.concatenate(out, axis=0)


def project(x, at, v, y, to, n, f1, z):
    v[to : to + n, 0:H] = nt(x[at : at + n, 0:H], f1[...])
    y[to : to + n, :] = x[at : at + n, H:N] - nt(v[to : to + n, 0:H], z[...])


def lead_start(v, to, at):
    to[...] = nt(v[at : at + H, 0:H], v[at : at + H, 0:H])


def lead_end(v, y, f2, to, at):
    top = nt(y[at : at + H, :], f2[...])
    v[at : at + H, H:N] = top
    to[...] = to[...] + nt(top, top)


def rest_products(v, to, at):
    to[0:H, :] = nt(v[at + H : at + N, :], v[at : at + N, :])
    to[H : H + 8, :] = nt(v[2 * N : 2 * N + 8, :], v[at : at + N, :])


def rest_rows(v, at, cols):
    return jnp.concatenate([v[at + H : at + N, cols], v[2 * N : 2 * N + 8, cols]], axis=0)


def rest_start(v, to, at):
    c = slice(0, H)
    to[...] = nt(rest_rows(v, at, c), v[at : at + N, c])


def rest_end(v, to, at):
    c = slice(H, N)
    to[...] = to[...] + nt(rest_rows(v, at, c), v[at : at + N, c])


def finish_rows(v, y, f2, at, n):
    v[at : at + n, H:N] = nt(y[at : at + n, :], f2[...])


def means(v, f1, f2, z):
    hi = nn(v[:, H:N], f2[...])
    lo = nn(v[:, 0:H] - nn(hi, z[...]), f1[...])
    return lo, hi


def kernel(
    diag, coup, info, out,
    d1, c0, c1, hin, d2, xl, xu, c1t, h1, ycat, v1, v2, f1a, f2a, za, f1b, f2b, zb, f1c, f2c, zc, hv, hy, xfirst, placed, gat, cols, cols_in, fold, fold_in, ga, gb,
    own_h, rc1, rc2, pu01, pu02, sx0, pl1, pl2, pu1, pu2, sx, xin, xown,
    g1_send, g1_recv, r1_recv, r2_recv, rx_recv, s_send, x_send, x_recv, own_sem, fold_send, fold_recv,
):
    s = lax.axis_index("tm")
    j = lax.axis_index("state")
    core = lax.rem(j, 2)
    sibling = j + 1 - 2 * core
    rows = pl.ds(pl.multiple_of(j * 32, 32), 32)

    even = lax.rem(s, 2) == 0

    level, dist = jnp.int32(6), jnp.int32(64)
    to_lower, to_upper = jnp.bool_(False), jnp.bool_(False)
    for k in range(6):
        d = 2**k
        mine = lax.rem(s, 2 * d) == d
        level, dist = jnp.where(mine, k, level), jnp.where(mine, d, dist)
        if k < 5:
            to_lower = to_lower | (mine & (lax.rem(s - d, 4 * d) == 2 * d))
            to_upper = to_upper | (mine & (s + d < 64) & (lax.rem(s + d, 4 * d) == 2 * d))
    inner = s > 0
    upper = s + dist < 64

    barrier = pltpu.get_barrier_semaphore()
    for r in range(1, 8):
        pl.semaphore_signal(
            barrier, inc=1, device_id=(s, lax.rem(j + r, 8)), device_id_type=MESH
        )

    def greet(k, carry):
        d, count = carry
        up = s + d < 64

        @pl.when(inner)
        def _():
            pl.semaphore_signal(barrier, inc=1, device_id=(s - d, j), device_id_type=MESH)

        @pl.when(up)
        def _():
            pl.semaphore_signal(barrier, inc=1, device_id=(s + d, j), device_id_type=MESH)

        return 2 * d, count + inner.astype(jnp.int32) + up.astype(jnp.int32)

    _, count = lax.fori_loop(0, level + 1, greet, (jnp.int32(1), jnp.int32(7)))

    root = s == 32
    reads_first = (s == 1) | (s == 2) | (s == 4) | (s == 8)
    count = count + reads_first.astype(jnp.int32) + 4 * root.astype(jnp.int32)

    @pl.when(reads_first)
    def _():
        pl.semaphore_signal(barrier, inc=1, device_id=(32, j), device_id_type=MESH)

    @pl.when(root)
    def _():
        for k in range(4):
            pl.semaphore_signal(barrier, inc=1, device_id=(2**k, j), device_id_type=MESH)

    first = [
        (diag.at[1, :, 0:H], d1.at[rows, 0:H]),
        (coup.at[0], c0.at[rows]),
        (coup.at[1], c1.at[rows]),
        (placed, hin.at[pl.ds(pl.multiple_of(j * 8, 8), 8)]),
        (diag.at[0], d2.at[rows]),
        (diag.at[1, :, H:N], d1.at[rows, H:N]),
    ]
    placed[...] = jnp.zeros((8, N), F32)
    for i in range(8):

        @pl.when(j == i)
        def _():
            placed[0:2, 32 * i : 32 * i + 32] = info[...]

    local = [
        pltpu.make_async_copy(src, dst, own_sem.at[a]) for a, (src, dst) in enumerate(first)
    ]
    for c in local:
        c.start()

    pl.semaphore_wait(barrier, count)

    def to(src, dst, send, recv, tm, state):
        return pltpu.make_async_remote_copy(
            src_ref=src, dst_ref=dst, send_sem=send, recv_sem=recv,
            device_id=(tm, state), device_id_type=MESH,
        )

    def peer(src, dst, sends, recvs, a, r):
        return to(src, dst, sends.at[a, r], recvs.at[a, r], s, lax.rem(j + r, 8))

    def gather(a, act):
        src, dst = first[a]
        for r in range(1, 8):
            act(peer(src, dst, g1_send, g1_recv, a, r))

    def direct(a, act):
        src, dst = first[a]
        for r in (2, 4, 6):
            act(peer(src, dst, g1_send, g1_recv, a, r))
        act(to(src, dst, g1_send.at[a, 1], g1_recv.at[a, 1], s, sibling))

    def hand_on(a, act):
        whole = (None, c0, c1, None, d2)[a]
        for r in (2, 4, 6):
            at = pl.ds(pl.multiple_of(lax.rem(j + 8 - r, 8) * 32, 32), 32)
            piece = whole.at[at]
            act(to(piece, piece, g1_send.at[a, r + 1], g1_recv.at[a, r + 1], s, sibling))

    def direct_arrived(a):
        src, dst = first[a]
        for r in (2, 4, 6):
            peer(src, dst, g1_send, g1_recv, a, r).wait_recv()

    def arrived(a):
        src, dst = first[a]
        local[a].wait()
        to(src, dst, g1_send.at[a, 1], g1_recv.at[a, 1], s, sibling).wait_recv()
        hand_on(a, lambda c: c.wait_recv())

    gather(0, lambda c: c.start())
    gather(5, lambda c: c.start())
    gather(0, lambda c: c.wait_send())
    gather(5, lambda c: c.wait_send())
    for a in (2, 1, 4):
        direct(a, lambda c: c.start())
    gather(3, lambda c: c.start())

    def gathered(a):
        local[a].wait()
        gather(a, lambda c: c.wait_recv())

    gathered(0)
    factor_start(d1, f1a)
    gathered(5)

    for a in (2, 1):
        direct_arrived(a)
        hand_on(a, lambda c: c.start())

    def fill0():
        arrived(2)
        arrived(1)
        gathered(3)
        info_all = sum8([hin[8 * i : 8 * i + 8, :] for i in range(8)])
        own_h[...] = row_of(info_all, 0)
        h1[...] = row_of(info_all, 1)
        c1t[...] = jnp.where(s == 63, 0.0, c1[...].T)
        project(c1t, 0, v1, ycat, N, H, f1a, za)
        lead_start(v1, pu01, N)
        project(c1t, H, v1, ycat, N + H, H, f1a, za)
        project(h1, 0, v1, ycat, 2 * N, 8, f1a, za)
        project(c0, 0, v1, ycat, 0, N, f1a, za)

    factor_rest(d1, {12: fill0}, f1a, f2a, za)
    lead_end(v1, ycat, f2a, pu01, N)

    up0 = s < 63

    def up0_sends(act):
        @pl.when(up0)
        def _():
            act(to(pu01, rc1.at[0], s_send.at[0], r1_recv.at[0], s + 1, j))

    def up0_rest(act):
        @pl.when(up0)
        def _():
            act(to(pu02, rc2.at[0], s_send.at[1], r2_recv.at[0], s + 1, j))

    def part_rows(part):
        return pl.ds(part * H, H)

    def up0_link(act):
        @pl.when(even)
        def _():
            for part in range(2):
                act(to(sx0.at[part], xl.at[part_rows(part)], s_send.at[2 + part], rx_recv.at[0, part], s + 1, j))

    up0_sends(lambda c: c.start())
    finish_rows(v1, ycat, f2a, N + H, H)
    finish_rows(v1, ycat, f2a, 2 * N, 8)
    rest_products(v1, pu02, N)
    up0_rest(lambda c: c.start())
    finish_rows(v1, ycat, f2a, 0, N)
    for part in range(2):
        sx0[part] = -nt(v1[part * H : part * H + H, :], v1[N : 2 * N, :])
    up0_link(lambda c: c.start())
    direct_arrived(4)
    hand_on(4, lambda c: c.start())
    back = nt(v1[2 * N : 2 * N + 8, :], v1[0:N, :])
    own_h[...] = own_h[...] - back
    arrived(4)
    hand_on(4, lambda c: c.wait_send())
    d2[0:H, 0:H] = d2[0:H, 0:H] - nt(v1[0:H, :], v1[0:H, :])
    d2[H:N, :] = d2[H:N, :] - nt(v1[H:N, :], v1[0:N, :])

    @pl.when(jnp.logical_not(even))
    def _():
        xu[...] = -nt(v1[N : 2 * N, :], v1[0:N, :])

    def take_lead(slot):
        to(pl1, rc1.at[slot], s_send.at[4], r1_recv.at[slot], s, j).wait_recv()
        d2[0:H, 0:H] = d2[0:H, 0:H] - rc1[slot]

    def take_rest(slot):
        to(pl2, rc2.at[slot], s_send.at[5], r2_recv.at[slot], s, j).wait_recv()
        d2[H:N, :] = d2[H:N, :] - rc2[slot, 0:H, :]
        own_h[...] = own_h[...] - rc2[slot, H : H + 8, :]

    @pl.when(even & inner)
    def _():
        take_lead(0)
        take_rest(0)

    def early(k, carry):
        @pl.when(inner)
        def _():
            take_lead(1 + 2 * k)
            take_rest(1 + 2 * k)

        take_lead(2 + 2 * k)
        take_rest(2 + 2 * k)
        return carry

    below = jnp.minimum(level, 5)
    lax.fori_loop(0, jnp.maximum(below - 1, 0), early, 0)

    left_slot = jnp.where(even, 2 * level - 1, 0)

    def take_last(take):
        @pl.when(inner)
        def _():
            take(left_slot)

        @pl.when(even)
        def _():
            take(2 * below)

    take_last(take_lead)

    def take_link(part):
        @pl.when(inner)
        def _():
            to(sx0.at[0], xl.at[part_rows(part)], s_send.at[2], rx_recv.at[0, part], s, j).wait_recv()

        @pl.when(even & inner)
        def _():
            to(sx0.at[0], xu.at[part_rows(part)], s_send.at[2], rx_recv.at[1, part], s, j).wait_recv()

    def first_lead():
        return to(pl1, rc1.at[12], s_send.at[4], r1_recv.at[12], 32, j)

    def first_rest():
        return to(pl2, rc2.at[12], s_send.at[6], r2_recv.at[12], 32, j)

    @pl.when(s == 0)
    def _():
        pl1[...] = d2[0:H, 0:H]
        first_lead().start()
        take_last(take_rest)
        pl2[0:H, :] = d2[H:N, :]
        pl2[H : H + 8, :] = own_h[...]
        first_rest().start()

    @pl.when(inner)
    def _():
        factor_start(d2, f1b)
        take_last(take_rest)
        take_link(0)

        def fill():
            project(own_h, 0, v2, ycat, 2 * N, 8, f1b, zb)
            for x, at, to_ in ((xl, 0, pl1), (xu, N, pu1)):
                project(x, 0, v2, ycat, at, H, f1b, zb)
                lead_start(v2, to_, at)

        def fill_rest():
            take_link(1)
            for x, at in ((xl, H), (xu, N + H)):
                project(x, H, v2, ycat, at, H, f1b, zb)
            rest_start(v2, pl2, 0)
            rest_start(v2, pu2, N)

        factor_rest(d2, {2: fill, 8: fill_rest}, f1b, f2b, zb)
        lead_end(v2, ycat, f2b, pl1, 0)
        lead_end(v2, ycat, f2b, pu1, N)

    sending = inner & jnp.logical_not(root)

    lower_slot, upper_slot = 2 + 2 * level, 1 + 2 * level

    def lead_sends(act):
        @pl.when(sending)
        def _():
            act(to(pl1, rc1.at[lower_slot], s_send.at[4], r1_recv.at[lower_slot], s - dist, j))

        @pl.when(upper)
        def _():
            act(to(pu1, rc1.at[upper_slot], s_send.at[5], r1_recv.at[upper_slot], s + dist, j))

    def rest_sends(act):
        @pl.when(sending)
        def _():
            act(to(pl2, rc2.at[lower_slot], s_send.at[6], r2_recv.at[lower_slot], s - dist, j))

        @pl.when(upper)
        def _():
            act(to(pu2, rc2.at[upper_slot], s_send.at[7], r2_recv.at[upper_slot], s + dist, j))

    def link_send(part, act):
        at = part_rows(part)

        @pl.when(to_lower)
        def _():
            act(to(sx.at[part], xu.at[at], s_send.at[8 + part], rx_recv.at[1, part], s - dist, j))

        @pl.when(to_upper)
        def _():
            act(to(sx.at[part], xl.at[at], s_send.at[8 + part], rx_recv.at[0, part], s + dist, j))

    lead_sends(lambda c: c.start())
    @pl.when(sending)
    def _():
        for at in (H, N + H):
            finish_rows(v2, ycat, f2b, at, H)
        finish_rows(v2, ycat, f2b, 2 * N, 8)
        rest_end(v2, pl2, 0)
        rest_end(v2, pu2, N)

    rest_sends(lambda c: c.start())

    for part in range(2):

        @pl.when(to_lower)
        def _():
            sx[part] = -nt(v2[N + part * H : N + part * H + H, :], v2[0:N, :])

        @pl.when(to_upper)
        def _():
            sx[part] = -nt(v2[part * H : part * H + H, :], v2[N : 2 * N, :])

        link_send(part, lambda c: c.start())

    def own_means():
        lo, hi = means(v2, f1b, f2b, zb)
        gb[:, 0:H] = lo
        gb[:, H:N] = hi

    def early_means():
        lo, hi = means(v1, f1a, f2a, za)
        ga[:, 0:H] = lo
        ga[:, H:N] = hi

    def columns_up():
        return to(cols, cols_in, fold_send.at[0], fold_recv.at[0], s + 1, j)

    def folded_down():
        return to(fold, fold_in, fold_send.at[1], fold_recv.at[1], s - 1, j)

    def columns():
        gat[...] = ga[N : 2 * N, :].T
        cols[...] = gat[rows, :]
        columns_up().start()

    def spread_first(act):
        for a, seg in enumerate((16, 8, 4, 2, 1, 0)):
            act(to(xfirst, xin.at[0], x_send.at[13 + a], x_recv.at[0], seg, j))

    @pl.when(root)
    def _():
        to(pl1, rc1.at[12], s_send.at[4], r1_recv.at[12], s, j).wait_recv()
        to(pl2, rc2.at[12], s_send.at[6], r2_recv.at[12], s, j).wait_recv()
        d1[0:H, 0:H] = rc1[12] - pl1[...]
        finish_rows(v2, ycat, f2b, H, H)
        finish_rows(v2, ycat, f2b, N, N)
        finish_rows(v2, ycat, f2b, 2 * N, 8)
        rest_end(v2, pl2, 0)
        d1[H:N, :] = rc2[12, 0:H, :] - pl2[0:H, :]
        h1[...] = rc2[12, H : H + 8, :] - pl2[H : H + 8, :]
        factor_start(d1, f1c)

        def fill():
            project(h1, 0, hv, hy, 0, 8, f1c, zc)
            own_means()

        factor_rest(d1, {2: fill}, f1c, f2c, zc)
        finish_rows(hv, hy, f2c, 0, 8)
        lo, hi = means(hv, f1c, f2c, zc)
        xfirst[:, 0:H] = lo
        xfirst[:, H:N] = hi
        spread_first(lambda c: c.start())
        xown[...] = gb[2 * N : 2 * N + 8, :] - nn(xfirst[...], gb[0:N, :])

    @pl.when(jnp.logical_not(root))
    def _():
        @pl.when(inner)
        def _():
            own_means()

        early_means()

    @pl.when(even & jnp.logical_not(root))
    def _():
        columns()

    @pl.when(jnp.logical_not(even))
    def _():
        to(cols, cols_in, fold_send.at[0], fold_recv.at[0], s, j).wait_recv()
        fold[0:32, :] = nt(cols_in[...], gb[0:N, :])
        fold[32:64, :] = nt(cols_in[...], gb[N : 2 * N, :])
        fold[64:72, :] = gb[2 * N : 2 * N + 8, :]
        folded_down().start()

    def wait_mean(a):
        to(xown, xin.at[a], x_send.at[0], x_recv.at[a], s, j).wait_recv()

    @pl.when(s == 0)
    def _():
        wait_mean(0)
        xown[...] = xin[0]
        xin[1] = jnp.zeros((8, N), F32)

    @pl.when(to_lower)
    def _():
        @pl.when(upper)
        def _():
            wait_mean(1)

        @pl.when(jnp.logical_not(upper))
        def _():
            xin[1] = jnp.zeros((8, N), F32)

        xown[...] = gb[2 * N : 2 * N + 8, :] - nn(xin[1], gb[N : 2 * N, :])
        wait_mean(0)
        xown[...] = xown[...] - nn(xin[0], gb[0:N, :])

    @pl.when(to_upper)
    def _():
        wait_mean(0)
        xown[...] = gb[2 * N : 2 * N + 8, :] - nn(xin[0], gb[0:N, :])
        wait_mean(1)
        xown[...] = xown[...] - nn(xin[1], gb[N : 2 * N, :])

    def spread(act):
        def step(i, d):
            k = level - 1 - i
            act(to(xown, xin.at[0], x_send.at[2 * k], x_recv.at[0], s + d, j))
            act(to(xown, xin.at[1], x_send.at[2 * k + 1], x_recv.at[1], s - d, j))
            return d // 2

        lax.fori_loop(0, jnp.where(inner, level, 0), step, dist // 2)

        @pl.when(even & inner)
        def _():
            act(to(xown, xin.at[2], x_send.at[12], x_recv.at[2], s - 2, j))

    spread(lambda c: c.start())

    @pl.when(root)
    def _():
        early_means()
        columns()

    part = ga[2 * N : 2 * N + 8, :] - nn(xown[...], ga[0:N, :])

    def put(later):
        both = jnp.concatenate([xown[0:1, :], later[0:1, :]], axis=0)
        for i in range(8):

            @pl.when(j == i)
            def _():
                out[...] = both[:, 32 * i : 32 * i + 32]

    @pl.when(jnp.logical_not(even))
    def _():
        put(part - nn(xin[1], ga[N : 2 * N, :]))

    @pl.when(even)
    def _():
        put(part)
        to(fold, fold_in, fold_send.at[1], fold_recv.at[1], s, j).wait_recv()
        share = nt(xown[...], fold_in[0:32, :]) - nt(fold_in[64:72, :], cols[...])

        @pl.when(s < 62)
        def _():
            to(xown, xin.at[2], x_send.at[12], x_recv.at[2], s, j).wait_recv()

        @pl.when(s == 62)
        def _():
            xin[2] = jnp.zeros((8, N), F32)

        share = share + nt(xin[2], fold_in[32:64, :])
        out[1:2, :] = out[1:2, :] + share[0:1, :]

    gather(3, lambda c: c.wait_send())
    for a in (1, 2, 4):
        direct(a, lambda c: c.wait_send())
    for a in (1, 2):
        hand_on(a, lambda c: c.wait_send())

    up0_sends(lambda c: c.wait_send())
    up0_link(lambda c: c.wait_send())
    up0_rest(lambda c: c.wait_send())


    @pl.when(s == 0)
    def _():
        first_lead().wait_send()
        first_rest().wait_send()

    @pl.when(root)
    def _():
        spread_first(lambda c: c.wait_send())

    @pl.when(even)
    def _():
        columns_up().wait_send()

    @pl.when(jnp.logical_not(even))
    def _():
        folded_down().wait_send()

    lead_sends(lambda c: c.wait_send())
    for part in range(2):
        link_send(part, lambda c: c.wait_send())
    rest_sends(lambda c: c.wait_send())
    spread(lambda c: c.wait_send())


def body(diagonal, coupling, info):
    vmem = pltpu.VMEM
    dma = pltpu.SemaphoreType.DMA
    square = vmem((N, N), F32)
    half = vmem((H, H), F32)
    tall = vmem((2 * N + 8, N), F32)
    slab = vmem((H + 8, N), F32)
    pair = vmem((2, H, N), F32)
    return pl.pallas_call(
        kernel,
        out_shape=jax.ShapeDtypeStruct((2, 32), F32),
        in_specs=[pl.BlockSpec(memory_space=m) for m in (pltpu.HBM, pltpu.HBM, vmem)],
        out_specs=pl.BlockSpec(memory_space=vmem),
        scratch_shapes=[
            square, square, square, vmem((64, N), F32), square, square, square, square, vmem((8, N), F32), vmem((2 * N + 8, H), F32), tall, tall,
            half, half, half, half, half, half, half, half, half,
            vmem((8, N), F32), vmem((8, H), F32), vmem((8, N), F32), vmem((8, N), F32),
            square, vmem((32, N), F32), vmem((32, N), F32), vmem((72, N), F32), vmem((72, N), F32), tall, tall,
            vmem((8, N), F32), vmem((13, H, H), F32), vmem((13, H + 8, N), F32),
            half, slab, pair, half, slab, half, slab, pair,
            vmem((3, 8, N), F32), vmem((8, N), F32),
            dma((6, 8)), dma((6, 8)),
            dma((13,)), dma((13,)), dma((2, 2)), dma((10,)), dma((19,)), dma((3,)), dma((6,)), dma((2,)), dma((2,)),
        ],
        compiler_params=pltpu.CompilerParams(
            collective_id=0, has_side_effects=True, vmem_limit_bytes=32 * 1024 * 1024
        ),
    )(diagonal, coupling, info)


def solution(mesh):
    placed = (P("tm", "state", None), P("tm", "state", None), P("tm", "state"))
    return jax.shard_map(
        body, mesh=mesh, in_specs=placed, out_specs=P("tm", "state"), check_vma=False
    )
```

```python
import jax
import jax.numpy as jnp
from jax import lax
from jax.experimental import pallas as pl
from jax.experimental.pallas import tpu as pltpu
from jax.sharding import PartitionSpec as P

N = 256
H = 128
F32 = jnp.float32
MESH = pl.DeviceIdType.MESH
EXACT = lax.Precision.HIGHEST


def nt(a, b):
    return lax.dot_general(
        a, b, (((1,), (1,)), ((), ())), precision=EXACT, preferred_element_type=F32
    )


def nn(a, b):
    return jnp.dot(a, b, precision=EXACT, preferred_element_type=F32)


def row_of(x, k):
    return jnp.broadcast_to(x[k : k + 1, :], x.shape)


def lane_of(x, l):
    return jnp.take_along_axis(x, jnp.full((8, H), l, jnp.int32), axis=1)


def sum8(t):
    return ((t[0] + t[1]) + (t[2] + t[3])) + ((t[4] + t[5]) + (t[6] + t[7]))


def pivot_block(w, b, sub, lane):
    at = 8 * b
    c = [lane_of(w[b], at + j) for j in range(8)]
    inside = (lane >= at) & (lane < at + 8)
    r = jnp.where(inside, (lane - at == sub).astype(F32), w[b])
    t = r
    pivots = jnp.ones((8, H), F32)
    inverses = []
    for k in range(0, 8, 2):
        first, second = sub == k, sub == k + 1
        p, q, o = row_of(c[k], k), row_of(c[k + 1], k), row_of(c[k + 1], k + 1)
        det = 1.0 / (p * o - q * q)
        m0 = jnp.where(first | second, 0.0, c[k])
        m1 = jnp.where(first | second, 0.0, c[k + 1])
        f0 = (m0 * o - m1 * q) * det
        f1 = (m1 * p - m0 * q) * det
        inverses.append((o * det, -q * det, p * det))
        ratio = q * (1.0 / p)
        r0, r1 = row_of(r, k), row_of(r, k + 1)
        t = jnp.where(first, r0, jnp.where(second, r1 - ratio * r0, t))
        pivots = jnp.where(first, p, jnp.where(second, o - ratio * q, pivots))
        for j in range(k + 2, 8):
            c[j] = c[j] - (f0 * row_of(c[j], k) + f1 * row_of(c[j], k + 1))
        r = r - (f0 * r0 + f1 * r1)
    if b < 15:
        rows = []
        for k in range(0, 8, 2):
            ia, ib, ic = inverses[k // 2]
            r0, r1 = row_of(r, k), row_of(r, k + 1)
            rows += [ia * r0 + ib * r1, ib * r0 + ic * r1]
        for i in range(b + 1, 16):
            cols = [lane_of(w[i], at + j) for j in range(8)]
            w[i] = jnp.where(inside, 0.0, w[i]) - sum8([cols[j] * rows[j] for j in range(8)])
    return jnp.where(lane < at + 8, t * lax.rsqrt(pivots), 0.0)


def factor_part(w, blocks):
    sub = lax.broadcasted_iota(jnp.int32, (8, H), 0)
    lane = lax.broadcasted_iota(jnp.int32, (8, H), 1)
    return [pivot_block(w, b, sub, lane) for b in blocks]


def groups(a):
    return [a[8 * r : 8 * r + 8, :] for r in range(16)]


def factor_start(block, f1):
    f1[...] = jnp.concatenate(factor_part(groups(block[0:H, 0:H]), range(16)), axis=0)


def factor_rest(block, steps, f1, f2, z):
    z[...] = nt(block[H:N, 0:H], f1[...])
    w = groups(block[H:N, H:N] - nt(z[...], z[...]))
    out = []
    for b in range(16):
        if b in steps:
            steps[b]()
        out += factor_part(w, [b])
    f2[...] = jnp.concatenate(out, axis=0)


def project(x, at, v, y, to, n, f1, z):
    v[to : to + n, 0:H] = nt(x[at : at + n, 0:H], f1[...])
    y[to : to + n, :] = x[at : at + n, H:N] - nt(v[to : to + n, 0:H], z[...])


def lead_start(v, to, at):
    to[...] = nt(v[at : at + H, 0:H], v[at : at + H, 0:H])


def lead_end(v, y, f2, to, at):
    top = nt(y[at : at + H, :], f2[...])
    v[at : at + H, H:N] = top
    to[...] = to[...] + nt(top, top)


def rest_products(v, to, at):
    to[0:H, :] = nt(v[at + H : at + N, :], v[at : at + N, :])
    to[H : H + 8, :] = nt(v[2 * N : 2 * N + 8, :], v[at : at + N, :])


def rest_rows(v, at, cols):
    return jnp.concatenate([v[at + H : at + N, cols], v[2 * N : 2 * N + 8, cols]], axis=0)


def rest_start(v, to, at):
    c = slice(0, H)
    to[...] = nt(rest_rows(v, at, c), v[at : at + N, c])


def rest_end(v, to, at):
    c = slice(H, N)
    to[...] = to[...] + nt(rest_rows(v, at, c), v[at : at + N, c])


def finish_rows(v, y, f2, at, n):
    v[at : at + n, H:N] = nt(y[at : at + n, :], f2[...])


def means(v, f1, f2, z):
    hi = nn(v[:, H:N], f2[...])
    lo = nn(v[:, 0:H] - nn(hi, z[...]), f1[...])
    return lo, hi


def kernel(
    diag, coup, info, out,
    d1, c0, c1, hin, d2, xl, xu, c1t, h1, ycat, v1, v2, f1a, f2a, za, f1b, f2b, zb, f1c, f2c, zc, hv, hy, xfirst, placed, gat, cols, cols_in, fold, fold_in, ga, gb,
    own_h, rc1, rc2, pu01, pu02, sx0, pl1, pl2, pu1, pu2, sx, xin, xown,
    g1_send, g1_recv, r1_recv, r2_recv, rx_recv, s_send, x_send, x_recv, own_sem, fold_send, fold_recv,
):
    s = lax.axis_index("tm")
    j = lax.axis_index("state")
    core = lax.rem(j, 2)
    sibling = j + 1 - 2 * core
    rows = pl.ds(pl.multiple_of(j * 32, 32), 32)

    even = lax.rem(s, 2) == 0

    level, dist = jnp.int32(6), jnp.int32(64)
    to_lower, to_upper = jnp.bool_(False), jnp.bool_(False)
    for k in range(6):
        d = 2**k
        mine = lax.rem(s, 2 * d) == d
        level, dist = jnp.where(mine, k, level), jnp.where(mine, d, dist)
        if k < 5:
            to_lower = to_lower | (mine & (lax.rem(s - d, 4 * d) == 2 * d))
            to_upper = to_upper | (mine & (s + d < 64) & (lax.rem(s + d, 4 * d) == 2 * d))
    inner = s > 0
    upper = s + dist < 64

    barrier = pltpu.get_barrier_semaphore()
    for r in range(1, 8):
        pl.semaphore_signal(
            barrier, inc=1, device_id=(s, lax.rem(j + r, 8)), device_id_type=MESH
        )

    def greet(k, carry):
        d, count = carry
        up = s + d < 64

        @pl.when(inner)
        def _():
            pl.semaphore_signal(barrier, inc=1, device_id=(s - d, j), device_id_type=MESH)

        @pl.when(up)
        def _():
            pl.semaphore_signal(barrier, inc=1, device_id=(s + d, j), device_id_type=MESH)

        return 2 * d, count + inner.astype(jnp.int32) + up.astype(jnp.int32)

    _, count = lax.fori_loop(0, level + 1, greet, (jnp.int32(1), jnp.int32(7)))

    root = s == 32
    reads_first = (s == 1) | (s == 2) | (s == 4) | (s == 8)
    count = count + reads_first.astype(jnp.int32) + 4 * root.astype(jnp.int32)

    @pl.when(reads_first)
    def _():
        pl.semaphore_signal(barrier, inc=1, device_id=(32, j), device_id_type=MESH)

    @pl.when(root)
    def _():
        for k in range(4):
            pl.semaphore_signal(barrier, inc=1, device_id=(2**k, j), device_id_type=MESH)

    first = [
        (diag.at[1, :, 0:H], d1.at[rows, 0:H]),
        (coup.at[0], c0.at[rows]),
        (coup.at[1], c1.at[rows]),
        (placed, hin.at[pl.ds(pl.multiple_of(j * 8, 8), 8)]),
        (diag.at[0], d2.at[rows]),
        (diag.at[1, :, H:N], d1.at[rows, H:N]),
    ]
    placed[...] = jnp.zeros((8, N), F32)
    for i in range(8):

        @pl.when(j == i)
        def _():
            placed[0:2, 32 * i : 32 * i + 32] = info[...]

    local = [
        pltpu.make_async_copy(src, dst, own_sem.at[a]) for a, (src, dst) in enumerate(first)
    ]
    for c in local:
        c.start()

    pl.semaphore_wait(barrier, count)

    def to(src, dst, send, recv, tm, state):
        return pltpu.make_async_remote_copy(
            src_ref=src, dst_ref=dst, send_sem=send, recv_sem=recv,
            device_id=(tm, state), device_id_type=MESH,
        )

    def peer(src, dst, sends, recvs, a, r):
        return to(src, dst, sends.at[a, r], recvs.at[a, r], s, lax.rem(j + r, 8))

    def gather(a, act):
        src, dst = first[a]
        for r in range(1, 8):
            act(peer(src, dst, g1_send, g1_recv, a, r))

    def direct(a, act):
        src, dst = first[a]
        for r in (2, 4, 6):
            act(peer(src, dst, g1_send, g1_recv, a, r))
        act(to(src, dst, g1_send.at[a, 1], g1_recv.at[a, 1], s, sibling))

    def hand_on(a, act):
        whole = (None, c0, c1, None, d2)[a]
        for r in (2, 4, 6):
            at = pl.ds(pl.multiple_of(lax.rem(j + 8 - r, 8) * 32, 32), 32)
            piece = whole.at[at]
            act(to(piece, piece, g1_send.at[a, r + 1], g1_recv.at[a, r + 1], s, sibling))

    def direct_arrived(a):
        src, dst = first[a]
        for r in (2, 4, 6):
            peer(src, dst, g1_send, g1_recv, a, r).wait_recv()

    def arrived(a):
        src, dst = first[a]
        local[a].wait()
        to(src, dst, g1_send.at[a, 1], g1_recv.at[a, 1], s, sibling).wait_recv()
        hand_on(a, lambda c: c.wait_recv())

    gather(0, lambda c: c.start())
    gather(5, lambda c: c.start())
    gather(0, lambda c: c.wait_send())
    gather(5, lambda c: c.wait_send())
    for a in (2, 1, 4):
        direct(a, lambda c: c.start())
    gather(3, lambda c: c.start())

    def gathered(a):
        local[a].wait()
        gather(a, lambda c: c.wait_recv())

    gathered(0)
    factor_start(d1, f1a)
    gathered(5)

    for a in (2, 1):
        direct_arrived(a)
        hand_on(a, lambda c: c.start())

    def fill0():
        arrived(2)
        arrived(1)
        gathered(3)
        info_all = sum8([hin[8 * i : 8 * i + 8, :] for i in range(8)])
        own_h[...] = row_of(info_all, 0)
        h1[...] = row_of(info_all, 1)
        c1t[...] = jnp.where(s == 63, 0.0, c1[...].T)
        project(c1t, 0, v1, ycat, N, H, f1a, za)
        lead_start(v1, pu01, N)
        project(c1t, H, v1, ycat, N + H, H, f1a, za)
        project(h1, 0, v1, ycat, 2 * N, 8, f1a, za)
        project(c0, 0, v1, ycat, 0, N, f1a, za)

    factor_rest(d1, {12: fill0}, f1a, f2a, za)
    lead_end(v1, ycat, f2a, pu01, N)

    up0 = s < 63

    def up0_sends(act):
        @pl.when(up0)
        def _():
            act(to(pu01, rc1.at[0], s_send.at[0], r1_recv.at[0], s + 1, j))

    def up0_rest(act):
        @pl.when(up0)
        def _():
            act(to(pu02, rc2.at[0], s_send.at[1], r2_recv.at[0], s + 1, j))

    def part_rows(part):
        return pl.ds(part * H, H)

    def up0_link(act):
        @pl.when(even)
        def _():
            for part in range(2):
                act(to(sx0.at[part], xl.at[part_rows(part)], s_send.at[2 + part], rx_recv.at[0, part], s + 1, j))

    up0_sends(lambda c: c.start())
    finish_rows(v1, ycat, f2a, N + H, H)
    finish_rows(v1, ycat, f2a, 2 * N, 8)
    rest_products(v1, pu02, N)
    up0_rest(lambda c: c.start())
    finish_rows(v1, ycat, f2a, 0, N)
    for part in range(2):
        sx0[part] = -nt(v1[part * H : part * H + H, :], v1[N : 2 * N, :])
    up0_link(lambda c: c.start())
    direct_arrived(4)
    hand_on(4, lambda c: c.start())
    back = nt(v1[2 * N : 2 * N + 8, :], v1[0:N, :])
    own_h[...] = own_h[...] - back
    arrived(4)
    hand_on(4, lambda c: c.wait_send())
    d2[0:H, 0:H] = d2[0:H, 0:H] - nt(v1[0:H, :], v1[0:H, :])
    d2[H:N, :] = d2[H:N, :] - nt(v1[H:N, :], v1[0:N, :])

    @pl.when(jnp.logical_not(even))
    def _():
        xu[...] = -nt(v1[N : 2 * N, :], v1[0:N, :])

    def take_lead(slot):
        to(pl1, rc1.at[slot], s_send.at[4], r1_recv.at[slot], s, j).wait_recv()
        d2[0:H, 0:H] = d2[0:H, 0:H] - rc1[slot]

    def take_rest(slot):
        to(pl2, rc2.at[slot], s_send.at[5], r2_recv.at[slot], s, j).wait_recv()
        d2[H:N, :] = d2[H:N, :] - rc2[slot, 0:H, :]
        own_h[...] = own_h[...] - rc2[slot, H : H + 8, :]

    @pl.when(even & inner)
    def _():
        take_lead(0)
        take_rest(0)

    def early(k, carry):
        @pl.when(inner)
        def _():
            take_lead(1 + 2 * k)
            take_rest(1 + 2 * k)

        take_lead(2 + 2 * k)
        take_rest(2 + 2 * k)
        return carry

    below = jnp.minimum(level, 5)
    lax.fori_loop(0, jnp.maximum(below - 1, 0), early, 0)

    left_slot = jnp.where(even, 2 * level - 1, 0)

    def take_last(take):
        @pl.when(inner)
        def _():
            take(left_slot)

        @pl.when(even)
        def _():
            take(2 * below)

    take_last(take_lead)

    def take_link(part):
        @pl.when(inner)
        def _():
            to(sx0.at[0], xl.at[part_rows(part)], s_send.at[2], rx_recv.at[0, part], s, j).wait_recv()

        @pl.when(even & inner)
        def _():
            to(sx0.at[0], xu.at[part_rows(part)], s_send.at[2], rx_recv.at[1, part], s, j).wait_recv()

    def first_lead():
        return to(pl1, rc1.at[12], s_send.at[4], r1_recv.at[12], 32, j)

    def first_rest():
        return to(pl2, rc2.at[12], s_send.at[6], r2_recv.at[12], 32, j)

    @pl.when(s == 0)
    def _():
        pl1[...] = d2[0:H, 0:H]
        first_lead().start()
        take_last(take_rest)
        pl2[0:H, :] = d2[H:N, :]
        pl2[H : H + 8, :] = own_h[...]
        first_rest().start()

    @pl.when(inner)
    def _():
        factor_start(d2, f1b)
        take_last(take_rest)
        take_link(0)

        def fill():
            project(own_h, 0, v2, ycat, 2 * N, 8, f1b, zb)
            for x, at, to_ in ((xl, 0, pl1), (xu, N, pu1)):
                project(x, 0, v2, ycat, at, H, f1b, zb)
                lead_start(v2, to_, at)

        def fill_rest():
            take_link(1)
            for x, at in ((xl, H), (xu, N + H)):
                project(x, H, v2, ycat, at, H, f1b, zb)
            rest_start(v2, pl2, 0)
            rest_start(v2, pu2, N)

        factor_rest(d2, {2: fill, 8: fill_rest}, f1b, f2b, zb)
        lead_end(v2, ycat, f2b, pl1, 0)
        lead_end(v2, ycat, f2b, pu1, N)

    sending = inner & jnp.logical_not(root)

    lower_slot, upper_slot = 2 + 2 * level, 1 + 2 * level

    def lead_sends(act):
        @pl.when(sending)
        def _():
            act(to(pl1, rc1.at[lower_slot], s_send.at[4], r1_recv.at[lower_slot], s - dist, j))

        @pl.when(upper)
        def _():
            act(to(pu1, rc1.at[upper_slot], s_send.at[5], r1_recv.at[upper_slot], s + dist, j))

    def rest_down(act):
        @pl.when(sending)
        def _():
            act(to(pl2, rc2.at[lower_slot], s_send.at[6], r2_recv.at[lower_slot], s - dist, j))

    def rest_up(act):
        @pl.when(upper)
        def _():
            act(to(pu2, rc2.at[upper_slot], s_send.at[7], r2_recv.at[upper_slot], s + dist, j))

    def link_send(part, act):
        at = part_rows(part)

        @pl.when(to_lower)
        def _():
            act(to(sx.at[part], xu.at[at], s_send.at[8 + part], rx_recv.at[1, part], s - dist, j))

        @pl.when(to_upper)
        def _():
            act(to(sx.at[part], xl.at[at], s_send.at[8 + part], rx_recv.at[0, part], s + dist, j))

    lead_sends(lambda c: c.start())
    @pl.when(sending)
    def _():
        for at in (H, N + H):
            finish_rows(v2, ycat, f2b, at, H)
        finish_rows(v2, ycat, f2b, 2 * N, 8)

    def rest_lower():
        rest_end(v2, pl2, 0)
        rest_down(lambda c: c.start())

    def rest_upper():
        rest_end(v2, pu2, N)
        rest_up(lambda c: c.start())

    @pl.when(to_lower)
    def _():
        rest_lower()
        rest_upper()

    @pl.when(to_upper)
    def _():
        rest_upper()
        rest_lower()


    for part in range(2):

        @pl.when(to_lower)
        def _():
            sx[part] = -nt(v2[N + part * H : N + part * H + H, :], v2[0:N, :])

        @pl.when(to_upper)
        def _():
            sx[part] = -nt(v2[part * H : part * H + H, :], v2[N : 2 * N, :])

        link_send(part, lambda c: c.start())

    def own_means():
        lo, hi = means(v2, f1b, f2b, zb)
        gb[:, 0:H] = lo
        gb[:, H:N] = hi

    def early_means():
        lo, hi = means(v1, f1a, f2a, za)
        ga[:, 0:H] = lo
        ga[:, H:N] = hi

    def columns_up():
        return to(cols, cols_in, fold_send.at[0], fold_recv.at[0], s + 1, j)

    def folded_down():
        return to(fold, fold_in, fold_send.at[1], fold_recv.at[1], s - 1, j)

    def columns():
        gat[...] = ga[N : 2 * N, :].T
        cols[...] = gat[rows, :]
        columns_up().start()

    def spread_first(act):
        for a, seg in enumerate((16, 8, 4, 2, 1, 0)):
            act(to(xfirst, xin.at[0], x_send.at[13 + a], x_recv.at[0], seg, j))

    @pl.when(root)
    def _():
        to(pl1, rc1.at[12], s_send.at[4], r1_recv.at[12], s, j).wait_recv()
        to(pl2, rc2.at[12], s_send.at[6], r2_recv.at[12], s, j).wait_recv()
        d1[0:H, 0:H] = rc1[12] - pl1[...]
        finish_rows(v2, ycat, f2b, H, H)
        finish_rows(v2, ycat, f2b, N, N)
        finish_rows(v2, ycat, f2b, 2 * N, 8)
        rest_end(v2, pl2, 0)
        d1[H:N, :] = rc2[12, 0:H, :] - pl2[0:H, :]
        h1[...] = rc2[12, H : H + 8, :] - pl2[H : H + 8, :]
        factor_start(d1, f1c)

        def fill():
            project(h1, 0, hv, hy, 0, 8, f1c, zc)
            own_means()

        factor_rest(d1, {2: fill}, f1c, f2c, zc)
        finish_rows(hv, hy, f2c, 0, 8)
        lo, hi = means(hv, f1c, f2c, zc)
        xfirst[:, 0:H] = lo
        xfirst[:, H:N] = hi
        spread_first(lambda c: c.start())
        xown[...] = gb[2 * N : 2 * N + 8, :] - nn(xfirst[...], gb[0:N, :])

    @pl.when(jnp.logical_not(root))
    def _():
        @pl.when(inner)
        def _():
            own_means()

        early_means()

    @pl.when(even & jnp.logical_not(root))
    def _():
        columns()

    @pl.when(jnp.logical_not(even))
    def _():
        to(cols, cols_in, fold_send.at[0], fold_recv.at[0], s, j).wait_recv()
        fold[0:32, :] = nt(cols_in[...], gb[0:N, :])
        fold[32:64, :] = nt(cols_in[...], gb[N : 2 * N, :])
        fold[64:72, :] = gb[2 * N : 2 * N + 8, :]
        folded_down().start()

    def wait_mean(a):
        to(xown, xin.at[a], x_send.at[0], x_recv.at[a], s, j).wait_recv()

    @pl.when(s == 0)
    def _():
        wait_mean(0)
        xown[...] = xin[0]
        xin[1] = jnp.zeros((8, N), F32)

    @pl.when(to_lower)
    def _():
        @pl.when(upper)
        def _():
            wait_mean(1)

        @pl.when(jnp.logical_not(upper))
        def _():
            xin[1] = jnp.zeros((8, N), F32)

        xown[...] = gb[2 * N : 2 * N + 8, :] - nn(xin[1], gb[N : 2 * N, :])
        wait_mean(0)
        xown[...] = xown[...] - nn(xin[0], gb[0:N, :])

    @pl.when(to_upper)
    def _():
        wait_mean(0)
        xown[...] = gb[2 * N : 2 * N + 8, :] - nn(xin[0], gb[0:N, :])
        wait_mean(1)
        xown[...] = xown[...] - nn(xin[1], gb[N : 2 * N, :])

    def spread(act):
        def step(i, d):
            k = level - 1 - i
            act(to(xown, xin.at[0], x_send.at[2 * k], x_recv.at[0], s + d, j))
            act(to(xown, xin.at[1], x_send.at[2 * k + 1], x_recv.at[1], s - d, j))
            return d // 2

        lax.fori_loop(0, jnp.where(inner, level, 0), step, dist // 2)

        @pl.when(even & inner)
        def _():
            act(to(xown, xin.at[2], x_send.at[12], x_recv.at[2], s - 2, j))

    spread(lambda c: c.start())

    @pl.when(root)
    def _():
        early_means()
        columns()

    part = ga[2 * N : 2 * N + 8, :] - nn(xown[...], ga[0:N, :])

    def put(later):
        both = jnp.concatenate([xown[0:1, :], later[0:1, :]], axis=0)
        for i in range(8):

            @pl.when(j == i)
            def _():
                out[...] = both[:, 32 * i : 32 * i + 32]

    @pl.when(jnp.logical_not(even))
    def _():
        put(part - nn(xin[1], ga[N : 2 * N, :]))

    @pl.when(even)
    def _():
        put(part)
        to(fold, fold_in, fold_send.at[1], fold_recv.at[1], s, j).wait_recv()
        share = nt(xown[...], fold_in[0:32, :]) - nt(fold_in[64:72, :], cols[...])

        @pl.when(s < 62)
        def _():
            to(xown, xin.at[2], x_send.at[12], x_recv.at[2], s, j).wait_recv()

        @pl.when(s == 62)
        def _():
            xin[2] = jnp.zeros((8, N), F32)

        share = share + nt(xin[2], fold_in[32:64, :])
        out[1:2, :] = out[1:2, :] + share[0:1, :]

    gather(3, lambda c: c.wait_send())
    for a in (1, 2, 4):
        direct(a, lambda c: c.wait_send())
    for a in (1, 2):
        hand_on(a, lambda c: c.wait_send())

    up0_sends(lambda c: c.wait_send())
    up0_link(lambda c: c.wait_send())
    up0_rest(lambda c: c.wait_send())


    @pl.when(s == 0)
    def _():
        first_lead().wait_send()
        first_rest().wait_send()

    @pl.when(root)
    def _():
        spread_first(lambda c: c.wait_send())

    @pl.when(even)
    def _():
        columns_up().wait_send()

    @pl.when(jnp.logical_not(even))
    def _():
        folded_down().wait_send()

    lead_sends(lambda c: c.wait_send())
    for part in range(2):
        link_send(part, lambda c: c.wait_send())
    rest_down(lambda c: c.wait_send())
    rest_up(lambda c: c.wait_send())
    spread(lambda c: c.wait_send())


def body(diagonal, coupling, info):
    vmem = pltpu.VMEM
    dma = pltpu.SemaphoreType.DMA
    square = vmem((N, N), F32)
    half = vmem((H, H), F32)
    tall = vmem((2 * N + 8, N), F32)
    slab = vmem((H + 8, N), F32)
    pair = vmem((2, H, N), F32)
    return pl.pallas_call(
        kernel,
        out_shape=jax.ShapeDtypeStruct((2, 32), F32),
        in_specs=[pl.BlockSpec(memory_space=m) for m in (pltpu.HBM, pltpu.HBM, vmem)],
        out_specs=pl.BlockSpec(memory_space=vmem),
        scratch_shapes=[
            square, square, square, vmem((64, N), F32), square, square, square, square, vmem((8, N), F32), vmem((2 * N + 8, H), F32), tall, tall,
            half, half, half, half, half, half, half, half, half,
            vmem((8, N), F32), vmem((8, H), F32), vmem((8, N), F32), vmem((8, N), F32),
            square, vmem((32, N), F32), vmem((32, N), F32), vmem((72, N), F32), vmem((72, N), F32), tall, tall,
            vmem((8, N), F32), vmem((13, H, H), F32), vmem((13, H + 8, N), F32),
            half, slab, pair, half, slab, half, slab, pair,
            vmem((3, 8, N), F32), vmem((8, N), F32),
            dma((6, 8)), dma((6, 8)),
            dma((13,)), dma((13,)), dma((2, 2)), dma((10,)), dma((19,)), dma((3,)), dma((6,)), dma((2,)), dma((2,)),
        ],
        compiler_params=pltpu.CompilerParams(
            collective_id=0, has_side_effects=True, vmem_limit_bytes=32 * 1024 * 1024
        ),
    )(diagonal, coupling, info)


def solution(mesh):
    placed = (P("tm", "state", None), P("tm", "state", None), P("tm", "state"))
    return jax.shard_map(
        body, mesh=mesh, in_specs=placed, out_specs=P("tm", "state"), check_vma=False
    )
```
